32 devices in a mesh: groups: 2 (over x), seq: 16 (over z, y, core).
Axes of the slice: x: 2, y: 2, z: 4, core: 2. Of those that a mesh axis runs over, the one named last changes fastest.
Arguments:
- query_states: bfloat16 [3584, 16, 128], P(('groups', 'seq')), parts along dimension 0, may hold values from -6 to 6
- key_states: bfloat16 [3584, 8, 128], P(('groups', 'seq')), parts along dimension 0, may hold values from -6 to 6
- value_states: bfloat16 [3584, 8, 128], P(('groups', 'seq')), parts along dimension 0, may hold values from -6 to 6
- query_gain: float32 [128], replicated, may hold values from 0.5 to 5.5
- key_gain: float32 [128], replicated, may hold values from 0.5 to 5.5
Outputs:
- attended: bfloat16 [3584, 16, 128], P(('groups', 'seq')), parts along dimension 0
The draws below stay inside these ranges and needn't reach their ends.
There are 2 independent parts, one for each index of `groups`. The reference program is written for one: setup_inputs(seed, part) draws one part's arguments, and reference() takes and returns one part's arrays. A program takes and returns all parts, laid end to end along the dimension named above; an argument that names none is the same for every part. Nothing has to cross between parts.
All inputs are finite; a program needn't handle non-finite values.
Results may differ from the reference program's by a relative error of at most 0.0025.
The reference program's roundings to bfloat16 on the way (of `query_rot`, `key_rot` and `weights`) count: a program that leaves them out, or rounds other values in their place, can miss the bound.
Values may be sent and summed in bfloat16 or wider, within the bound.
No kernel may reach another device: no remote copies, remote signals or barrier semaphores. Data moves between devices by JAX's collectives and lax.ppermute only.
A program may use at most 64 MiB of HBM per device.

```python
import math
import jax
import jax.numpy as jnp
from jax import lax

HD = 128
KV_HEADS = 8
BLOCK = 896
HEADS = 16
TOKENS = 1792


def shared_keys(key):
    return jax.random.normal(jax.random.fold_in(key, 101), (TOKENS, KV_HEADS, HD), jnp.float32)


def draw_query_states(key, part):
    key = jax.random.fold_in(key, 3)
    queries = jax.random.normal(key, (TOKENS, HEADS, HD), jnp.float32)
    return jnp.clip(queries, -6.0, 6.0).astype(jnp.bfloat16)


def draw_key_states(key, part):
    base_normal = shared_keys(key)
    return jnp.clip(base_normal, -6.0, 6.0).astype(jnp.bfloat16)


def draw_query_gain(key, part):
    key = jax.random.fold_in(key, 11)
    return jax.random.uniform(key, (HD,), jnp.float32, 0.5, 2.0)


def draw_key_gain(key, part):
    key = jax.random.fold_in(key, 13)
    return jax.random.uniform(key, (HD,), jnp.float32, 0.5, 2.0)


def shard_levels(stream_key, dims, shards, least, high):
    loudness, own = 1.0, jax.random.fold_in(stream_key, 6)
    for dim, shards_of in shards:
        draws = jnp.exp(jax.random.uniform(jax.random.fold_in(own, dim), (shards_of,), jnp.float32, least / len(shards), high / len(shards)))
        loudness = loudness * jnp.repeat(draws, dims[dim] // shards_of).reshape([-1 if axis == dim else 1 for axis in range(len(dims))])
    return loudness


def centred(key, dims, scale, bound, shards=(), kind=jnp.bfloat16):
    array = jax.random.normal(key, dims, jnp.float32) * scale
    if len(shards) > 0:
        array = shard_levels(key, dims, shards, -0.22, 0.18) * array
    return jnp.clip(array, min=-bound, max=bound).astype(kind)


def setup_inputs(seed: int = 0, part: int = 0) -> dict:
    arg_keys = jax.random.split(jax.random.key(seed), 6)
    own_keys = jax.random.split(jax.random.fold_in(arg_keys[5], part), 6)
    query_states = draw_query_states(jax.random.fold_in(jax.random.fold_in(arg_keys[5], part), 71), part)
    key_states = draw_key_states(jax.random.fold_in(jax.random.fold_in(arg_keys[5], part), 71), part)
    value_states = centred(own_keys[2], (TOKENS, KV_HEADS, HD), 1.0, 6.0, ((0, 16),))
    query_gain = draw_query_gain(jax.random.fold_in(arg_keys[5], 71), part)
    key_gain = draw_key_gain(jax.random.fold_in(arg_keys[5], 71), part)
    return {"query_states": query_states, "key_states": key_states, "value_states": value_states, "query_gain": query_gain, "key_gain": key_gain}


ROPE_BASE = 1000000.0
EPSILON = 1e-06
MASKED = -1e+30

def rotate(tensor, norm_gain, positions):
    floats = tensor.astype(jnp.float32)
    mean_square = lax.optimization_barrier(jnp.mean(floats * floats, axis=-1, keepdims=True))
    normed = floats * lax.rsqrt(mean_square + EPSILON) * norm_gain
    halfway = tensor.shape[-1] // 2
    frequency = ROPE_BASE ** (-(jnp.arange(halfway, dtype=jnp.float32) * 2.0 / tensor.shape[-1]))
    angles = positions.astype(jnp.float32)[:, None] * frequency[None, :]
    cosine = jnp.cos(angles)[:, None, :]
    sine_vals = jnp.sin(angles)[:, None, :]
    first_half = normed[..., :halfway]
    second_half = normed[..., halfway:]
    rotated = jnp.concatenate([first_half * cosine - second_half * sine_vals, second_half * cosine + first_half * sine_vals], axis=-1)
    return rotated.astype(jnp.bfloat16)

def reference(query_states, key_states, value_states, query_gain, key_gain):
    length = query_states.shape[0]
    positions = jnp.arange(length, dtype=jnp.int32)
    query_rot = rotate(query_states, query_gain, positions)
    key_rot = rotate(key_states, key_gain, positions)
    group_size = HEADS // KV_HEADS
    factor = 1.0 / math.sqrt(HD)
    pieces = []
    for block_index in range(length // BLOCK):
        key_count = (block_index + 1) * BLOCK
        query_block = query_rot[block_index * BLOCK:(block_index + 1) * BLOCK].reshape(BLOCK, KV_HEADS, group_size, HD)
        row_ids = block_index * BLOCK + jnp.arange(BLOCK, dtype=jnp.int32)
        col_ids = jnp.arange(key_count, dtype=jnp.int32)
        allowed = col_ids[None, :] <= row_ids[:, None]

        def per_group(operands):
            query_group, key_group, value_group = operands
            scores = jnp.einsum('bgd,kd->gbk', query_group.astype(jnp.float32), key_group.astype(jnp.float32)) * factor
            scores = jnp.where(allowed[None], scores, MASKED)
            highest = lax.optimization_barrier(jnp.max(scores, axis=-1, keepdims=True))
            probs = jnp.where(allowed[None], jnp.exp(scores - highest), 0.0)
            total = lax.optimization_barrier(jnp.sum(probs, axis=-1))
            weights = probs.astype(jnp.bfloat16)
            summed = jnp.einsum('gbk,kd->bgd', weights.astype(jnp.float32), value_group.astype(jnp.float32))
            return summed / jnp.transpose(total)[:, :, None]
        grouped = lax.map(per_group, (jnp.transpose(query_block, (1, 0, 2, 3)), jnp.transpose(key_rot[:key_count], (1, 0, 2)), jnp.transpose(value_states[:key_count], (1, 0, 2))))
        pieces.append(jnp.transpose(grouped, (1, 0, 2, 3)).reshape(BLOCK, HEADS, HD).astype(jnp.bfloat16))
    return jnp.concatenate(pieces, axis=0)
```

```python
import functools
import math

import jax
import jax.numpy as jnp
import numpy as np
from jax import lax
from jax.experimental import pallas as pl
from jax.experimental.pallas import tpu as pltpu
from jax.sharding import PartitionSpec as P

ROPE_BASE = 1000000.0
EPSILON = 1e-06
MASKED = -1e30
VMEM_LIMIT = 48 * 1024 * 1024


def rope_table(length, width):
    half = width // 2
    frequency = np.float64(ROPE_BASE) ** (-(np.arange(half, dtype=np.float64) * 2.0 / width))
    angles = np.arange(length, dtype=np.float32)[:, None] * frequency.astype(np.float32)[None, :]
    wide = angles.astype(np.float64)
    return np.concatenate([np.cos(wide), np.sin(wide)], axis=-1).astype(np.float32)


def pack_kernel(rep, q_ref, k_ref, v_ref, table_ref, qg_ref, kg_ref, out_ref, qf_ref, kf_ref, vf_ref):
    tokens, heads, width = q_ref.shape
    kv_heads = k_ref.shape[1]
    chips, rows = out_ref.shape[:2]
    per_chip = rows - 2
    qf_ref[...] = q_ref[...].astype(jnp.float32).reshape(tokens * heads, width)
    kf_ref[...] = k_ref[...].astype(jnp.float32).reshape(tokens * kv_heads, width)
    vf_ref[...] = v_ref[...].astype(jnp.float32).reshape(tokens * kv_heads, width)
    table = table_ref[...]
    swapped = pltpu.roll(table, width // 2, 1)
    first = lax.broadcasted_iota(jnp.int32, table.shape, 1) < width // 2
    cosine = jnp.where(first, table, swapped)
    sine = jnp.where(first, -swapped, table)

    def rotate(floats, gain):
        mean_square = jnp.mean(floats * floats, axis=-1, keepdims=True)
        normed = floats * lax.rsqrt(mean_square + EPSILON) * gain
        turned = pltpu.roll(normed, width // 2, 1)
        return (normed * cosine + turned * sine).astype(jnp.bfloat16)

    query_gain, key_gain = qg_ref[...], kg_ref[...]
    for head in range(heads):
        floats = qf_ref[pl.ds(head, tokens, stride=heads), :]
        out_ref[head // per_chip, head % per_chip] = rotate(floats, query_gain)
    for head in range(kv_heads):
        floats = kf_ref[pl.ds(head, tokens, stride=kv_heads), :]
        rotated = rotate(floats, key_gain)
        values = vf_ref[pl.ds(head, tokens, stride=kv_heads), :].astype(jnp.bfloat16)
        for copy in range(rep):
            out_ref[head * rep + copy, per_chip] = rotated
            out_ref[head * rep + copy, per_chip + 1] = values


def attention_kernel(core_ref, x_ref, other_ref, out_ref):
    blocks, rows, tokens, width = x_ref.shape
    per_chip = rows - 2
    core = core_ref[0]
    scale = math.log2(math.e) / math.sqrt(width)
    keys_own = x_ref[:, per_chip].reshape(blocks * tokens, width)
    values_own = x_ref[:, per_chip + 1].reshape(blocks * tokens, width)
    keys_other = other_ref[:, 0].reshape(blocks * tokens, width)
    values_other = other_ref[:, 1].reshape(blocks * tokens, width)
    contract = (((1,), (1,)), ((), ()))
    for block in range(blocks):
        queries = x_ref[block, :per_chip].reshape(per_chip * tokens, width)
        reach = (block + 1) * tokens
        own = lax.dot_general(queries, keys_own[:reach], contract, preferred_element_type=jnp.float32)
        other = lax.dot_general(queries, keys_other[:reach], contract, preferred_element_type=jnp.float32)
        row = lax.broadcasted_iota(jnp.int32, (per_chip, tokens, reach), 1).reshape(per_chip * tokens, reach)
        column = lax.broadcasted_iota(jnp.int32, (per_chip * tokens, reach), 1)
        own = jnp.where(column <= row + block * tokens, own, MASKED)
        other = jnp.where(column < (block + core) * tokens, other, MASKED)
        highest = jnp.maximum(
            jnp.max(own, axis=-1, keepdims=True), jnp.max(other, axis=-1, keepdims=True)
        )
        probs_own = jnp.exp2((own - highest) * scale)
        probs_other = jnp.exp2((other - highest) * scale)
        total = jnp.sum(probs_own, axis=-1, keepdims=True) + jnp.sum(probs_other, axis=-1, keepdims=True)
        summed = jnp.dot(
            probs_own.astype(jnp.bfloat16), values_own[:reach], preferred_element_type=jnp.float32
        ) + jnp.dot(
            probs_other.astype(jnp.bfloat16), values_other[:reach], preferred_element_type=jnp.float32
        )
        out_ref[block] = (summed / total).astype(jnp.bfloat16).reshape(per_chip, tokens, width)


def looped_kernel(core_ref, x_ref, other_ref, out_ref):
    _, rows, tokens, width = x_ref.shape
    per_chip = rows - 2
    core = core_ref[0]
    block = pl.program_id(0)
    scale = math.log2(math.e) / math.sqrt(width)
    contract = (((1,), (1,)), ((), ()))
    queries = x_ref[block, :per_chip].reshape(per_chip * tokens, width)
    row = lax.broadcasted_iota(jnp.int32, (per_chip, tokens, tokens), 1).reshape(per_chip * tokens, tokens)
    column = lax.broadcasted_iota(jnp.int32, (per_chip * tokens, tokens), 1)

    def merge(carried, keys, values, allowed):
        highest, total, weighted = carried
        scores = lax.dot_general(queries, keys, contract, preferred_element_type=jnp.float32)
        scores = jnp.where(allowed, scores, MASKED)
        new = jnp.maximum(highest, jnp.max(scores, axis=-1, keepdims=True))
        probs = jnp.exp2((scores - new) * scale)
        factor = jnp.exp2((highest - new) * scale)
        total = total * factor + jnp.sum(probs, axis=-1, keepdims=True)
        summed = jnp.dot(probs.astype(jnp.bfloat16), values, preferred_element_type=jnp.float32)
        return new, total, weighted * factor + summed

    def advance(index, carried):
        behind = (block - index) * tokens
        carried = merge(carried, x_ref[index, per_chip], x_ref[index, per_chip + 1], column <= row + behind)
        return merge(carried, other_ref[index, 0], other_ref[index, 1], column < behind + core * tokens)

    initial = (
        jnp.full((per_chip * tokens, 1), MASKED, jnp.float32),
        jnp.zeros((per_chip * tokens, 1), jnp.float32),
        jnp.zeros((per_chip * tokens, width), jnp.float32),
    )
    _, total, weighted = lax.fori_loop(0, block + 1, advance, initial)
    out_ref[block] = (weighted / total).astype(jnp.bfloat16).reshape(per_chip, tokens, width)


def on_device(length, devices, query_states, key_states, value_states, query_gain, key_gain):
    tokens, heads, width = query_states.shape
    kv_heads = key_states.shape[1]
    chips = devices // 2
    per_chip = heads // chips
    rep = (heads // kv_heads) // per_chip
    me = lax.axis_index("seq")
    core = lax.rem(me, 2)
    same_core = [list(range(start, devices, 2)) for start in range(2)]
    swap = [(device, device ^ 1) for device in range(devices)]
    table = lax.dynamic_slice_in_dim(jnp.asarray(rope_table(length, width)), me * tokens, tokens, 0)
    vmem = pl.BlockSpec(memory_space=pltpu.VMEM)
    packed = pl.pallas_call(
        functools.partial(pack_kernel, rep),
        out_shape=jax.ShapeDtypeStruct((chips, per_chip + 2, tokens, width), jnp.bfloat16),
        in_specs=[vmem] * 6,
        out_specs=vmem,
        scratch_shapes=[
            pltpu.VMEM((tokens * heads, width), jnp.float32),
            pltpu.VMEM((tokens * kv_heads, width), jnp.float32),
            pltpu.VMEM((tokens * kv_heads, width), jnp.float32),
        ],
        compiler_params=pltpu.CompilerParams(vmem_limit_bytes=VMEM_LIMIT),
        name="pack",
    )(query_states, key_states, value_states, table, query_gain[None], key_gain[None])
    arrived = lax.all_to_all(
        packed, "seq", split_axis=0, concat_axis=0, axis_index_groups=same_core, tiled=True
    )
    other = lax.ppermute(arrived[:, per_chip:], "seq", swap)
    short = chips <= 8
    attended = pl.pallas_call(
        attention_kernel if short else looped_kernel,
        grid=() if short else (chips,),
        out_shape=jax.ShapeDtypeStruct((chips, per_chip, tokens, width), jnp.bfloat16),
        in_specs=[pl.BlockSpec(memory_space=pltpu.SMEM), vmem, vmem],
        out_specs=vmem,
        compiler_params=pltpu.CompilerParams(vmem_limit_bytes=VMEM_LIMIT),
        name="attention",
    )(core[None], arrived, other)
    returned = lax.all_to_all(
        attended, "seq", split_axis=0, concat_axis=0, axis_index_groups=same_core, tiled=True
    )
    return jnp.transpose(returned.reshape(heads, tokens, width), (1, 0, 2))


def solution(mesh):
    devices = mesh.shape["seq"]
    groups = mesh.shape["groups"]
    placed = P(("groups", "seq"), None, None)

    def run(query_states, key_states, value_states, query_gain, key_gain):
        length = query_states.shape[0] // groups
        return jax.shard_map(
            functools.partial(on_device, length, devices),
            mesh=mesh,
            in_specs=(placed, placed, placed, P(), P()),
            out_specs=placed,
            check_vma=False,
        )(query_states, key_states, value_states, query_gain, key_gain)

    return run
```

```python
import functools
import math

import jax
import jax.numpy as jnp
import numpy as np
from jax import lax
from jax.experimental import pallas as pl
from jax.experimental.pallas import tpu as pltpu
from jax.sharding import PartitionSpec as P

ROPE_BASE = 1000000.0
EPSILON = 1e-06
MASKED = -1e30
PACK_VMEM = 56 * 1024 * 1024
VMEM_LIMIT = 24 * 1024 * 1024
VMEM = pl.BlockSpec(memory_space=pltpu.VMEM)
SMEM = pl.BlockSpec(memory_space=pltpu.SMEM)
ANY = pl.BlockSpec(memory_space=pl.ANY)


def rope_table(length, width):
    half = width // 2
    frequency = np.float64(ROPE_BASE) ** (-(np.arange(half, dtype=np.float64) * 2.0 / width))
    angles = np.arange(length, dtype=np.float32)[:, None] * frequency.astype(np.float32)[None, :]
    wide = angles.astype(np.float64)
    return np.concatenate([np.cos(wide), np.sin(wide)], axis=-1).astype(np.float32)


def pack_kernel(chips, me_ref, q_hbm, k_hbm, v_hbm, table_hbm, qg_ref, kg_ref, *refs):
    query_outs, pair_outs = refs[:chips], refs[chips : 2 * chips]
    q_ref, k_ref, v_ref, table_ref, qf_ref, kf_ref, vf_ref, sems = refs[2 * chips :]
    tokens, heads, width = q_ref.shape
    kv_heads = k_ref.shape[1]
    per_chip = heads // chips
    me = me_ref[0]
    chip = me // 2
    copies = [
        pltpu.make_async_copy(table_hbm.at[pl.ds(pl.multiple_of(me * tokens, 8), tokens)], table_ref, sems.at[0]),
        pltpu.make_async_copy(k_hbm, k_ref, sems.at[1]),
        pltpu.make_async_copy(v_hbm, v_ref, sems.at[2]),
        pltpu.make_async_copy(q_hbm, q_ref, sems.at[3]),
    ]
    for copy in copies:
        copy.start()
    copies[0].wait()
    table = table_ref[...]
    swapped = pltpu.roll(table, width // 2, 1)
    first = lax.broadcasted_iota(jnp.int32, table.shape, 1) < width // 2
    cosine = jnp.where(first, table, swapped)
    sine = jnp.where(first, -swapped, table)

    def rotate(floats, gain):
        mean_square = jnp.mean(floats * floats, axis=-1, keepdims=True)
        normed = floats * lax.rsqrt(mean_square + EPSILON) * gain
        turned = pltpu.roll(normed, width // 2, 1)
        return (normed * cosine + turned * sine).astype(jnp.bfloat16)

    query_gain, key_gain = qg_ref[...], kg_ref[...]
    copies[1].wait()
    kf_ref[...] = k_ref[...].astype(jnp.float32).reshape(tokens * kv_heads, width)
    copies[2].wait()
    vf_ref[...] = v_ref[...].astype(jnp.float32).reshape(tokens * kv_heads, width)
    for step in range(chips):
        head = (chip ^ step) * kv_heads // chips
        pair_outs[step][0] = rotate(kf_ref[pl.ds(head, tokens, stride=kv_heads), :], key_gain)
        pair_outs[step][1] = vf_ref[pl.ds(head, tokens, stride=kv_heads), :].astype(jnp.bfloat16)
    copies[3].wait()
    qf_ref[...] = q_ref[...].astype(jnp.float32).reshape(tokens * heads, width)
    for step in range(chips):
        for row in range(per_chip):
            head = (chip ^ step) * per_chip + row
            query_outs[step][row] = rotate(qf_ref[pl.ds(head, tokens, stride=heads), :], query_gain)


def gather_blocks(chips, me_ref, refs, scratches):
    chip = me_ref[0] // 2
    for scratch, parts in zip(scratches, refs):
        for step in range(chips):
            scratch[chip ^ step] = parts[step][...]


def scatter_blocks(chips, me_ref, scratch, outs):
    chip = me_ref[0] // 2
    for step in range(chips):
        outs[step][...] = scratch[chip ^ step]


def attention_kernel(chips, me_ref, *refs):
    outs, (q_ref, own_ref, other_ref, out_ref) = refs[3 * chips : 4 * chips], refs[4 * chips :]
    gather_blocks(chips, me_ref, [refs[i * chips : (i + 1) * chips] for i in range(3)], (q_ref, own_ref, other_ref))
    blocks, per_chip, tokens, width = q_ref.shape
    core = lax.rem(me_ref[0], 2)
    scale = math.log2(math.e) / math.sqrt(width)
    keys_own, values_own, keys_other, values_other = [
        ref[:, i].reshape(blocks * tokens, width) for ref in (own_ref, other_ref) for i in range(2)
    ]
    contract = (((1,), (1,)), ((), ()))
    for block in range(blocks):
        queries = q_ref[block].reshape(per_chip * tokens, width)
        reach = (block + 1) * tokens
        own = lax.dot_general(queries, keys_own[:reach], contract, preferred_element_type=jnp.float32)
        other = lax.dot_general(queries, keys_other[:reach], contract, preferred_element_type=jnp.float32)
        row = lax.broadcasted_iota(jnp.int32, (per_chip, tokens, reach), 1).reshape(per_chip * tokens, reach)
        column = lax.broadcasted_iota(jnp.int32, (per_chip * tokens, reach), 1)
        own = jnp.where(column <= row + block * tokens, own, MASKED)
        other = jnp.where(column < (block + core) * tokens, other, MASKED)
        highest = jnp.maximum(
            jnp.max(own, axis=-1, keepdims=True), jnp.max(other, axis=-1, keepdims=True)
        )
        probs_own = jnp.exp2((own - highest) * scale)
        probs_other = jnp.exp2((other - highest) * scale)
        total = jnp.sum(probs_own, axis=-1, keepdims=True) + jnp.sum(probs_other, axis=-1, keepdims=True)
        summed = jnp.dot(
            probs_own.astype(jnp.bfloat16), values_own[:reach], preferred_element_type=jnp.float32
        ) + jnp.dot(
            probs_other.astype(jnp.bfloat16), values_other[:reach], preferred_element_type=jnp.float32
        )
        out_ref[block] = (summed / total).astype(jnp.bfloat16).reshape(per_chip, tokens, width)
    scatter_blocks(chips, me_ref, out_ref, outs)


def looped_kernel(chips, me_ref, *refs):
    outs, (q_ref, own_ref, other_ref, out_ref) = refs[3 * chips : 4 * chips], refs[4 * chips :]
    gather_blocks(chips, me_ref, [refs[i * chips : (i + 1) * chips] for i in range(3)], (q_ref, own_ref, other_ref))
    blocks, per_chip, tokens, width = q_ref.shape
    core = lax.rem(me_ref[0], 2)
    scale = math.log2(math.e) / math.sqrt(width)
    contract = (((1,), (1,)), ((), ()))
    row = lax.broadcasted_iota(jnp.int32, (per_chip, tokens, tokens), 1).reshape(per_chip * tokens, tokens)
    column = lax.broadcasted_iota(jnp.int32, (per_chip * tokens, tokens), 1)

    def query_block(block, _):
        queries = q_ref[block].reshape(per_chip * tokens, width)

        def merge(carried, keys, values, allowed):
            highest, total, weighted = carried
            scores = lax.dot_general(queries, keys, contract, preferred_element_type=jnp.float32)
            scores = jnp.where(allowed, scores, MASKED)
            new = jnp.maximum(highest, jnp.max(scores, axis=-1, keepdims=True))
            probs = jnp.exp2((scores - new) * scale)
            factor = jnp.exp2((highest - new) * scale)
            total = total * factor + jnp.sum(probs, axis=-1, keepdims=True)
            summed = jnp.dot(probs.astype(jnp.bfloat16), values, preferred_element_type=jnp.float32)
            return new, total, weighted * factor + summed

        def advance(index, carried):
            behind = (block - index) * tokens
            carried = merge(carried, own_ref[index, 0], own_ref[index, 1], column <= row + behind)
            return merge(carried, other_ref[index, 0], other_ref[index, 1], column < behind + core * tokens)

        initial = (
            jnp.full((per_chip * tokens, 1), MASKED, jnp.float32),
            jnp.zeros((per_chip * tokens, 1), jnp.float32),
            jnp.zeros((per_chip * tokens, width), jnp.float32),
        )
        _, total, weighted = lax.fori_loop(0, block + 1, advance, initial)
        out_ref[block] = (weighted / total).astype(jnp.bfloat16).reshape(per_chip, tokens, width)
        return 0

    lax.fori_loop(0, blocks, query_block, 0)
    scatter_blocks(chips, me_ref, out_ref, outs)


def unpack_kernel(chips, me_ref, *refs):
    parts, (out_ref, floats_ref) = refs[:chips], refs[chips:]
    tokens, heads, width = out_ref.shape
    per_chip = heads // chips
    chip = me_ref[0] // 2
    for step in range(chips):
        for row in range(per_chip):
            head = (chip ^ step) * per_chip + row
            floats_ref[pl.ds(head, tokens, stride=heads), :] = parts[step][row].astype(jnp.float32)
    out_ref[...] = floats_ref[...].reshape(tokens, heads, width).astype(jnp.bfloat16)


def on_device(length, devices, query_states, key_states, value_states, query_gain, key_gain):
    tokens, heads, width = query_states.shape
    kv_heads = key_states.shape[1]
    chips = devices // 2
    per_chip = heads // chips
    me = lax.axis_index("seq")[None]
    params = pltpu.CompilerParams(vmem_limit_bytes=VMEM_LIMIT)
    bf16, f32 = jnp.bfloat16, jnp.float32
    queries_type = jax.ShapeDtypeStruct((per_chip, tokens, width), bf16)
    pair_type = jax.ShapeDtypeStruct((2, tokens, width), bf16)
    order = sorted(range(1, chips), key=lambda step: -step)

    def to_partner(step, array):
        links = [(device, ((device // 2) ^ step) * 2 + device % 2) for device in range(devices)]
        return lax.ppermute(array, "seq", links)

    packed = pl.pallas_call(
        functools.partial(pack_kernel, chips),
        out_shape=[queries_type] * chips + [pair_type] * chips,
        in_specs=[SMEM, ANY, ANY, ANY, ANY, VMEM, VMEM],
        out_specs=[VMEM] * (2 * chips),
        scratch_shapes=[
            pltpu.VMEM((tokens, heads, width), bf16),
            pltpu.VMEM((tokens, kv_heads, width), bf16),
            pltpu.VMEM((tokens, kv_heads, width), bf16),
            pltpu.VMEM((tokens, width), f32),
            pltpu.VMEM((tokens * heads, width), f32),
            pltpu.VMEM((tokens * kv_heads, width), f32),
            pltpu.VMEM((tokens * kv_heads, width), f32),
            pltpu.SemaphoreType.DMA((4,)),
        ],
        compiler_params=pltpu.CompilerParams(vmem_limit_bytes=PACK_VMEM),
        name="pack",
    )(me, query_states, key_states, value_states, rope_table(length, width), query_gain[None], key_gain[None])
    queries, own = list(packed[:chips]), list(packed[chips:])
    for step in order:
        own[step] = to_partner(step, own[step])
    for step in order:
        queries[step] = to_partner(step, queries[step])
    swap = [(device, device ^ 1) for device in range(devices)]
    other = [lax.ppermute(pair, "seq", swap) for pair in own]
    attended = pl.pallas_call(
        functools.partial(attention_kernel if chips <= 8 else looped_kernel, chips),
        out_shape=[queries_type] * chips,
        in_specs=[SMEM] + [VMEM] * (3 * chips),
        out_specs=[VMEM] * chips,
        scratch_shapes=[
            pltpu.VMEM((chips, per_chip, tokens, width), bf16),
            pltpu.VMEM((chips, 2, tokens, width), bf16),
            pltpu.VMEM((chips, 2, tokens, width), bf16),
            pltpu.VMEM((chips, per_chip, tokens, width), bf16),
        ],
        compiler_params=params,
        name="attention",
    )(me, *queries, *own, *other)
    returned = list(attended)
    for step in order:
        returned[step] = to_partner(step, returned[step])
    return pl.pallas_call(
        functools.partial(unpack_kernel, chips),
        out_shape=jax.ShapeDtypeStruct((tokens, heads, width), bf16),
        in_specs=[SMEM] + [VMEM] * chips,
        out_specs=VMEM,
        scratch_shapes=[pltpu.VMEM((tokens * heads, width), f32)],
        compiler_params=params,
        name="unpack",
    )(me, *returned)


def solution(mesh):
    devices = mesh.shape["seq"]
    groups = mesh.shape["groups"]
    placed = P(("groups", "seq"), None, None)

    def run(query_states, key_states, value_states, query_gain, key_gain):
        length = query_states.shape[0] // groups
        return jax.shard_map(
            functools.partial(on_device, length, devices),
            mesh=mesh,
            in_specs=(placed, placed, placed, P(), P()),
            out_specs=placed,
            check_vma=False,
        )(query_states, key_states, value_states, query_gain, key_gain)

    return run
```

```python
import functools
import math

import jax
import jax.numpy as jnp
import numpy as np
from jax import lax
from jax.experimental import pallas as pl
from jax.experimental.pallas import tpu as pltpu
from jax.sharding import PartitionSpec as P

ROPE_BASE = 1000000.0
EPSILON = 1e-06
MASKED = -1e30
VMEM_LIMIT = 24 * 1024 * 1024
PACK_VMEM = 56 * 1024 * 1024
VMEM = pl.BlockSpec(memory_space=pltpu.VMEM)
SMEM = pl.BlockSpec(memory_space=pltpu.SMEM)
ANY = pl.BlockSpec(memory_space=pl.ANY)
CONTRACT = (((1,), (1,)), ((), ()))


def rope_table(length, width):
    half = width // 2
    frequency = np.float64(ROPE_BASE) ** (-(np.arange(half, dtype=np.float64) * 2.0 / width))
    angles = np.arange(length, dtype=np.float32)[:, None] * frequency.astype(np.float32)[None, :]
    wide = angles.astype(np.float64)
    return np.concatenate([np.cos(wide), np.sin(wide)], axis=-1).astype(np.float32)


def pack_kernel(rep, q_ref, k_ref, v_ref, table_ref, qg_ref, kg_ref, out_ref, qf_ref, kf_ref, vf_ref):
    tokens, heads, width = q_ref.shape
    kv_heads = k_ref.shape[1]
    chips, rows = out_ref.shape[:2]
    per_chip = rows - 2
    qf_ref[...] = q_ref[...].astype(jnp.float32).reshape(tokens * heads, width)
    kf_ref[...] = k_ref[...].astype(jnp.float32).reshape(tokens * kv_heads, width)
    vf_ref[...] = v_ref[...].astype(jnp.float32).reshape(tokens * kv_heads, width)
    table = table_ref[...]
    swapped = pltpu.roll(table, width // 2, 1)
    first = lax.broadcasted_iota(jnp.int32, table.shape, 1) < width // 2
    cosine = jnp.where(first, table, swapped)
    sine = jnp.where(first, -swapped, table)

    def rotate(floats, gain):
        mean_square = jnp.mean(floats * floats, axis=-1, keepdims=True)
        normed = floats * lax.rsqrt(mean_square + EPSILON) * gain
        turned = pltpu.roll(normed, width // 2, 1)
        return (normed * cosine + turned * sine).astype(jnp.bfloat16)

    query_gain, key_gain = qg_ref[...], kg_ref[...]
    for head in range(heads):
        floats = qf_ref[pl.ds(head, tokens, stride=heads), :]
        out_ref[head // per_chip, head % per_chip] = rotate(floats, query_gain)
    for head in range(kv_heads):
        floats = kf_ref[pl.ds(head, tokens, stride=kv_heads), :]
        rotated = rotate(floats, key_gain)
        values = vf_ref[pl.ds(head, tokens, stride=kv_heads), :].astype(jnp.bfloat16)
        for copy in range(rep):
            out_ref[head * rep + copy, per_chip] = rotated
            out_ref[head * rep + copy, per_chip + 1] = values


def looped_kernel(core_ref, x_ref, other_ref, out_ref):
    _, rows, tokens, width = x_ref.shape
    per_chip = rows - 2
    core = core_ref[0]
    block = pl.program_id(0)
    scale = math.log2(math.e) / math.sqrt(width)
    queries = x_ref[block, :per_chip].reshape(per_chip * tokens, width)
    row = lax.broadcasted_iota(jnp.int32, (per_chip, tokens, tokens), 1).reshape(per_chip * tokens, tokens)
    column = lax.broadcasted_iota(jnp.int32, (per_chip * tokens, tokens), 1)

    def merge(carried, keys, values, allowed):
        highest, total, weighted = carried
        scores = lax.dot_general(queries, keys, CONTRACT, preferred_element_type=jnp.float32)
        scores = jnp.where(allowed, scores, MASKED)
        new = jnp.maximum(highest, jnp.max(scores, axis=-1, keepdims=True))
        probs = jnp.exp2((scores - new) * scale)
        factor = jnp.exp2((highest - new) * scale)
        total = total * factor + jnp.sum(probs, axis=-1, keepdims=True)
        summed = jnp.dot(probs.astype(jnp.bfloat16), values, preferred_element_type=jnp.float32)
        return new, total, weighted * factor + summed

    def advance(index, carried):
        behind = (block - index) * tokens
        carried = merge(carried, x_ref[index, per_chip], x_ref[index, per_chip + 1], column <= row + behind)
        return merge(carried, other_ref[index, 0], other_ref[index, 1], column < behind + core * tokens)

    initial = (
        jnp.full((per_chip * tokens, 1), MASKED, jnp.float32),
        jnp.zeros((per_chip * tokens, 1), jnp.float32),
        jnp.zeros((per_chip * tokens, width), jnp.float32),
    )
    _, total, weighted = lax.fori_loop(0, block + 1, advance, initial)
    out_ref[block] = (weighted / total).astype(jnp.bfloat16).reshape(per_chip, tokens, width)


def general_plan(length, devices, query_states, key_states, value_states, query_gain, key_gain):
    tokens, heads, width = query_states.shape
    kv_heads = key_states.shape[1]
    chips = devices // 2
    per_chip = heads // chips
    rep = (heads // kv_heads) // per_chip
    me = lax.axis_index("seq")
    core = lax.rem(me, 2)
    same_core = [list(range(start, devices, 2)) for start in range(2)]
    swap = [(device, device ^ 1) for device in range(devices)]
    table = lax.dynamic_slice_in_dim(jnp.asarray(rope_table(length, width)), me * tokens, tokens, 0)
    packed = pl.pallas_call(
        functools.partial(pack_kernel, rep),
        out_shape=jax.ShapeDtypeStruct((chips, per_chip + 2, tokens, width), jnp.bfloat16),
        in_specs=[VMEM] * 6,
        out_specs=VMEM,
        scratch_shapes=[
            pltpu.VMEM((tokens * heads, width), jnp.float32),
            pltpu.VMEM((tokens * kv_heads, width), jnp.float32),
            pltpu.VMEM((tokens * kv_heads, width), jnp.float32),
        ],
        compiler_params=pltpu.CompilerParams(vmem_limit_bytes=48 * 1024 * 1024),
        name="pack",
    )(query_states, key_states, value_states, table, query_gain[None], key_gain[None])
    arrived = lax.all_to_all(
        packed, "seq", split_axis=0, concat_axis=0, axis_index_groups=same_core, tiled=True
    )
    other = lax.ppermute(arrived[:, per_chip:], "seq", swap)
    attended = pl.pallas_call(
        looped_kernel,
        grid=(chips,),
        out_shape=jax.ShapeDtypeStruct((chips, per_chip, tokens, width), jnp.bfloat16),
        in_specs=[SMEM, VMEM, VMEM],
        out_specs=VMEM,
        compiler_params=pltpu.CompilerParams(vmem_limit_bytes=48 * 1024 * 1024),
        name="attention",
    )(core[None], arrived, other)
    returned = lax.all_to_all(
        attended, "seq", split_axis=0, concat_axis=0, axis_index_groups=same_core, tiled=True
    )
    return jnp.transpose(returned.reshape(heads, tokens, width), (1, 0, 2))


def rope_factors(table):
    half = table.shape[1] // 2
    swapped = pltpu.roll(table, half, 1)
    first = lax.broadcasted_iota(jnp.int32, table.shape, 1) < half
    return jnp.where(first, table, swapped), jnp.where(first, -swapped, table)


def rotate(floats, gain, cosine, sine):
    mean_square = jnp.mean(floats * floats, axis=-1, keepdims=True)
    normed = floats * lax.rsqrt(mean_square + EPSILON) * gain
    turned = pltpu.roll(normed, floats.shape[1] // 2, 1)
    return (normed * cosine + turned * sine).astype(jnp.bfloat16)


def pack_pairs_kernel(me_ref, k_hbm, v_hbm, table_hbm, gain_ref, *refs):
    outs, (k_ref, v_ref, table_ref, kf_ref, vf_ref, sems) = refs[:-6], refs[-6:]
    tokens, kv_heads, width = k_ref.shape
    me = me_ref[0]
    place, core = lax.rem(me, kv_heads), lax.rem(me, 2)
    start = pl.multiple_of(me * tokens, 8)
    copies = [
        pltpu.make_async_copy(v_hbm, v_ref, sems.at[0]),
        pltpu.make_async_copy(k_hbm, k_ref, sems.at[1]),
        pltpu.make_async_copy(table_hbm.at[pl.ds(start, tokens)], table_ref, sems.at[2]),
    ]
    for copy in copies:
        copy.start()
    heads = [
        (step, side, ((place // 2) ^ step) * 2 + lax.rem(core + side, 2)) for step in range(len(outs)) for side in range(2)
    ]
    copies[0].wait()
    vf_ref[...] = v_ref[...].astype(jnp.float32).reshape(tokens * kv_heads, width)
    for step, side, head in heads:
        outs[step][side, 1] = vf_ref[pl.ds(head, tokens, stride=kv_heads), :].astype(jnp.bfloat16)
    copies[1].wait()
    kf_ref[...] = k_ref[...].astype(jnp.float32).reshape(tokens * kv_heads, width)
    copies[2].wait()
    cosine, sine = rope_factors(table_ref[...])
    for step, side, head in heads:
        floats = kf_ref[pl.ds(head, tokens, stride=kv_heads), :]
        outs[step][side, 0] = rotate(floats, gain_ref[...], cosine, sine)


def pack_all_kernel(me_ref, q_hbm, table_hbm, gain_ref, *refs):
    pairs, (out_ref, q_ref, table_ref, qf_ref, sems) = refs[:-5], refs[-5:]
    tokens, heads, width = q_ref.shape
    owners, rows = out_ref.shape[:2]
    group = rows - 2
    me = me_ref[0]
    place, core = lax.rem(me, owners), lax.rem(me, 2)
    start = pl.multiple_of(me * tokens, 8)
    copies = [
        pltpu.make_async_copy(table_hbm.at[pl.ds(start, tokens)], table_ref, sems.at[0]),
        pltpu.make_async_copy(q_hbm, q_ref, sems.at[1]),
    ]
    for copy in copies:
        copy.start()
    for step, pair in enumerate(pairs):
        for side in range(2):
            out_ref[((place // 2) ^ step) * 2 + lax.rem(core + side, 2), group:] = pair[side]
    copies[0].wait()
    cosine, sine = rope_factors(table_ref[...])
    copies[1].wait()
    qf_ref[...] = q_ref[...].astype(jnp.float32).reshape(tokens * heads, width)
    for head in range(heads):
        floats = qf_ref[pl.ds(head, tokens, stride=heads), :]
        out_ref[head // group, head % group] = rotate(floats, gain_ref[...], cosine, sine)


def near_kernel(x_ref, highest_ref, total_ref, weighted_ref):
    blocks, rows, tokens, width = x_ref.shape
    group = rows - 2
    scale = math.log2(math.e) / math.sqrt(width)
    keys = x_ref[:, group].reshape(blocks * tokens, width)
    values = x_ref[:, group + 1].reshape(blocks * tokens, width)
    for block in range(blocks):
        queries = x_ref[block, :group].reshape(group * tokens, width)
        reach = (block + 1) * tokens
        scores = lax.dot_general(queries, keys[:reach], CONTRACT, preferred_element_type=jnp.float32)
        row = lax.broadcasted_iota(jnp.int32, (group, tokens, reach), 1).reshape(group * tokens, reach)
        column = lax.broadcasted_iota(jnp.int32, (group * tokens, reach), 1)
        scores = jnp.where(column <= row + block * tokens, scores, MASKED)
        highest = jnp.max(scores, axis=-1, keepdims=True)
        probs = jnp.exp2((scores - highest) * scale)
        highest_ref[block] = highest
        total_ref[block] = jnp.sum(probs, axis=-1, keepdims=True)
        weighted_ref[block] = jnp.dot(
            probs.astype(jnp.bfloat16), values[:reach], preferred_element_type=jnp.float32
        )


def far_kernel(half, me_ref, x_ref, highest_ref, total_ref, weighted_ref, *refs):
    steps = (len(refs) - 1) // 2
    mine, neighbours, out_ref = refs[:steps], refs[steps : 2 * steps], refs[2 * steps]
    blocks, rows, tokens, width = x_ref.shape
    group = rows - 2
    scale = math.log2(math.e) / math.sqrt(width)
    upper = me_ref[0] >= half

    def finish(block, weighted, total):
        out_ref[block] = (weighted / total).astype(jnp.bfloat16).reshape(group, tokens, width)

    @pl.when(upper)
    def _():
        keys = jnp.concatenate([ref[0, 0] for ref in mine] + [ref[1, 0] for ref in neighbours], axis=0)
        values = jnp.concatenate([ref[0, 1] for ref in mine] + [ref[1, 1] for ref in neighbours], axis=0)
        for block in range(blocks):
            queries = x_ref[block, :group].reshape(group * tokens, width)
            scores = lax.dot_general(queries, keys, CONTRACT, preferred_element_type=jnp.float32)
            before = highest_ref[block]
            highest = jnp.maximum(before, jnp.max(scores, axis=-1, keepdims=True))
            probs = jnp.exp2((scores - highest) * scale)
            factor = jnp.exp2((before - highest) * scale)
            total = total_ref[block] * factor + jnp.sum(probs, axis=-1, keepdims=True)
            summed = jnp.dot(probs.astype(jnp.bfloat16), values, preferred_element_type=jnp.float32)
            finish(block, weighted_ref[block] * factor + summed, total)

    @pl.when(jnp.logical_not(upper))
    def _():
        for block in range(blocks):
            finish(block, weighted_ref[block], total_ref[block])


def halves_plan(length, devices, query_states, key_states, value_states, query_gain, key_gain):
    tokens, heads, width = query_states.shape
    kv_heads = key_states.shape[1]
    group = heads // kv_heads
    half = devices // 2
    steps = half // 2
    bf16, f32 = jnp.bfloat16, jnp.float32
    me = lax.axis_index("seq")[None]
    table = jnp.asarray(rope_table(length, width))
    halves = [list(range(half)), list(range(half, devices))]
    own_copies = pltpu.CompilerParams(vmem_limit_bytes=PACK_VMEM)
    params = pltpu.CompilerParams(vmem_limit_bytes=VMEM_LIMIT)
    pairs = pl.pallas_call(
        pack_pairs_kernel,
        out_shape=[jax.ShapeDtypeStruct((2, 2, tokens, width), bf16)] * steps,
        in_specs=[SMEM, ANY, ANY, ANY, VMEM],
        out_specs=[VMEM] * steps,
        scratch_shapes=[
            pltpu.VMEM((tokens, kv_heads, width), bf16),
            pltpu.VMEM((tokens, kv_heads, width), bf16),
            pltpu.VMEM((tokens, width), f32),
            pltpu.VMEM((tokens * kv_heads, width), f32),
            pltpu.VMEM((tokens * kv_heads, width), f32),
            pltpu.SemaphoreType.DMA((3,)),
        ],
        compiler_params=own_copies,
        name="pack_pairs",
    )(me, key_states, value_states, table, key_gain[None])
    mine = [
        lax.ppermute(
            pair,
            "seq",
            [(device, half + ((device // 2) ^ step) * 2 + device % 2) for device in range(half)],
        )
        for step, pair in enumerate(pairs)
    ]
    packed = pl.pallas_call(
        pack_all_kernel,
        out_shape=jax.ShapeDtypeStruct((half, group + 2, tokens, width), bf16),
        in_specs=[SMEM, ANY, ANY, VMEM] + [VMEM] * steps,
        out_specs=VMEM,
        scratch_shapes=[
            pltpu.VMEM((tokens, heads, width), bf16),
            pltpu.VMEM((tokens, width), f32),
            pltpu.VMEM((tokens * heads, width), f32),
            pltpu.SemaphoreType.DMA((2,)),
        ],
        compiler_params=own_copies,
        name="pack_all",
    )(me, query_states, table, query_gain[None], *pairs)
    arrived = lax.all_to_all(packed, "seq", split_axis=0, concat_axis=0, axis_index_groups=halves, tiled=True)
    rows = group * tokens
    near = pl.pallas_call(
        near_kernel,
        out_shape=[
            jax.ShapeDtypeStruct((half, rows, 1), f32),
            jax.ShapeDtypeStruct((half, rows, 1), f32),
            jax.ShapeDtypeStruct((half, rows, width), f32),
        ],
        in_specs=[VMEM],
        out_specs=[VMEM] * 3,
        compiler_params=params,
        name="near",
    )(arrived)
    near, mine = lax.optimization_barrier((near, mine))
    swap = [(device, device ^ 1) for device in range(half, devices)]
    neighbours = [lax.ppermute(pair, "seq", swap) for pair in mine]
    attended = pl.pallas_call(
        functools.partial(far_kernel, half),
        out_shape=jax.ShapeDtypeStruct((half, group, tokens, width), bf16),
        in_specs=[SMEM] + [VMEM] * (4 + 2 * steps),
        out_specs=VMEM,
        compiler_params=params,
        name="far",
    )(me, arrived, *near, *mine, *neighbours)
    returned = lax.all_to_all(attended, "seq", split_axis=0, concat_axis=0, axis_index_groups=halves, tiled=True)
    return jnp.transpose(returned.reshape(heads, tokens, width), (1, 0, 2))


def solution(mesh):
    devices = mesh.shape["seq"]
    groups = mesh.shape["groups"]
    placed = P(("groups", "seq"), None, None)

    def run(query_states, key_states, value_states, query_gain, key_gain):
        length = query_states.shape[0] // groups
        plan = halves_plan if devices == 2 * key_states.shape[1] else general_plan
        return jax.shard_map(
            functools.partial(plan, length, devices),
            mesh=mesh,
            in_specs=(placed, placed, placed, P(), P()),
            out_specs=placed,
            check_vma=False,
        )(query_states, key_states, value_states, query_gain, key_gain)

    return run
```

```python
import functools
import math

import jax
import jax.numpy as jnp
import numpy as np
from jax import lax
from jax.experimental import pallas as pl
from jax.experimental.pallas import tpu as pltpu
from jax.sharding import PartitionSpec as P

ROPE_BASE = 1000000.0
EPSILON = 1e-06
MASKED = -1e30
VMEM_LIMIT = 24 * 1024 * 1024
PACK_VMEM = 56 * 1024 * 1024
VMEM = pl.BlockSpec(memory_space=pltpu.VMEM)
SMEM = pl.BlockSpec(memory_space=pltpu.SMEM)
HBM = pl.BlockSpec(memory_space=pltpu.HBM)
CONTRACT = (((1,), (1,)), ((), ()))


def rope_table(length, width):
    half = width // 2
    frequency = np.float64(ROPE_BASE) ** (-(np.arange(half, dtype=np.float64) * 2.0 / width))
    angles = np.arange(length, dtype=np.float32)[:, None] * frequency.astype(np.float32)[None, :]
    wide = angles.astype(np.float64)
    return np.concatenate([np.cos(wide), np.sin(wide)], axis=-1).astype(np.float32)


def pack_kernel(rep, q_ref, k_ref, v_ref, table_ref, qg_ref, kg_ref, out_ref, qf_ref, kf_ref, vf_ref):
    tokens, heads, width = q_ref.shape
    kv_heads = k_ref.shape[1]
    chips, rows = out_ref.shape[:2]
    per_chip = rows - 2
    qf_ref[...] = q_ref[...].astype(jnp.float32).reshape(tokens * heads, width)
    kf_ref[...] = k_ref[...].astype(jnp.float32).reshape(tokens * kv_heads, width)
    vf_ref[...] = v_ref[...].astype(jnp.float32).reshape(tokens * kv_heads, width)
    table = table_ref[...]
    swapped = pltpu.roll(table, width // 2, 1)
    first = lax.broadcasted_iota(jnp.int32, table.shape, 1) < width // 2
    cosine = jnp.where(first, table, swapped)
    sine = jnp.where(first, -swapped, table)

    def rotate(floats, gain):
        mean_square = jnp.mean(floats * floats, axis=-1, keepdims=True)
        normed = floats * lax.rsqrt(mean_square + EPSILON) * gain
        turned = pltpu.roll(normed, width // 2, 1)
        return (normed * cosine + turned * sine).astype(jnp.bfloat16)

    query_gain, key_gain = qg_ref[...], kg_ref[...]
    for head in range(heads):
        floats = qf_ref[pl.ds(head, tokens, stride=heads), :]
        out_ref[head // per_chip, head % per_chip] = rotate(floats, query_gain)
    for head in range(kv_heads):
        floats = kf_ref[pl.ds(head, tokens, stride=kv_heads), :]
        rotated = rotate(floats, key_gain)
        values = vf_ref[pl.ds(head, tokens, stride=kv_heads), :].astype(jnp.bfloat16)
        for copy in range(rep):
            out_ref[head * rep + copy, per_chip] = rotated
            out_ref[head * rep + copy, per_chip + 1] = values


def looped_kernel(core_ref, x_ref, other_ref, out_ref):
    _, rows, tokens, width = x_ref.shape
    per_chip = rows - 2
    core = core_ref[0]
    block = pl.program_id(0)
    scale = math.log2(math.e) / math.sqrt(width)
    queries = x_ref[block, :per_chip].reshape(per_chip * tokens, width)
    row = lax.broadcasted_iota(jnp.int32, (per_chip, tokens, tokens), 1).reshape(per_chip * tokens, tokens)
    column = lax.broadcasted_iota(jnp.int32, (per_chip * tokens, tokens), 1)

    def merge(carried, keys, values, allowed):
        highest, total, weighted = carried
        scores = lax.dot_general(queries, keys, CONTRACT, preferred_element_type=jnp.float32)
        scores = jnp.where(allowed, scores, MASKED)
        new = jnp.maximum(highest, jnp.max(scores, axis=-1, keepdims=True))
        probs = jnp.exp2((scores - new) * scale)
        factor = jnp.exp2((highest - new) * scale)
        total = total * factor + jnp.sum(probs, axis=-1, keepdims=True)
        summed = jnp.dot(probs.astype(jnp.bfloat16), values, preferred_element_type=jnp.float32)
        return new, total, weighted * factor + summed

    def advance(index, carried):
        behind = (block - index) * tokens
        carried = merge(carried, x_ref[index, per_chip], x_ref[index, per_chip + 1], column <= row + behind)
        return merge(carried, other_ref[index, 0], other_ref[index, 1], column < behind + core * tokens)

    initial = (
        jnp.full((per_chip * tokens, 1), MASKED, jnp.float32),
        jnp.zeros((per_chip * tokens, 1), jnp.float32),
        jnp.zeros((per_chip * tokens, width), jnp.float32),
    )
    _, total, weighted = lax.fori_loop(0, block + 1, advance, initial)
    out_ref[block] = (weighted / total).astype(jnp.bfloat16).reshape(per_chip, tokens, width)


def general_plan(length, devices, query_states, key_states, value_states, query_gain, key_gain):
    tokens, heads, width = query_states.shape
    kv_heads = key_states.shape[1]
    chips = devices // 2
    per_chip = heads // chips
    rep = (heads // kv_heads) // per_chip
    me = lax.axis_index("seq")
    core = lax.rem(me, 2)
    same_core = [list(range(start, devices, 2)) for start in range(2)]
    swap = [(device, device ^ 1) for device in range(devices)]
    table = lax.dynamic_slice_in_dim(jnp.asarray(rope_table(length, width)), me * tokens, tokens, 0)
    packed = pl.pallas_call(
        functools.partial(pack_kernel, rep),
        out_shape=jax.ShapeDtypeStruct((chips, per_chip + 2, tokens, width), jnp.bfloat16),
        in_specs=[VMEM] * 6,
        out_specs=VMEM,
        scratch_shapes=[
            pltpu.VMEM((tokens * heads, width), jnp.float32),
            pltpu.VMEM((tokens * kv_heads, width), jnp.float32),
            pltpu.VMEM((tokens * kv_heads, width), jnp.float32),
        ],
        compiler_params=pltpu.CompilerParams(vmem_limit_bytes=48 * 1024 * 1024),
        name="pack",
    )(query_states, key_states, value_states, table, query_gain[None], key_gain[None])
    arrived = lax.all_to_all(
        packed, "seq", split_axis=0, concat_axis=0, axis_index_groups=same_core, tiled=True
    )
    other = lax.ppermute(arrived[:, per_chip:], "seq", swap)
    attended = pl.pallas_call(
        looped_kernel,
        grid=(chips,),
        out_shape=jax.ShapeDtypeStruct((chips, per_chip, tokens, width), jnp.bfloat16),
        in_specs=[SMEM, VMEM, VMEM],
        out_specs=VMEM,
        compiler_params=pltpu.CompilerParams(vmem_limit_bytes=48 * 1024 * 1024),
        name="attention",
    )(core[None], arrived, other)
    returned = lax.all_to_all(
        attended, "seq", split_axis=0, concat_axis=0, axis_index_groups=same_core, tiled=True
    )
    return jnp.transpose(returned.reshape(heads, tokens, width), (1, 0, 2))


def rope_factors(table):
    half = table.shape[1] // 2
    swapped = pltpu.roll(table, half, 1)
    first = lax.broadcasted_iota(jnp.int32, table.shape, 1) < half
    return jnp.where(first, table, swapped), jnp.where(first, -swapped, table)


def normalize(rows):
    floats = rows.astype(jnp.float32)
    squares = floats * floats
    large = squares.astype(jnp.bfloat16)
    small = (squares - large.astype(jnp.float32)).astype(jnp.bfloat16)
    width = rows.shape[1]
    ones = jnp.ones((2 * width, width), jnp.bfloat16)
    added = jnp.dot(jnp.concatenate([large, small], axis=1), ones, preferred_element_type=jnp.float32)
    return floats * lax.rsqrt(added * (1.0 / width) + EPSILON)


def turn(normed, gain, cosine, sine):
    scaled = normed * gain
    return (scaled * cosine + pltpu.roll(scaled, scaled.shape[1] // 2, 1) * sine).astype(jnp.bfloat16)


def send_kernel(me_ref, q_hbm, k_hbm, v_hbm, table_hbm, query_gain_ref, key_gain_ref, *refs):
    outs, (q_ref, k_ref, v_ref, table_ref, qf_ref, kf_ref, vf_ref, sems) = refs[:-8], refs[-8:]
    steps = len(outs) // 2
    pairs, fulls = outs[:steps], outs[steps:]
    tokens, heads, width = q_ref.shape
    kv_heads, per_chip = k_ref.shape[1], pairs[0].shape[0]
    first, per_full = 2 * per_chip, heads // steps
    me = me_ref[0]
    chip = lax.rem(me // 2, steps)
    start = pl.multiple_of(me * tokens, 8)
    copies = [
        pltpu.make_async_copy(k_hbm, k_ref, sems.at[0]),
        pltpu.make_async_copy(table_hbm.at[pl.ds(start, tokens)], table_ref, sems.at[1]),
        pltpu.make_async_copy(v_hbm, v_ref, sems.at[2]),
        pltpu.make_async_copy(q_hbm, q_ref, sems.at[3]),
    ]
    for copy in copies:
        copy.start()
    copies[0].wait()
    kf_ref[...] = normalize(k_ref[...].reshape(tokens * kv_heads, width))
    copies[1].wait()
    cosine, sine = rope_factors(table_ref[...])
    copies[2].wait()
    vf_ref[...] = v_ref[...].astype(jnp.float32).reshape(tokens * kv_heads, width)
    for step in range(steps):
        for row in range(per_chip):
            head = (chip ^ step) * per_chip + row
            keys = turn(kf_ref[pl.ds(head, tokens, stride=kv_heads), :], key_gain_ref[...], cosine, sine)
            values = vf_ref[pl.ds(head, tokens, stride=kv_heads), :].astype(jnp.bfloat16)
            pairs[step][row, 0] = keys
            fulls[step][2 * row] = keys
            pairs[step][row, 1] = values
            fulls[step][2 * row + 1] = values
    copies[3].wait()
    qf_ref[...] = normalize(q_ref[...].reshape(tokens * heads, width))
    for step in range(steps):
        for row in range(per_full):
            normed = qf_ref[pl.ds((chip ^ step) * per_full + row, tokens, stride=heads), :]
            fulls[step][first + row] = turn(normed, query_gain_ref[...], cosine, sine)


def order_kernel(me_ref, *refs):
    arrays, (pair_ref, query_ref) = refs[:-2], refs[-2:]
    steps, per_chip = pair_ref.shape[0], pair_ref.shape[1]
    chip = lax.rem(me_ref[0] // 2, steps)
    for step in range(steps):
        pair_ref[chip ^ step] = arrays[step][: 2 * per_chip].reshape(pair_ref.shape[1:])
        query_ref[chip ^ step] = arrays[step][2 * per_chip :].reshape(query_ref.shape[1:])


def near_kernel(me_ref, q_ref, own_ref, other_ref, highest_ref, total_ref, weighted_ref):
    blocks, kv_heads, group, tokens, width = q_ref.shape
    core = lax.rem(me_ref[0], 2)
    scale = math.log2(math.e) / math.sqrt(width)
    rows = group * tokens
    for head in range(kv_heads):
        keys_own, values_own, keys_other, values_other = [
            ref[:, head, i].reshape(blocks * tokens, width) for ref in (own_ref, other_ref) for i in range(2)
        ]
        for block in range(blocks):
            queries = q_ref[block, head].reshape(rows, width)
            reach = (block + 1) * tokens
            own = lax.dot_general(queries, keys_own[:reach], CONTRACT, preferred_element_type=jnp.float32)
            other = lax.dot_general(queries, keys_other[:reach], CONTRACT, preferred_element_type=jnp.float32)
            row = lax.broadcasted_iota(jnp.int32, (group, tokens, reach), 1).reshape(rows, reach)
            column = lax.broadcasted_iota(jnp.int32, (rows, reach), 1)
            own = jnp.where(column <= row + block * tokens, own, MASKED)
            other = jnp.where(column < (block + core) * tokens, other, MASKED)
            highest = jnp.maximum(
                jnp.max(own, axis=-1, keepdims=True), jnp.max(other, axis=-1, keepdims=True)
            )
            probs_own = jnp.exp2((own - highest) * scale)
            probs_other = jnp.exp2((other - highest) * scale)
            place = pl.ds(block * rows, rows)
            highest_ref[head, place] = highest
            total_ref[head, place] = jnp.sum(probs_own, axis=-1, keepdims=True) + jnp.sum(
                probs_other, axis=-1, keepdims=True
            )
            weighted_ref[head, place] = jnp.dot(
                probs_own.astype(jnp.bfloat16), values_own[:reach], preferred_element_type=jnp.float32
            ) + jnp.dot(
                probs_other.astype(jnp.bfloat16), values_other[:reach], preferred_element_type=jnp.float32
            )


def add_far(q_ref, highest_ref, total_ref, weighted_ref, pairs, store):
    blocks, kv_heads, group, tokens, width = q_ref.shape
    scale = math.log2(math.e) / math.sqrt(width)
    rows = group * tokens
    for head in range(kv_heads):
        keys = jnp.concatenate([ref[head, 0] for ref in pairs], axis=0)
        values = jnp.concatenate([ref[head, 1] for ref in pairs], axis=0)
        for block in range(blocks):
            queries = q_ref[block, head].reshape(rows, width)
            place = pl.ds(block * rows, rows)
            scores = lax.dot_general(queries, keys, CONTRACT, preferred_element_type=jnp.float32)
            before = highest_ref[head, place]
            highest = jnp.maximum(before, jnp.max(scores, axis=-1, keepdims=True))
            probs = jnp.exp2((scores - highest) * scale)
            factor = jnp.exp2((before - highest) * scale)
            total = total_ref[head, place] * factor + jnp.sum(probs, axis=-1, keepdims=True)
            summed = jnp.dot(probs.astype(jnp.bfloat16), values, preferred_element_type=jnp.float32)
            store(head, block, highest, total, weighted_ref[head, place] * factor + summed)


def far_kernel(half, me_ref, q_ref, highest_ref, total_ref, weighted_ref, *refs):
    pairs, outs = refs[:-3], refs[-3:]
    rows = q_ref.shape[2] * q_ref.shape[3]

    def store(head, block, *values):
        for ref, value in zip(outs, values):
            ref[head, pl.ds(block * rows, rows)] = value

    @pl.when(me_ref[0] >= half)
    def _():
        add_far(q_ref, highest_ref, total_ref, weighted_ref, pairs, store)

    @pl.when(me_ref[0] < half)
    def _():
        for ref, before in zip(outs, (highest_ref, total_ref, weighted_ref)):
            ref[...] = before[...]


def last_kernel(half, me_ref, q_ref, highest_ref, total_ref, weighted_ref, *refs):
    blocks, kv_heads, group, tokens, width = q_ref.shape
    pairs, outs, out_ref = refs[: -blocks - 1], refs[-blocks - 1 : -1], refs[-1]
    rows = group * tokens

    def store(head, block, highest, total, weighted):
        result = (weighted / total).astype(jnp.bfloat16).reshape(group, tokens, width)
        out_ref[block, pl.ds(head * group, group)] = result

    @pl.when(me_ref[0] >= half)
    def _():
        add_far(q_ref, highest_ref, total_ref, weighted_ref, pairs, store)

    @pl.when(me_ref[0] < half)
    def _():
        for head in range(kv_heads):
            for block in range(blocks):
                place = pl.ds(block * rows, rows)
                store(head, block, None, total_ref[head, place], weighted_ref[head, place])

    chip = lax.rem(me_ref[0] // 2, blocks)
    for step in range(blocks):
        outs[step][...] = out_ref[chip ^ step]


def unpack_kernel(me_ref, *refs):
    parts, (out_ref, floats_ref) = refs[:-2], refs[-2:]
    tokens, heads, width = out_ref.shape
    steps = len(parts)
    per_chip = heads // steps
    chip = lax.rem(me_ref[0] // 2, steps)
    for step in range(steps):
        for row in range(per_chip):
            head = (chip ^ step) * per_chip + row
            floats_ref[pl.ds(head, tokens, stride=heads), :] = parts[step][row].astype(jnp.float32)
    out_ref[...] = floats_ref[...].reshape(tokens, heads, width).astype(jnp.bfloat16)


def halves_plan(length, devices, query_states, key_states, value_states, query_gain, key_gain):
    tokens, heads, width = query_states.shape
    kv_heads = key_states.shape[1]
    group = heads // kv_heads
    half = devices // 2
    steps = half // 2
    per_chip = kv_heads // steps
    bf16, f32 = jnp.bfloat16, jnp.float32
    me = lax.axis_index("seq")[None]

    def call(kernel, name, outs, *operands, scratch=(), specs=None, limit=VMEM_LIMIT):
        return pl.pallas_call(
            kernel,
            out_shape=outs,
            in_specs=specs or [SMEM] + [VMEM] * len(operands),
            out_specs=jax.tree.map(lambda _: VMEM, outs),
            scratch_shapes=scratch,
            compiler_params=pltpu.CompilerParams(vmem_limit_bytes=limit),
            name=name,
        )(me, *operands)

    def to_upper(step, array):
        links = [(device, half + ((device // 2) ^ step) * 2 + device % 2) for device in range(half)]
        return lax.ppermute(array, "seq", links)

    def to_chip(step, array):
        links = [(device, ((device // 2) ^ step) * 2 + device % 2) for device in range(devices)]
        return lax.ppermute(array, "seq", links)

    def to_core(array, lowest):
        return lax.ppermute(array, "seq", [(device, device ^ 1) for device in range(lowest, devices)])

    shape = jax.ShapeDtypeStruct
    packed = call(
        send_kernel,
        "send",
        [shape((per_chip, 2, tokens, width), bf16)] * steps
        + [shape((per_chip * (2 + group), tokens, width), bf16)] * steps,
        query_states,
        key_states,
        value_states,
        jnp.asarray(rope_table(length, width)),
        query_gain[None],
        key_gain[None],
        specs=[SMEM, HBM, HBM, HBM, HBM, VMEM, VMEM],
        scratch=[
            pltpu.VMEM((tokens, heads, width), bf16),
            pltpu.VMEM((tokens, kv_heads, width), bf16),
            pltpu.VMEM((tokens, kv_heads, width), bf16),
            pltpu.VMEM((tokens, width), f32),
            pltpu.VMEM((tokens * heads, width), f32),
            pltpu.VMEM((tokens * kv_heads, width), f32),
            pltpu.VMEM((tokens * kv_heads, width), f32),
            pltpu.SemaphoreType.DMA((4,)),
        ],
        limit=PACK_VMEM,
    )
    pairs, near = packed[:steps], packed[steps:]
    early = steps // 2
    far = [to_upper(step, pairs[step]) for step in range(early)]
    near = [near[0]] + [to_chip(step, near[step]) for step in range(1, steps)]
    near, far, late = lax.optimization_barrier((near, far, pairs[early:]))
    far = far + [to_upper(early + i, pair) for i, pair in enumerate(late)]
    own, queries = call(
        order_kernel,
        "order",
        [shape((steps, per_chip, 2, tokens, width), bf16), shape((steps, per_chip, group, tokens, width), bf16)],
        *near,
    )
    other = to_core(own, 0)
    far_other = [to_core(pair, half) for pair in far[:early]]
    rows = steps * group * tokens
    state = [
        shape((per_chip, rows, 1), f32),
        shape((per_chip, rows, 1), f32),
        shape((per_chip, rows, width), f32),
    ]
    carried = call(near_kernel, "near", state, queries, own, other)
    carried = call(
        functools.partial(far_kernel, half), "far", state, queries, *carried, *far[:early], *far_other
    )
    carried, last = lax.optimization_barrier((carried, far[early:]))
    last_other = [to_core(pair, half) for pair in last]
    returned = call(
        functools.partial(last_kernel, half),
        "last",
        [shape((per_chip * group, tokens, width), bf16)] * steps,
        queries,
        *carried,
        *last,
        *last_other,
        scratch=[pltpu.VMEM((steps, per_chip * group, tokens, width), bf16)],
    )
    returned = [returned[0]] + [to_chip(step, returned[step]) for step in range(1, steps)]
    return call(
        unpack_kernel,
        "unpack",
        shape((tokens, heads, width), bf16),
        *returned,
        scratch=[pltpu.VMEM((tokens * heads, width), f32)],
    )


def solution(mesh):
    devices = mesh.shape["seq"]
    groups = mesh.shape["groups"]
    placed = P(("groups", "seq"), None, None)

    def run(query_states, key_states, value_states, query_gain, key_gain):
        length = query_states.shape[0] // groups
        plan = halves_plan if devices == 2 * key_states.shape[1] else general_plan
        return jax.shard_map(
            functools.partial(plan, length, devices),
            mesh=mesh,
            in_specs=(placed, placed, placed, P(), P()),
            out_specs=placed,
            check_vma=False,
        )(query_states, key_states, value_states, query_gain, key_gain)

    return run
```

```python
import functools
import math

import jax
import jax.numpy as jnp
import numpy as np
from jax import lax
from jax.experimental import pallas as pl
from jax.experimental.pallas import tpu as pltpu
from jax.sharding import PartitionSpec as P

ROPE_BASE = 1000000.0
EPSILON = 1e-06
MASKED = -1e30
VMEM_LIMIT = 24 * 1024 * 1024
PACK_VMEM = 56 * 1024 * 1024
VMEM = pl.BlockSpec(memory_space=pltpu.VMEM)
SMEM = pl.BlockSpec(memory_space=pltpu.SMEM)
HBM = pl.BlockSpec(memory_space=pltpu.HBM)
CONTRACT = (((1,), (1,)), ((), ()))


def rope_table(length, width):
    half = width // 2
    frequency = np.float64(ROPE_BASE) ** (-(np.arange(half, dtype=np.float64) * 2.0 / width))
    angles = np.arange(length, dtype=np.float32)[:, None] * frequency.astype(np.float32)[None, :]
    wide = angles.astype(np.float64)
    return np.concatenate([np.cos(wide), np.sin(wide)], axis=-1).astype(np.float32)


def pack_kernel(rep, q_ref, k_ref, v_ref, table_ref, qg_ref, kg_ref, out_ref, qf_ref, kf_ref, vf_ref):
    tokens, heads, width = q_ref.shape
    kv_heads = k_ref.shape[1]
    chips, rows = out_ref.shape[:2]
    per_chip = rows - 2
    qf_ref[...] = q_ref[...].astype(jnp.float32).reshape(tokens * heads, width)
    kf_ref[...] = k_ref[...].astype(jnp.float32).reshape(tokens * kv_heads, width)
    vf_ref[...] = v_ref[...].astype(jnp.float32).reshape(tokens * kv_heads, width)
    table = table_ref[...]
    swapped = pltpu.roll(table, width // 2, 1)
    first = lax.broadcasted_iota(jnp.int32, table.shape, 1) < width // 2
    cosine = jnp.where(first, table, swapped)
    sine = jnp.where(first, -swapped, table)

    def rotate(floats, gain):
        mean_square = jnp.mean(floats * floats, axis=-1, keepdims=True)
        normed = floats * lax.rsqrt(mean_square + EPSILON) * gain
        turned = pltpu.roll(normed, width // 2, 1)
        return (normed * cosine + turned * sine).astype(jnp.bfloat16)

    query_gain, key_gain = qg_ref[...], kg_ref[...]
    for head in range(heads):
        floats = qf_ref[pl.ds(head, tokens, stride=heads), :]
        out_ref[head // per_chip, head % per_chip] = rotate(floats, query_gain)
    for head in range(kv_heads):
        floats = kf_ref[pl.ds(head, tokens, stride=kv_heads), :]
        rotated = rotate(floats, key_gain)
        values = vf_ref[pl.ds(head, tokens, stride=kv_heads), :].astype(jnp.bfloat16)
        for copy in range(rep):
            out_ref[head * rep + copy, per_chip] = rotated
            out_ref[head * rep + copy, per_chip + 1] = values


def looped_kernel(core_ref, x_ref, other_ref, out_ref):
    _, rows, tokens, width = x_ref.shape
    per_chip = rows - 2
    core = core_ref[0]
    block = pl.program_id(0)
    scale = math.log2(math.e) / math.sqrt(width)
    queries = x_ref[block, :per_chip].reshape(per_chip * tokens, width)
    row = lax.broadcasted_iota(jnp.int32, (per_chip, tokens, tokens), 1).reshape(per_chip * tokens, tokens)
    column = lax.broadcasted_iota(jnp.int32, (per_chip * tokens, tokens), 1)

    def merge(carried, keys, values, allowed):
        highest, total, weighted = carried
        scores = lax.dot_general(queries, keys, CONTRACT, preferred_element_type=jnp.float32)
        scores = jnp.where(allowed, scores, MASKED)
        new = jnp.maximum(highest, jnp.max(scores, axis=-1, keepdims=True))
        probs = jnp.exp2((scores - new) * scale)
        factor = jnp.exp2((highest - new) * scale)
        total = total * factor + jnp.sum(probs, axis=-1, keepdims=True)
        summed = jnp.dot(probs.astype(jnp.bfloat16), values, preferred_element_type=jnp.float32)
        return new, total, weighted * factor + summed

    def advance(index, carried):
        behind = (block - index) * tokens
        carried = merge(carried, x_ref[index, per_chip], x_ref[index, per_chip + 1], column <= row + behind)
        return merge(carried, other_ref[index, 0], other_ref[index, 1], column < behind + core * tokens)

    initial = (
        jnp.full((per_chip * tokens, 1), MASKED, jnp.float32),
        jnp.zeros((per_chip * tokens, 1), jnp.float32),
        jnp.zeros((per_chip * tokens, width), jnp.float32),
    )
    _, total, weighted = lax.fori_loop(0, block + 1, advance, initial)
    out_ref[block] = (weighted / total).astype(jnp.bfloat16).reshape(per_chip, tokens, width)


def general_plan(length, devices, query_states, key_states, value_states, query_gain, key_gain):
    tokens, heads, width = query_states.shape
    kv_heads = key_states.shape[1]
    chips = devices // 2
    per_chip = heads // chips
    rep = (heads // kv_heads) // per_chip
    me = lax.axis_index("seq")
    core = lax.rem(me, 2)
    same_core = [list(range(start, devices, 2)) for start in range(2)]
    swap = [(device, device ^ 1) for device in range(devices)]
    table = lax.dynamic_slice_in_dim(jnp.asarray(rope_table(length, width)), me * tokens, tokens, 0)
    packed = pl.pallas_call(
        functools.partial(pack_kernel, rep),
        out_shape=jax.ShapeDtypeStruct((chips, per_chip + 2, tokens, width), jnp.bfloat16),
        in_specs=[VMEM] * 6,
        out_specs=VMEM,
        scratch_shapes=[
            pltpu.VMEM((tokens * heads, width), jnp.float32),
            pltpu.VMEM((tokens * kv_heads, width), jnp.float32),
            pltpu.VMEM((tokens * kv_heads, width), jnp.float32),
        ],
        compiler_params=pltpu.CompilerParams(vmem_limit_bytes=48 * 1024 * 1024),
        name="pack",
    )(query_states, key_states, value_states, table, query_gain[None], key_gain[None])
    arrived = lax.all_to_all(
        packed, "seq", split_axis=0, concat_axis=0, axis_index_groups=same_core, tiled=True
    )
    other = lax.ppermute(arrived[:, per_chip:], "seq", swap)
    attended = pl.pallas_call(
        looped_kernel,
        grid=(chips,),
        out_shape=jax.ShapeDtypeStruct((chips, per_chip, tokens, width), jnp.bfloat16),
        in_specs=[SMEM, VMEM, VMEM],
        out_specs=VMEM,
        compiler_params=pltpu.CompilerParams(vmem_limit_bytes=48 * 1024 * 1024),
        name="attention",
    )(core[None], arrived, other)
    returned = lax.all_to_all(
        attended, "seq", split_axis=0, concat_axis=0, axis_index_groups=same_core, tiled=True
    )
    return jnp.transpose(returned.reshape(heads, tokens, width), (1, 0, 2))


def rope_factors(table):
    half = table.shape[1] // 2
    swapped = pltpu.roll(table, half, 1)
    first = lax.broadcasted_iota(jnp.int32, table.shape, 1) < half
    return jnp.where(first, table, swapped), jnp.where(first, -swapped, table)


def normalize(rows):
    floats = rows.astype(jnp.float32)
    squares = floats * floats
    large = squares.astype(jnp.bfloat16)
    small = (squares - large.astype(jnp.float32)).astype(jnp.bfloat16)
    width = rows.shape[1]
    ones = jnp.ones((2 * width, width), jnp.bfloat16)
    added = jnp.dot(jnp.concatenate([large, small], axis=1), ones, preferred_element_type=jnp.float32)
    return floats * lax.rsqrt(added * (1.0 / width) + EPSILON)


def turn(normed, gain, cosine, sine):
    scaled = normed * gain
    return (scaled * cosine + pltpu.roll(scaled, scaled.shape[1] // 2, 1) * sine).astype(jnp.bfloat16)


def send_kernel(me_ref, q_hbm, k_hbm, v_hbm, table_hbm, query_gain_ref, key_gain_ref, *refs):
    outs, (q_ref, k_ref, v_ref, table_ref, qf_ref, kf_ref, vf_ref, sems) = refs[:-8], refs[-8:]
    tokens, heads, width = q_ref.shape
    kv_heads = k_ref.shape[1]
    crossing, near_ref = outs[:-1], outs[-1]
    half = len(crossing)
    per_chip = near_ref.shape[1] - 2
    me = me_ref[0]
    chip = me // 2
    base = chip // half * half
    start = pl.multiple_of(me * tokens, 8)
    copies = [
        pltpu.make_async_copy(k_hbm, k_ref, sems.at[0]),
        pltpu.make_async_copy(table_hbm.at[pl.ds(start, tokens)], table_ref, sems.at[1]),
        pltpu.make_async_copy(v_hbm, v_ref, sems.at[2]),
        pltpu.make_async_copy(q_hbm, q_ref, sems.at[3]),
    ]
    for copy in copies:
        copy.start()
    targets = [(chip ^ (half + step), ref) for step, ref in enumerate(crossing)]
    targets += [(base + place, near_ref.at[place]) for place in range(half)]
    copies[0].wait()
    kf_ref[...] = normalize(k_ref[...].reshape(tokens * kv_heads, width))
    copies[1].wait()
    cosine, sine = rope_factors(table_ref[...])
    copies[2].wait()
    vf_ref[...] = v_ref[...].astype(jnp.float32).reshape(tokens * kv_heads, width)
    for target, ref in targets:
        rows = pl.ds(target, tokens, stride=kv_heads)
        ref[per_chip] = turn(kf_ref[rows, :], key_gain_ref[...], cosine, sine)
        ref[per_chip + 1] = vf_ref[rows, :].astype(jnp.bfloat16)
    copies[3].wait()
    qf_ref[...] = normalize(q_ref[...].reshape(tokens * heads, width))
    for target, ref in targets:
        for row in range(per_chip):
            normed = qf_ref[pl.ds(target * per_chip + row, tokens, stride=heads), :]
            ref[row] = turn(normed, query_gain_ref[...], cosine, sine)


def order_kernel(me_ref, *refs):
    crossed, (near_ref, query_ref, pair_ref) = refs[:-3], refs[-3:]
    half, per_chip = len(crossed), query_ref.shape[1]
    chip = me_ref[0] // 2
    base = chip // half * half
    sources = [(chip ^ (half + step), ref) for step, ref in enumerate(crossed)]
    sources += [(base + place, near_ref.at[place]) for place in range(half)]
    for source, ref in sources:
        query_ref[source] = ref[:per_chip]
        pair_ref[source] = ref[per_chip:]


def attention_kernel(me_ref, q_ref, own_ref, other_ref, *refs):
    outs, out_ref = refs[:-1], refs[-1]
    crossing, near_ref = outs[:-1], outs[-1]
    blocks, per_chip, tokens, width = q_ref.shape
    chip, core = me_ref[0] // 2, lax.rem(me_ref[0], 2)
    scale = math.log2(math.e) / math.sqrt(width)
    keys_own, values_own, keys_other, values_other = [
        ref[:, i].reshape(blocks * tokens, width) for ref in (own_ref, other_ref) for i in range(2)
    ]
    rows = per_chip * tokens
    for block in range(blocks):
        queries = q_ref[block].reshape(rows, width)
        reach = (block + 1) * tokens
        own = lax.dot_general(queries, keys_own[:reach], CONTRACT, preferred_element_type=jnp.float32)
        other = lax.dot_general(queries, keys_other[:reach], CONTRACT, preferred_element_type=jnp.float32)
        row = lax.broadcasted_iota(jnp.int32, (per_chip, tokens, reach), 1).reshape(rows, reach)
        column = lax.broadcasted_iota(jnp.int32, (rows, reach), 1)
        own = jnp.where(column <= row + block * tokens, own, MASKED)
        other = jnp.where(column < (block + core) * tokens, other, MASKED)
        highest = jnp.maximum(
            jnp.max(own, axis=-1, keepdims=True), jnp.max(other, axis=-1, keepdims=True)
        )
        probs_own = jnp.exp2((own - highest) * scale)
        probs_other = jnp.exp2((other - highest) * scale)
        total = jnp.sum(probs_own, axis=-1, keepdims=True) + jnp.sum(probs_other, axis=-1, keepdims=True)
        summed = jnp.dot(
            probs_own.astype(jnp.bfloat16), values_own[:reach], preferred_element_type=jnp.float32
        ) + jnp.dot(
            probs_other.astype(jnp.bfloat16), values_other[:reach], preferred_element_type=jnp.float32
        )
        out_ref[block] = (summed / total).astype(jnp.bfloat16).reshape(per_chip, tokens, width)
    half = len(crossing)
    base = chip // half * half
    for step, ref in enumerate(crossing):
        ref[...] = out_ref[chip ^ (half + step)]
    near_ref[...] = out_ref[pl.ds(base, half)]


def unpack_kernel(me_ref, *refs):
    crossed, (near_ref, out_ref, floats_ref) = refs[:-3], refs[-3:]
    tokens, heads, width = out_ref.shape
    half, per_chip = len(crossed), near_ref.shape[1]
    chip = me_ref[0] // 2
    base = chip // half * half
    sources = [(base + place, near_ref.at[place]) for place in range(half)]
    sources += [(chip ^ (half + step), ref) for step, ref in enumerate(crossed)]
    for source, ref in sources:
        for row in range(per_chip):
            floats_ref[pl.ds(source * per_chip + row, tokens, stride=heads), :] = ref[row].astype(jnp.float32)
    out_ref[...] = floats_ref[...].reshape(tokens, heads, width).astype(jnp.bfloat16)


def short_plan(length, devices, query_states, key_states, value_states, query_gain, key_gain):
    tokens, heads, width = query_states.shape
    kv_heads = key_states.shape[1]
    chips = devices // 2
    half = chips // 2
    per_chip = heads // chips
    bf16, f32 = jnp.bfloat16, jnp.float32
    me = lax.axis_index("seq")[None]

    def call(kernel, name, outs, *operands, scratch=(), specs=None, limit=VMEM_LIMIT):
        return pl.pallas_call(
            kernel,
            out_shape=outs,
            in_specs=specs or [SMEM] + [VMEM] * len(operands),
            out_specs=jax.tree.map(lambda _: VMEM, outs),
            scratch_shapes=scratch,
            compiler_params=pltpu.CompilerParams(vmem_limit_bytes=limit),
            name=name,
        )(me, *operands)

    def exchange(crossing, near):
        links = [
            [(device, ((device // 2) ^ (half + step)) * 2 + device % 2) for device in range(devices)]
            for step in range(half)
        ]
        groups = [[(base + place) * 2 + core for place in range(half)] for base in (0, half) for core in range(2)]
        crossed = [lax.ppermute(array, "seq", links[step]) for step, array in enumerate(crossing)]
        return crossed + [
            lax.all_to_all(near, "seq", split_axis=0, concat_axis=0, axis_index_groups=groups, tiled=True)
        ]

    shape = jax.ShapeDtypeStruct
    *crossing, near = call(
        send_kernel,
        "send",
        [shape((per_chip + 2, tokens, width), bf16)] * half + [shape((half, per_chip + 2, tokens, width), bf16)],
        query_states,
        key_states,
        value_states,
        jnp.asarray(rope_table(length, width)),
        query_gain[None],
        key_gain[None],
        specs=[SMEM, HBM, HBM, HBM, HBM, VMEM, VMEM],
        scratch=[
            pltpu.VMEM((tokens, heads, width), bf16),
            pltpu.VMEM((tokens, kv_heads, width), bf16),
            pltpu.VMEM((tokens, kv_heads, width), bf16),
            pltpu.VMEM((tokens, width), f32),
            pltpu.VMEM((tokens * heads, width), f32),
            pltpu.VMEM((tokens * kv_heads, width), f32),
            pltpu.VMEM((tokens * kv_heads, width), f32),
            pltpu.SemaphoreType.DMA((4,)),
        ],
        limit=PACK_VMEM,
    )
    queries, own = call(
        order_kernel,
        "order",
        [shape((chips, per_chip, tokens, width), bf16), shape((chips, 2, tokens, width), bf16)],
        *exchange(crossing, near),
    )
    other = lax.ppermute(own, "seq", [(device, device ^ 1) for device in range(devices)])
    *crossing, near = call(
        attention_kernel,
        "attention",
        [shape((per_chip, tokens, width), bf16)] * half + [shape((half, per_chip, tokens, width), bf16)],
        queries,
        own,
        other,
        scratch=[pltpu.VMEM((chips, per_chip, tokens, width), bf16)],
    )
    return call(
        unpack_kernel,
        "unpack",
        shape((tokens, heads, width), bf16),
        *exchange(crossing, near),
        scratch=[pltpu.VMEM((tokens * heads, width), f32)],
    )


def solution(mesh):
    devices = mesh.shape["seq"]
    groups = mesh.shape["groups"]
    placed = P(("groups", "seq"), None, None)

    def run(query_states, key_states, value_states, query_gain, key_gain):
        length = query_states.shape[0] // groups
        plan = short_plan if devices == 2 * key_states.shape[1] else general_plan
        return jax.shard_map(
            functools.partial(plan, length, devices),
            mesh=mesh,
            in_specs=(placed, placed, placed, P(), P()),
            out_specs=placed,
            check_vma=False,
        )(query_states, key_states, value_states, query_gain, key_gain)

    return run
```

```python
import functools
import math

import jax
import jax.numpy as jnp
import numpy as np
from jax import lax
from jax.experimental import pallas as pl
from jax.experimental.pallas import tpu as pltpu
from jax.sharding import PartitionSpec as P

ROPE_BASE = 1000000.0
EPSILON = 1e-06
MASKED = -1e30
VMEM_LIMIT = 24 * 1024 * 1024
PACK_VMEM = 56 * 1024 * 1024
VMEM = pl.BlockSpec(memory_space=pltpu.VMEM)
SMEM = pl.BlockSpec(memory_space=pltpu.SMEM)
HBM = pl.BlockSpec(memory_space=pltpu.HBM)
CONTRACT = (((1,), (1,)), ((), ()))


def rope_table(length, width):
    half = width // 2
    frequency = np.float64(ROPE_BASE) ** (-(np.arange(half, dtype=np.float64) * 2.0 / width))
    angles = np.arange(length, dtype=np.float32)[:, None] * frequency.astype(np.float32)[None, :]
    wide = angles.astype(np.float64)
    return np.concatenate([np.cos(wide), np.sin(wide)], axis=-1).astype(np.float32)


def pack_kernel(rep, q_ref, k_ref, v_ref, table_ref, qg_ref, kg_ref, out_ref, qf_ref, kf_ref, vf_ref):
    tokens, heads, width = q_ref.shape
    kv_heads = k_ref.shape[1]
    chips, rows = out_ref.shape[:2]
    per_chip = rows - 2
    qf_ref[...] = q_ref[...].astype(jnp.float32).reshape(tokens * heads, width)
    kf_ref[...] = k_ref[...].astype(jnp.float32).reshape(tokens * kv_heads, width)
    vf_ref[...] = v_ref[...].astype(jnp.float32).reshape(tokens * kv_heads, width)
    table = table_ref[...]
    swapped = pltpu.roll(table, width // 2, 1)
    first = lax.broadcasted_iota(jnp.int32, table.shape, 1) < width // 2
    cosine = jnp.where(first, table, swapped)
    sine = jnp.where(first, -swapped, table)

    def rotate(floats, gain):
        mean_square = jnp.mean(floats * floats, axis=-1, keepdims=True)
        normed = floats * lax.rsqrt(mean_square + EPSILON) * gain
        turned = pltpu.roll(normed, width // 2, 1)
        return (normed * cosine + turned * sine).astype(jnp.bfloat16)

    query_gain, key_gain = qg_ref[...], kg_ref[...]
    for head in range(heads):
        floats = qf_ref[pl.ds(head, tokens, stride=heads), :]
        out_ref[head // per_chip, head % per_chip] = rotate(floats, query_gain)
    for head in range(kv_heads):
        floats = kf_ref[pl.ds(head, tokens, stride=kv_heads), :]
        rotated = rotate(floats, key_gain)
        values = vf_ref[pl.ds(head, tokens, stride=kv_heads), :].astype(jnp.bfloat16)
        for copy in range(rep):
            out_ref[head * rep + copy, per_chip] = rotated
            out_ref[head * rep + copy, per_chip + 1] = values


def looped_kernel(core_ref, x_ref, other_ref, out_ref):
    _, rows, tokens, width = x_ref.shape
    per_chip = rows - 2
    core = core_ref[0]
    block = pl.program_id(0)
    scale = math.log2(math.e) / math.sqrt(width)
    queries = x_ref[block, :per_chip].reshape(per_chip * tokens, width)
    row = lax.broadcasted_iota(jnp.int32, (per_chip, tokens, tokens), 1).reshape(per_chip * tokens, tokens)
    column = lax.broadcasted_iota(jnp.int32, (per_chip * tokens, tokens), 1)

    def merge(carried, keys, values, allowed):
        highest, total, weighted = carried
        scores = lax.dot_general(queries, keys, CONTRACT, preferred_element_type=jnp.float32)
        scores = jnp.where(allowed, scores, MASKED)
        new = jnp.maximum(highest, jnp.max(scores, axis=-1, keepdims=True))
        probs = jnp.exp2((scores - new) * scale)
        factor = jnp.exp2((highest - new) * scale)
        total = total * factor + jnp.sum(probs, axis=-1, keepdims=True)
        summed = jnp.dot(probs.astype(jnp.bfloat16), values, preferred_element_type=jnp.float32)
        return new, total, weighted * factor + summed

    def advance(index, carried):
        behind = (block - index) * tokens
        carried = merge(carried, x_ref[index, per_chip], x_ref[index, per_chip + 1], column <= row + behind)
        return merge(carried, other_ref[index, 0], other_ref[index, 1], column < behind + core * tokens)

    initial = (
        jnp.full((per_chip * tokens, 1), MASKED, jnp.float32),
        jnp.zeros((per_chip * tokens, 1), jnp.float32),
        jnp.zeros((per_chip * tokens, width), jnp.float32),
    )
    _, total, weighted = lax.fori_loop(0, block + 1, advance, initial)
    out_ref[block] = (weighted / total).astype(jnp.bfloat16).reshape(per_chip, tokens, width)


def general_plan(length, devices, query_states, key_states, value_states, query_gain, key_gain):
    tokens, heads, width = query_states.shape
    kv_heads = key_states.shape[1]
    chips = devices // 2
    per_chip = heads // chips
    rep = (heads // kv_heads) // per_chip
    me = lax.axis_index("seq")
    core = lax.rem(me, 2)
    same_core = [list(range(start, devices, 2)) for start in range(2)]
    swap = [(device, device ^ 1) for device in range(devices)]
    table = lax.dynamic_slice_in_dim(jnp.asarray(rope_table(length, width)), me * tokens, tokens, 0)
    packed = pl.pallas_call(
        functools.partial(pack_kernel, rep),
        out_shape=jax.ShapeDtypeStruct((chips, per_chip + 2, tokens, width), jnp.bfloat16),
        in_specs=[VMEM] * 6,
        out_specs=VMEM,
        scratch_shapes=[
            pltpu.VMEM((tokens * heads, width), jnp.float32),
            pltpu.VMEM((tokens * kv_heads, width), jnp.float32),
            pltpu.VMEM((tokens * kv_heads, width), jnp.float32),
        ],
        compiler_params=pltpu.CompilerParams(vmem_limit_bytes=48 * 1024 * 1024),
        name="pack",
    )(query_states, key_states, value_states, table, query_gain[None], key_gain[None])
    arrived = lax.all_to_all(
        packed, "seq", split_axis=0, concat_axis=0, axis_index_groups=same_core, tiled=True
    )
    other = lax.ppermute(arrived[:, per_chip:], "seq", swap)
    attended = pl.pallas_call(
        looped_kernel,
        grid=(chips,),
        out_shape=jax.ShapeDtypeStruct((chips, per_chip, tokens, width), jnp.bfloat16),
        in_specs=[SMEM, VMEM, VMEM],
        out_specs=VMEM,
        compiler_params=pltpu.CompilerParams(vmem_limit_bytes=48 * 1024 * 1024),
        name="attention",
    )(core[None], arrived, other)
    returned = lax.all_to_all(
        attended, "seq", split_axis=0, concat_axis=0, axis_index_groups=same_core, tiled=True
    )
    return jnp.transpose(returned.reshape(heads, tokens, width), (1, 0, 2))


def rope_factors(table):
    half = table.shape[1] // 2
    swapped = pltpu.roll(table, half, 1)
    first = lax.broadcasted_iota(jnp.int32, table.shape, 1) < half
    return jnp.where(first, table, swapped), jnp.where(first, -swapped, table)


def normalize(rows):
    floats = rows.astype(jnp.float32)
    squares = floats * floats
    large = squares.astype(jnp.bfloat16)
    small = (squares - large.astype(jnp.float32)).astype(jnp.bfloat16)
    width = rows.shape[1]
    ones = jnp.ones((2 * width, width), jnp.bfloat16)
    added = jnp.dot(jnp.concatenate([large, small], axis=1), ones, preferred_element_type=jnp.float32)
    return floats * lax.rsqrt(added * (1.0 / width) + EPSILON)


def turn(normed, gain, cosine, sine):
    scaled = normed * gain
    return (scaled * cosine + pltpu.roll(scaled, scaled.shape[1] // 2, 1) * sine).astype(jnp.bfloat16)


def send_kernel(me_ref, q_hbm, k_hbm, v_hbm, table_hbm, query_gain_ref, key_gain_ref, *refs):
    pairs, (near_ref, q_ref, k_ref, v_ref, table_ref, qf_ref, kf_ref, vf_ref, sems) = refs[:-9], refs[-9:]
    tokens, heads, width = q_ref.shape
    kv_heads = k_ref.shape[1]
    group = heads // kv_heads
    me = me_ref[0]
    chip, core = lax.rem(me // 2, len(pairs)), lax.rem(me, 2)
    start = pl.multiple_of(me * tokens, 8)
    copies = [
        pltpu.make_async_copy(k_hbm, k_ref, sems.at[0]),
        pltpu.make_async_copy(table_hbm.at[pl.ds(start, tokens)], table_ref, sems.at[1]),
        pltpu.make_async_copy(v_hbm, v_ref, sems.at[2]),
        pltpu.make_async_copy(q_hbm, q_ref, sems.at[3]),
    ]
    for copy in copies:
        copy.start()
    copies[0].wait()
    kf_ref[...] = normalize(k_ref[...].reshape(tokens * kv_heads, width))
    copies[1].wait()
    cosine, sine = rope_factors(table_ref[...])
    copies[2].wait()
    vf_ref[...] = v_ref[...].astype(jnp.float32).reshape(tokens * kv_heads, width)
    for step, pair in enumerate(pairs):
        for side in range(2):
            head = (chip ^ step) * 2 + lax.rem(core + side, 2)
            keys = turn(kf_ref[pl.ds(head, tokens, stride=kv_heads), :], key_gain_ref[...], cosine, sine)
            values = vf_ref[pl.ds(head, tokens, stride=kv_heads), :].astype(jnp.bfloat16)
            pair[side, 0] = keys
            near_ref[head, group] = keys
            pair[side, 1] = values
            near_ref[head, group + 1] = values
    copies[3].wait()
    qf_ref[...] = normalize(q_ref[...].reshape(tokens * heads, width))
    for head in range(heads):
        normed = qf_ref[pl.ds(head, tokens, stride=heads), :]
        near_ref[head // group, head % group] = turn(normed, query_gain_ref[...], cosine, sine)


def near_kernel(x_ref, highest_ref, total_ref, weighted_ref):
    blocks, rows, tokens, width = x_ref.shape
    group = rows - 2
    scale = math.log2(math.e) / math.sqrt(width)
    keys = x_ref[:, group].reshape(blocks * tokens, width)
    values = x_ref[:, group + 1].reshape(blocks * tokens, width)
    for block in range(blocks):
        queries = x_ref[block, :group].reshape(group * tokens, width)
        reach = (block + 1) * tokens
        scores = lax.dot_general(queries, keys[:reach], CONTRACT, preferred_element_type=jnp.float32)
        row = lax.broadcasted_iota(jnp.int32, (group, tokens, reach), 1).reshape(group * tokens, reach)
        column = lax.broadcasted_iota(jnp.int32, (group * tokens, reach), 1)
        scores = jnp.where(column <= row + block * tokens, scores, MASKED)
        highest = jnp.max(scores, axis=-1, keepdims=True)
        probs = jnp.exp2((scores - highest) * scale)
        highest_ref[block] = highest
        total_ref[block] = jnp.sum(probs, axis=-1, keepdims=True)
        weighted_ref[block] = jnp.dot(
            probs.astype(jnp.bfloat16), values[:reach], preferred_element_type=jnp.float32
        )


def split_kernel(*refs):
    for step, ref in enumerate(refs[:-2]):
        for side in range(2):
            refs[side - 2][step] = ref[side]


def add_far(x_ref, state, pairs_ref, store):
    steps, _, tokens, width = pairs_ref.shape
    group = x_ref.shape[1] - 2
    scale = math.log2(math.e) / math.sqrt(width)
    highest_ref, total_ref, weighted_ref = state
    keys = pairs_ref[:, 0].reshape(steps * tokens, width)
    values = pairs_ref[:, 1].reshape(steps * tokens, width)
    for block in range(x_ref.shape[0]):
        queries = x_ref[block, :group].reshape(group * tokens, width)
        scores = lax.dot_general(queries, keys, CONTRACT, preferred_element_type=jnp.float32)
        before = highest_ref[block]
        highest = jnp.maximum(before, jnp.max(scores, axis=-1, keepdims=True))
        probs = jnp.exp2((scores - highest) * scale)
        factor = jnp.exp2((before - highest) * scale)
        total = total_ref[block] * factor + jnp.sum(probs, axis=-1, keepdims=True)
        summed = jnp.dot(probs.astype(jnp.bfloat16), values, preferred_element_type=jnp.float32)
        store(block, highest, total, weighted_ref[block] * factor + summed)


def far_kernel(half, me_ref, x_ref, pairs_ref, *refs):
    state, outs = refs[:3], refs[3:]

    def store(block, *values):
        for ref, value in zip(outs, values):
            ref[block] = value

    @pl.when(me_ref[0] >= half)
    def _():
        add_far(x_ref, state, pairs_ref, store)

    @pl.when(me_ref[0] < half)
    def _():
        for ref, before in zip(outs, state):
            ref[...] = before[...]


def last_kernel(half, me_ref, x_ref, pairs_ref, *refs):
    state, out_ref = refs[:3], refs[3]

    def store(block, highest, total, weighted):
        out_ref[block] = (weighted / total).astype(jnp.bfloat16).reshape(out_ref.shape[1:])

    @pl.when(me_ref[0] >= half)
    def _():
        add_far(x_ref, state, pairs_ref, store)

    @pl.when(me_ref[0] < half)
    def _():
        for block in range(out_ref.shape[0]):
            store(block, None, state[1][block], state[2][block])


def halves_plan(length, devices, query_states, key_states, value_states, query_gain, key_gain):
    tokens, heads, width = query_states.shape
    kv_heads = key_states.shape[1]
    group = heads // kv_heads
    half = devices // 2
    steps = half // 2
    bf16, f32 = jnp.bfloat16, jnp.float32
    me = lax.axis_index("seq")[None]

    def call(kernel, name, outs, *operands, scratch=(), specs=None, limit=VMEM_LIMIT):
        return pl.pallas_call(
            kernel,
            out_shape=outs,
            in_specs=specs or [SMEM] + [VMEM] * len(operands),
            out_specs=jax.tree.map(lambda _: VMEM, outs),
            scratch_shapes=scratch,
            compiler_params=pltpu.CompilerParams(vmem_limit_bytes=limit),
            name=name,
        )(*([me] if specs is None or SMEM in specs else []), *operands)

    def to_upper(step, array):
        links = [(device, half + ((device // 2) ^ step) * 2 + device % 2) for device in range(half)]
        return lax.ppermute(array, "seq", links)

    def to_core(array, lowest):
        return lax.ppermute(array, "seq", [(device, device ^ 1) for device in range(lowest, devices)])

    shape = jax.ShapeDtypeStruct
    *pairs, near = call(
        send_kernel,
        "send",
        [shape((2, 2, tokens, width), bf16)] * steps + [shape((half, group + 2, tokens, width), bf16)],
        query_states,
        key_states,
        value_states,
        jnp.asarray(rope_table(length, width)),
        query_gain[None],
        key_gain[None],
        specs=[SMEM, HBM, HBM, HBM, HBM, VMEM, VMEM],
        scratch=[
            pltpu.VMEM((tokens, heads, width), bf16),
            pltpu.VMEM((tokens, kv_heads, width), bf16),
            pltpu.VMEM((tokens, kv_heads, width), bf16),
            pltpu.VMEM((tokens, width), f32),
            pltpu.VMEM((tokens * heads, width), f32),
            pltpu.VMEM((tokens * kv_heads, width), f32),
            pltpu.VMEM((tokens * kv_heads, width), f32),
            pltpu.SemaphoreType.DMA((4,)),
        ],
        limit=PACK_VMEM,
    )
    groups = [list(range(half)), list(range(half, devices))]

    def inside(array):
        return lax.all_to_all(array, "seq", split_axis=0, concat_axis=0, axis_index_groups=groups, tiled=True)

    far = [to_upper(step, pair) for step, pair in enumerate(pairs)]
    arrived = inside(near)
    rows = group * tokens
    state = [shape((half, rows, 1), f32), shape((half, rows, 1), f32), shape((half, rows, width), f32)]
    carried = call(near_kernel, "near", state, arrived, specs=[VMEM])
    carried, far = lax.optimization_barrier((carried, far))
    mine, others = call(
        split_kernel, "split", [shape((steps, 2, tokens, width), bf16)] * 2, *far, specs=[VMEM] * steps
    )
    neighbours = to_core(others, half)
    carried = call(functools.partial(far_kernel, half), "far", state, arrived, mine, *carried)
    attended = call(
        functools.partial(last_kernel, half),
        "last",
        shape((half, group, tokens, width), bf16),
        arrived,
        neighbours,
        *carried,
    )
    return jnp.transpose(inside(attended).reshape(heads, tokens, width), (1, 0, 2))


def solution(mesh):
    devices = mesh.shape["seq"]
    groups = mesh.shape["groups"]
    placed = P(("groups", "seq"), None, None)

    def run(query_states, key_states, value_states, query_gain, key_gain):
        length = query_states.shape[0] // groups
        plan = halves_plan if devices == 2 * key_states.shape[1] else general_plan
        return jax.shard_map(
            functools.partial(plan, length, devices),
            mesh=mesh,
            in_specs=(placed, placed, placed, P(), P()),
            out_specs=placed,
            check_vma=False,
        )(query_states, key_states, value_states, query_gain, key_gain)

    return run
```

```python
import functools
import math

import jax
import jax.numpy as jnp
import numpy as np
from jax import lax
from jax.experimental import pallas as pl
from jax.experimental.pallas import tpu as pltpu
from jax.sharding import PartitionSpec as P

ROPE_BASE = 1000000.0
EPSILON = 1e-06
MASKED = -1e30
VMEM_LIMIT = 24 * 1024 * 1024
PACK_VMEM = 56 * 1024 * 1024
VMEM = pl.BlockSpec(memory_space=pltpu.VMEM)
SMEM = pl.BlockSpec(memory_space=pltpu.SMEM)
HBM = pl.BlockSpec(memory_space=pltpu.HBM)
NEAR_BLOCKS = 2
FAR_BLOCKS = 2
CONTRACT = (((1,), (1,)), ((), ()))


def rope_table(length, width):
    half = width // 2
    frequency = np.float64(ROPE_BASE) ** (-(np.arange(half, dtype=np.float64) * 2.0 / width))
    angles = np.arange(length, dtype=np.float32)[:, None] * frequency.astype(np.float32)[None, :]
    wide = angles.astype(np.float64)
    return np.concatenate([np.cos(wide), np.sin(wide)], axis=-1).astype(np.float32)


def pack_kernel(rep, q_ref, k_ref, v_ref, table_ref, qg_ref, kg_ref, out_ref, qf_ref, kf_ref, vf_ref):
    tokens, heads, width = q_ref.shape
    kv_heads = k_ref.shape[1]
    chips, rows = out_ref.shape[:2]
    per_chip = rows - 2
    qf_ref[...] = q_ref[...].astype(jnp.float32).reshape(tokens * heads, width)
    kf_ref[...] = k_ref[...].astype(jnp.float32).reshape(tokens * kv_heads, width)
    vf_ref[...] = v_ref[...].astype(jnp.float32).reshape(tokens * kv_heads, width)
    table = table_ref[...]
    swapped = pltpu.roll(table, width // 2, 1)
    first = lax.broadcasted_iota(jnp.int32, table.shape, 1) < width // 2
    cosine = jnp.where(first, table, swapped)
    sine = jnp.where(first, -swapped, table)

    def rotate(floats, gain):
        mean_square = jnp.mean(floats * floats, axis=-1, keepdims=True)
        normed = floats * lax.rsqrt(mean_square + EPSILON) * gain
        turned = pltpu.roll(normed, width // 2, 1)
        return (normed * cosine + turned * sine).astype(jnp.bfloat16)

    query_gain, key_gain = qg_ref[...], kg_ref[...]
    for head in range(heads):
        floats = qf_ref[pl.ds(head, tokens, stride=heads), :]
        out_ref[head // per_chip, head % per_chip] = rotate(floats, query_gain)
    for head in range(kv_heads):
        floats = kf_ref[pl.ds(head, tokens, stride=kv_heads), :]
        rotated = rotate(floats, key_gain)
        values = vf_ref[pl.ds(head, tokens, stride=kv_heads), :].astype(jnp.bfloat16)
        for copy in range(rep):
            out_ref[head * rep + copy, per_chip] = rotated
            out_ref[head * rep + copy, per_chip + 1] = values


def looped_kernel(core_ref, x_ref, other_ref, out_ref):
    _, rows, tokens, width = x_ref.shape
    per_chip = rows - 2
    core = core_ref[0]
    block = pl.program_id(0)
    scale = math.log2(math.e) / math.sqrt(width)
    queries = x_ref[block, :per_chip].reshape(per_chip * tokens, width)
    row = lax.broadcasted_iota(jnp.int32, (per_chip, tokens, tokens), 1).reshape(per_chip * tokens, tokens)
    column = lax.broadcasted_iota(jnp.int32, (per_chip * tokens, tokens), 1)

    def merge(carried, keys, values, allowed):
        highest, total, weighted = carried
        scores = lax.dot_general(queries, keys, CONTRACT, preferred_element_type=jnp.float32)
        scores = jnp.where(allowed, scores, MASKED)
        new = jnp.maximum(highest, jnp.max(scores, axis=-1, keepdims=True))
        probs = jnp.exp2((scores - new) * scale)
        factor = jnp.exp2((highest - new) * scale)
        total = total * factor + jnp.sum(probs, axis=-1, keepdims=True)
        summed = jnp.dot(probs.astype(jnp.bfloat16), values, preferred_element_type=jnp.float32)
        return new, total, weighted * factor + summed

    def advance(index, carried):
        behind = (block - index) * tokens
        carried = merge(carried, x_ref[index, per_chip], x_ref[index, per_chip + 1], column <= row + behind)
        return merge(carried, other_ref[index, 0], other_ref[index, 1], column < behind + core * tokens)

    initial = (
        jnp.full((per_chip * tokens, 1), MASKED, jnp.float32),
        jnp.zeros((per_chip * tokens, 1), jnp.float32),
        jnp.zeros((per_chip * tokens, width), jnp.float32),
    )
    _, total, weighted = lax.fori_loop(0, block + 1, advance, initial)
    out_ref[block] = (weighted / total).astype(jnp.bfloat16).reshape(per_chip, tokens, width)


def general_plan(length, devices, query_states, key_states, value_states, query_gain, key_gain):
    tokens, heads, width = query_states.shape
    kv_heads = key_states.shape[1]
    chips = devices // 2
    per_chip = heads // chips
    rep = (heads // kv_heads) // per_chip
    me = lax.axis_index("seq")
    core = lax.rem(me, 2)
    same_core = [list(range(start, devices, 2)) for start in range(2)]
    swap = [(device, device ^ 1) for device in range(devices)]
    table = lax.dynamic_slice_in_dim(jnp.asarray(rope_table(length, width)), me * tokens, tokens, 0)
    packed = pl.pallas_call(
        functools.partial(pack_kernel, rep),
        out_shape=jax.ShapeDtypeStruct((chips, per_chip + 2, tokens, width), jnp.bfloat16),
        in_specs=[VMEM] * 6,
        out_specs=VMEM,
        scratch_shapes=[
            pltpu.VMEM((tokens * heads, width), jnp.float32),
            pltpu.VMEM((tokens * kv_heads, width), jnp.float32),
            pltpu.VMEM((tokens * kv_heads, width), jnp.float32),
        ],
        compiler_params=pltpu.CompilerParams(vmem_limit_bytes=48 * 1024 * 1024),
        name="pack",
    )(query_states, key_states, value_states, table, query_gain[None], key_gain[None])
    arrived = lax.all_to_all(
        packed, "seq", split_axis=0, concat_axis=0, axis_index_groups=same_core, tiled=True
    )
    other = lax.ppermute(arrived[:, per_chip:], "seq", swap)
    attended = pl.pallas_call(
        looped_kernel,
        grid=(chips,),
        out_shape=jax.ShapeDtypeStruct((chips, per_chip, tokens, width), jnp.bfloat16),
        in_specs=[SMEM, VMEM, VMEM],
        out_specs=VMEM,
        compiler_params=pltpu.CompilerParams(vmem_limit_bytes=48 * 1024 * 1024),
        name="attention",
    )(core[None], arrived, other)
    returned = lax.all_to_all(
        attended, "seq", split_axis=0, concat_axis=0, axis_index_groups=same_core, tiled=True
    )
    return jnp.transpose(returned.reshape(heads, tokens, width), (1, 0, 2))


def rope_factors(table):
    half = table.shape[1] // 2
    swapped = pltpu.roll(table, half, 1)
    first = lax.broadcasted_iota(jnp.int32, table.shape, 1) < half
    return jnp.where(first, table, swapped), jnp.where(first, -swapped, table)


def normalize(rows):
    floats = rows.astype(jnp.float32)
    squares = floats * floats
    large = squares.astype(jnp.bfloat16)
    small = (squares - large.astype(jnp.float32)).astype(jnp.bfloat16)
    width = rows.shape[1]
    ones = jnp.ones((2 * width, width), jnp.bfloat16)
    added = jnp.dot(jnp.concatenate([large, small], axis=1), ones, preferred_element_type=jnp.float32)
    return floats * lax.rsqrt(added * (1.0 / width) + EPSILON)


def turn(normed, gain, cosine, sine):
    scaled = normed * gain
    return (scaled * cosine + pltpu.roll(scaled, scaled.shape[1] // 2, 1) * sine).astype(jnp.bfloat16)


def send_kernel(me_ref, q_hbm, k_hbm, v_hbm, table_hbm, query_gain_ref, key_gain_ref, *refs):
    pairs, (near_ref, q_ref, k_ref, v_ref, table_ref, qf_ref, kf_ref, vf_ref, sems) = refs[:-9], refs[-9:]
    tokens, heads, width = q_ref.shape
    kv_heads = k_ref.shape[1]
    group = heads // kv_heads
    me = me_ref[0]
    chip, core = lax.rem(me // 2, len(pairs)), lax.rem(me, 2)
    start = pl.multiple_of(me * tokens, 8)
    copies = [
        pltpu.make_async_copy(k_hbm, k_ref, sems.at[0]),
        pltpu.make_async_copy(table_hbm.at[pl.ds(start, tokens)], table_ref, sems.at[1]),
        pltpu.make_async_copy(v_hbm, v_ref, sems.at[2]),
        pltpu.make_async_copy(q_hbm, q_ref, sems.at[3]),
    ]
    for copy in copies:
        copy.start()
    copies[0].wait()
    kf_ref[...] = normalize(k_ref[...].reshape(tokens * kv_heads, width))
    copies[1].wait()
    cosine, sine = rope_factors(table_ref[...])
    copies[2].wait()
    vf_ref[...] = v_ref[...].astype(jnp.float32).reshape(tokens * kv_heads, width)
    for step, pair in enumerate(pairs):
        for side in range(2):
            head = (chip ^ step) * 2 + lax.rem(core + side, 2)
            keys = turn(kf_ref[pl.ds(head, tokens, stride=kv_heads), :], key_gain_ref[...], cosine, sine)
            values = vf_ref[pl.ds(head, tokens, stride=kv_heads), :].astype(jnp.bfloat16)
            pair[side, 0] = keys
            near_ref[head, group] = keys
            pair[side, 1] = values
            near_ref[head, group + 1] = values
    copies[3].wait()
    qf_ref[...] = normalize(q_ref[...].reshape(tokens * heads, width))
    for head in range(heads):
        normed = qf_ref[pl.ds(head, tokens, stride=heads), :]
        near_ref[head // group, head % group] = turn(normed, query_gain_ref[...], cosine, sine)


def weigh(keys, values, queries, allowed, state):
    scale = math.log2(math.e) / math.sqrt(keys.shape[1])
    scores = lax.dot_general(keys, queries, CONTRACT, preferred_element_type=jnp.float32)
    if allowed is not None:
        scores = jnp.where(allowed, scores, MASKED)
    highest = jnp.max(scores, axis=0, keepdims=True)
    if state is not None:
        highest = jnp.maximum(state[0], highest)
    probs = jnp.exp2((scores - highest) * scale)
    total = jnp.sum(probs, axis=0, keepdims=True)
    weighted = lax.dot_general(
        values, probs.astype(jnp.bfloat16), (((0,), (0,)), ((), ())), preferred_element_type=jnp.float32
    )
    if state is not None:
        factor = jnp.exp2((state[0] - highest) * scale)
        total, weighted = state[1] * factor + total, state[2] * factor + weighted
    return highest, total, weighted


def near_kernel(position_ref, x_ref, highest_ref, total_ref, weighted_ref):
    blocks, rows, tokens, width = x_ref.shape
    group = rows - 2
    keys = x_ref[:, group].reshape(blocks * tokens, width)
    values = x_ref[:, group + 1].reshape(blocks * tokens, width)
    lanes = NEAR_BLOCKS * group * tokens
    for first in range(0, blocks, NEAR_BLOCKS):
        queries = x_ref[first : first + NEAR_BLOCKS, :group].reshape(lanes, width)
        reach = (first + NEAR_BLOCKS) * tokens
        place = slice(first * group * tokens, first * group * tokens + lanes)
        index = lax.broadcasted_iota(jnp.int32, (reach, lanes), 0)
        allowed = index <= position_ref[:, place]
        results = weigh(keys[:reach], values[:reach], queries, allowed, None)
        for ref, value in zip((highest_ref, total_ref, weighted_ref), results):
            ref[:, place] = value


def split_kernel(*refs):
    for step, ref in enumerate(refs[:-2]):
        for side in range(2):
            refs[side - 2][step] = ref[side]


def add_far(x_ref, pairs_ref, state_refs, store):
    blocks, rows, tokens, width = x_ref.shape
    group = rows - 2
    keys, values = [pairs_ref[:, i].reshape(pairs_ref.shape[0] * tokens, width) for i in range(2)]
    lanes = FAR_BLOCKS * group * tokens
    for first in range(0, blocks, FAR_BLOCKS):
        queries = x_ref[first : first + FAR_BLOCKS, :group].reshape(lanes, width)
        place = slice(first * group * tokens, first * group * tokens + lanes)
        store(first, place, *weigh(keys, values, queries, None, [ref[:, place] for ref in state_refs]))


def far_kernel(half, me_ref, x_ref, pairs_ref, *refs):
    state, outs = refs[:3], refs[3:]

    def store(first, place, *values):
        for ref, value in zip(outs, values):
            ref[:, place] = value

    @pl.when(me_ref[0] >= half)
    def _():
        add_far(x_ref, pairs_ref, state, store)

    @pl.when(me_ref[0] < half)
    def _():
        for ref, before in zip(outs, state):
            ref[...] = before[...]


def last_kernel(half, me_ref, x_ref, pairs_ref, *refs):
    state, out_ref = refs[:3], refs[3]
    blocks, group, tokens, width = out_ref.shape

    def store(first, place, highest, total, weighted):
        result = jnp.transpose(weighted * (1.0 / total)).astype(jnp.bfloat16)
        out_ref[first : first + FAR_BLOCKS] = result.reshape(FAR_BLOCKS, group, tokens, width)

    @pl.when(me_ref[0] >= half)
    def _():
        add_far(x_ref, pairs_ref, state, store)

    @pl.when(me_ref[0] < half)
    def _():
        lanes = FAR_BLOCKS * group * tokens
        for first in range(0, blocks, FAR_BLOCKS):
            place = slice(first * group * tokens, first * group * tokens + lanes)
            store(first, place, None, state[1][:, place], state[2][:, place])


def halves_plan(length, devices, query_states, key_states, value_states, query_gain, key_gain):
    tokens, heads, width = query_states.shape
    kv_heads = key_states.shape[1]
    group = heads // kv_heads
    half = devices // 2
    steps = half // 2
    bf16, f32 = jnp.bfloat16, jnp.float32
    me = lax.axis_index("seq")[None]

    def call(kernel, name, outs, *operands, scratch=(), specs=None, limit=VMEM_LIMIT):
        return pl.pallas_call(
            kernel,
            out_shape=outs,
            in_specs=specs or [SMEM] + [VMEM] * len(operands),
            out_specs=jax.tree.map(lambda _: VMEM, outs),
            scratch_shapes=scratch,
            compiler_params=pltpu.CompilerParams(vmem_limit_bytes=limit),
            name=name,
        )(*([me] if specs is None or SMEM in specs else []), *operands)

    def to_upper(step, array):
        links = [(device, half + ((device // 2) ^ step) * 2 + device % 2) for device in range(half)]
        return lax.ppermute(array, "seq", links)

    def to_core(array, lowest):
        return lax.ppermute(array, "seq", [(device, device ^ 1) for device in range(lowest, devices)])

    shape = jax.ShapeDtypeStruct
    *pairs, near = call(
        send_kernel,
        "send",
        [shape((2, 2, tokens, width), bf16)] * steps + [shape((half, group + 2, tokens, width), bf16)],
        query_states,
        key_states,
        value_states,
        jnp.asarray(rope_table(length, width)),
        query_gain[None],
        key_gain[None],
        specs=[SMEM, HBM, HBM, HBM, HBM, VMEM, VMEM],
        scratch=[
            pltpu.VMEM((tokens, heads, width), bf16),
            pltpu.VMEM((tokens, kv_heads, width), bf16),
            pltpu.VMEM((tokens, kv_heads, width), bf16),
            pltpu.VMEM((tokens, width), f32),
            pltpu.VMEM((tokens * heads, width), f32),
            pltpu.VMEM((tokens * kv_heads, width), f32),
            pltpu.VMEM((tokens * kv_heads, width), f32),
            pltpu.SemaphoreType.DMA((4,)),
        ],
        limit=PACK_VMEM,
    )
    groups = [list(range(half)), list(range(half, devices))]

    def inside(array):
        return lax.all_to_all(array, "seq", split_axis=0, concat_axis=0, axis_index_groups=groups, tiled=True)

    far = [to_upper(step, pair) for step, pair in enumerate(pairs)]
    arrived = inside(near)
    lanes = half * group * tokens
    state = [shape((1, lanes), f32), shape((1, lanes), f32), shape((width, lanes), f32)]
    positions = np.broadcast_to(np.arange(half * tokens, dtype=np.int32).reshape(half, 1, tokens), (half, group, tokens))
    carried = call(near_kernel, "near", state, jnp.asarray(positions.reshape(1, lanes)), arrived, specs=[VMEM] * 2)

    carried, far = lax.optimization_barrier((carried, far))
    mine, others = call(
        split_kernel, "split", [shape((steps, 2, tokens, width), bf16)] * 2, *far, specs=[VMEM] * steps
    )
    neighbours = to_core(others, half)
    carried = call(functools.partial(far_kernel, half), "far", state, arrived, mine, *carried)
    attended = call(
        functools.partial(last_kernel, half),
        "last",
        shape((half, group, tokens, width), bf16),
        arrived,
        neighbours,
        *carried,
    )
    return jnp.transpose(inside(attended).reshape(heads, tokens, width), (1, 0, 2))


def solution(mesh):
    devices = mesh.shape["seq"]
    groups = mesh.shape["groups"]
    placed = P(("groups", "seq"), None, None)

    def run(query_states, key_states, value_states, query_gain, key_gain):
        length = query_states.shape[0] // groups
        plan = halves_plan if devices == 2 * key_states.shape[1] else general_plan
        return jax.shard_map(
            functools.partial(plan, length, devices),
            mesh=mesh,
            in_specs=(placed, placed, placed, P(), P()),
            out_specs=placed,
            check_vma=False,
        )(query_states, key_states, value_states, query_gain, key_gain)

    return run
```

```python
import functools
import math

import jax
import jax.numpy as jnp
import numpy as np
from jax import lax
from jax.experimental import pallas as pl
from jax.experimental.pallas import tpu as pltpu
from jax.sharding import PartitionSpec as P

ROPE_BASE = 1000000.0
EPSILON = 1e-06
MASKED = -1e30
VMEM_LIMIT = 24 * 1024 * 1024
PACK_VMEM = 56 * 1024 * 1024
VMEM = pl.BlockSpec(memory_space=pltpu.VMEM)
SMEM = pl.BlockSpec(memory_space=pltpu.SMEM)
HBM = pl.BlockSpec(memory_space=pltpu.HBM)
NEAR_BLOCKS = 2
FAR_BLOCKS = 2
CONTRACT = (((1,), (1,)), ((), ()))


def rope_table(length, width):
    half = width // 2
    frequency = np.float64(ROPE_BASE) ** (-(np.arange(half, dtype=np.float64) * 2.0 / width))
    angles = np.arange(length, dtype=np.float32)[:, None] * frequency.astype(np.float32)[None, :]
    wide = angles.astype(np.float64)
    return np.concatenate([np.cos(wide), np.sin(wide)], axis=-1).astype(np.float32)


def pack_kernel(rep, q_ref, k_ref, v_ref, table_ref, qg_ref, kg_ref, out_ref, qf_ref, kf_ref, vf_ref):
    tokens, heads, width = q_ref.shape
    kv_heads = k_ref.shape[1]
    chips, rows = out_ref.shape[:2]
    per_chip = rows - 2
    qf_ref[...] = q_ref[...].astype(jnp.float32).reshape(tokens * heads, width)
    kf_ref[...] = k_ref[...].astype(jnp.float32).reshape(tokens * kv_heads, width)
    vf_ref[...] = v_ref[...].astype(jnp.float32).reshape(tokens * kv_heads, width)
    table = table_ref[...]
    swapped = pltpu.roll(table, width // 2, 1)
    first = lax.broadcasted_iota(jnp.int32, table.shape, 1) < width // 2
    cosine = jnp.where(first, table, swapped)
    sine = jnp.where(first, -swapped, table)

    def rotate(floats, gain):
        mean_square = jnp.mean(floats * floats, axis=-1, keepdims=True)
        normed = floats * lax.rsqrt(mean_square + EPSILON) * gain
        turned = pltpu.roll(normed, width // 2, 1)
        return (normed * cosine + turned * sine).astype(jnp.bfloat16)

    query_gain, key_gain = qg_ref[...], kg_ref[...]
    for head in range(heads):
        floats = qf_ref[pl.ds(head, tokens, stride=heads), :]
        out_ref[head // per_chip, head % per_chip] = rotate(floats, query_gain)
    for head in range(kv_heads):
        floats = kf_ref[pl.ds(head, tokens, stride=kv_heads), :]
        rotated = rotate(floats, key_gain)
        values = vf_ref[pl.ds(head, tokens, stride=kv_heads), :].astype(jnp.bfloat16)
        for copy in range(rep):
            out_ref[head * rep + copy, per_chip] = rotated
            out_ref[head * rep + copy, per_chip + 1] = values


def looped_kernel(core_ref, x_ref, other_ref, out_ref):
    _, rows, tokens, width = x_ref.shape
    per_chip = rows - 2
    core = core_ref[0]
    block = pl.program_id(0)
    scale = math.log2(math.e) / math.sqrt(width)
    queries = x_ref[block, :per_chip].reshape(per_chip * tokens, width)
    row = lax.broadcasted_iota(jnp.int32, (per_chip, tokens, tokens), 1).reshape(per_chip * tokens, tokens)
    column = lax.broadcasted_iota(jnp.int32, (per_chip * tokens, tokens), 1)

    def merge(carried, keys, values, allowed):
        highest, total, weighted = carried
        scores = lax.dot_general(queries, keys, CONTRACT, preferred_element_type=jnp.float32)
        scores = jnp.where(allowed, scores, MASKED)
        new = jnp.maximum(highest, jnp.max(scores, axis=-1, keepdims=True))
        probs = jnp.exp2((scores - new) * scale)
        factor = jnp.exp2((highest - new) * scale)
        total = total * factor + jnp.sum(probs, axis=-1, keepdims=True)
        summed = jnp.dot(probs.astype(jnp.bfloat16), values, preferred_element_type=jnp.float32)
        return new, total, weighted * factor + summed

    def advance(index, carried):
        behind = (block - index) * tokens
        carried = merge(carried, x_ref[index, per_chip], x_ref[index, per_chip + 1], column <= row + behind)
        return merge(carried, other_ref[index, 0], other_ref[index, 1], column < behind + core * tokens)

    initial = (
        jnp.full((per_chip * tokens, 1), MASKED, jnp.float32),
        jnp.zeros((per_chip * tokens, 1), jnp.float32),
        jnp.zeros((per_chip * tokens, width), jnp.float32),
    )
    _, total, weighted = lax.fori_loop(0, block + 1, advance, initial)
    out_ref[block] = (weighted / total).astype(jnp.bfloat16).reshape(per_chip, tokens, width)


def general_plan(length, devices, query_states, key_states, value_states, query_gain, key_gain):
    tokens, heads, width = query_states.shape
    kv_heads = key_states.shape[1]
    chips = devices // 2
    per_chip = heads // chips
    rep = (heads // kv_heads) // per_chip
    me = lax.axis_index("seq")
    core = lax.rem(me, 2)
    same_core = [list(range(start, devices, 2)) for start in range(2)]
    swap = [(device, device ^ 1) for device in range(devices)]
    table = lax.dynamic_slice_in_dim(jnp.asarray(rope_table(length, width)), me * tokens, tokens, 0)
    packed = pl.pallas_call(
        functools.partial(pack_kernel, rep),
        out_shape=jax.ShapeDtypeStruct((chips, per_chip + 2, tokens, width), jnp.bfloat16),
        in_specs=[VMEM] * 6,
        out_specs=VMEM,
        scratch_shapes=[
            pltpu.VMEM((tokens * heads, width), jnp.float32),
            pltpu.VMEM((tokens * kv_heads, width), jnp.float32),
            pltpu.VMEM((tokens * kv_heads, width), jnp.float32),
        ],
        compiler_params=pltpu.CompilerParams(vmem_limit_bytes=48 * 1024 * 1024),
        name="pack",
    )(query_states, key_states, value_states, table, query_gain[None], key_gain[None])
    arrived = lax.all_to_all(
        packed, "seq", split_axis=0, concat_axis=0, axis_index_groups=same_core, tiled=True
    )
    other = lax.ppermute(arrived[:, per_chip:], "seq", swap)
    attended = pl.pallas_call(
        looped_kernel,
        grid=(chips,),
        out_shape=jax.ShapeDtypeStruct((chips, per_chip, tokens, width), jnp.bfloat16),
        in_specs=[SMEM, VMEM, VMEM],
        out_specs=VMEM,
        compiler_params=pltpu.CompilerParams(vmem_limit_bytes=48 * 1024 * 1024),
        name="attention",
    )(core[None], arrived, other)
    returned = lax.all_to_all(
        attended, "seq", split_axis=0, concat_axis=0, axis_index_groups=same_core, tiled=True
    )
    return jnp.transpose(returned.reshape(heads, tokens, width), (1, 0, 2))


def rope_factors(table):
    half = table.shape[1] // 2
    swapped = pltpu.roll(table, half, 1)
    first = lax.broadcasted_iota(jnp.int32, table.shape, 1) < half
    return jnp.where(first, table, swapped), jnp.where(first, -swapped, table)


def normalize(rows):
    floats = rows.astype(jnp.float32)
    squares = floats * floats
    large = squares.astype(jnp.bfloat16)
    small = (squares - large.astype(jnp.float32)).astype(jnp.bfloat16)
    width = rows.shape[1]
    ones = jnp.ones((2 * width, width), jnp.bfloat16)
    added = jnp.dot(jnp.concatenate([large, small], axis=1), ones, preferred_element_type=jnp.float32)
    return floats * lax.rsqrt(added * (1.0 / width) + EPSILON)


def turn(normed, gain, cosine, sine):
    scaled = normed * gain
    return (scaled * cosine + pltpu.roll(scaled, scaled.shape[1] // 2, 1) * sine).astype(jnp.bfloat16)


def send_kernel(me_ref, q_hbm, k_hbm, v_hbm, table_hbm, query_gain_ref, key_gain_ref, *refs):
    pairs, (near_ref, q_ref, k_ref, v_ref, table_ref, qf_ref, kf_ref, vf_ref, sems) = refs[:-9], refs[-9:]
    tokens, heads, width = q_ref.shape
    kv_heads = k_ref.shape[1]
    group = heads // kv_heads
    me = me_ref[0]
    chip, core = lax.rem(me // 2, len(pairs)), lax.rem(me, 2)
    start = pl.multiple_of(me * tokens, 8)
    copies = [
        pltpu.make_async_copy(k_hbm, k_ref, sems.at[0]),
        pltpu.make_async_copy(table_hbm.at[pl.ds(start, tokens)], table_ref, sems.at[1]),
        pltpu.make_async_copy(v_hbm, v_ref, sems.at[2]),
        pltpu.make_async_copy(q_hbm, q_ref, sems.at[3]),
    ]
    for copy in copies:
        copy.start()
    copies[0].wait()
    kf_ref[...] = normalize(k_ref[...].reshape(tokens * kv_heads, width))
    copies[1].wait()
    cosine, sine = rope_factors(table_ref[...])
    copies[2].wait()
    vf_ref[...] = v_ref[...].astype(jnp.float32).reshape(tokens * kv_heads, width)
    for step, pair in enumerate(pairs):
        for side in range(2):
            head = (chip ^ step) * 2 + lax.rem(core + side, 2)
            keys = turn(kf_ref[pl.ds(head, tokens, stride=kv_heads), :], key_gain_ref[...], cosine, sine)
            values = vf_ref[pl.ds(head, tokens, stride=kv_heads), :].astype(jnp.bfloat16)
            pair[side, 0] = keys
            near_ref[head, group] = keys
            pair[side, 1] = values
            near_ref[head, group + 1] = values
    copies[3].wait()
    qf_ref[...] = normalize(q_ref[...].reshape(tokens * heads, width))
    for head in range(heads):
        normed = qf_ref[pl.ds(head, tokens, stride=heads), :]
        near_ref[head // group, head % group] = turn(normed, query_gain_ref[...], cosine, sine)


def weigh(keys, values, queries, allowed, state):
    scale = math.log2(math.e) / math.sqrt(keys.shape[1])
    scores = lax.dot_general(keys, queries, CONTRACT, preferred_element_type=jnp.float32)
    if allowed is not None:
        scores = jnp.where(allowed, scores, MASKED)
    highest = jnp.max(scores, axis=0, keepdims=True)
    if state is not None:
        highest = jnp.maximum(state[0], highest)
    probs = jnp.exp2((scores - highest) * scale)
    total = jnp.sum(probs, axis=0, keepdims=True)
    weighted = lax.dot_general(
        values, probs.astype(jnp.bfloat16), (((0,), (0,)), ((), ())), preferred_element_type=jnp.float32
    )
    if state is not None:
        factor = jnp.exp2((state[0] - highest) * scale)
        total, weighted = state[1] * factor + total, state[2] * factor + weighted
    return highest, total, weighted


def near_kernel(position_ref, x_ref, highest_ref, total_ref, weighted_ref):
    blocks, rows, tokens, width = x_ref.shape
    group = rows - 2
    keys = x_ref[:, group].reshape(blocks * tokens, width)
    values = x_ref[:, group + 1].reshape(blocks * tokens, width)
    lanes = NEAR_BLOCKS * group * tokens
    for first in range(0, blocks, NEAR_BLOCKS):
        queries = x_ref[first : first + NEAR_BLOCKS, :group].reshape(lanes, width)
        reach = (first + NEAR_BLOCKS) * tokens
        place = slice(first * group * tokens, first * group * tokens + lanes)
        index = lax.broadcasted_iota(jnp.int32, (reach, lanes), 0)
        allowed = index <= position_ref[:, place]
        results = weigh(keys[:reach], values[:reach], queries, allowed, None)
        for ref, value in zip((highest_ref, total_ref, weighted_ref), results):
            ref[:, place] = value


def split_kernel(*refs):
    for step, ref in enumerate(refs[:-2]):
        for side in range(2):
            refs[side - 2][step] = ref[side]


def add_far(x_ref, pair_refs, state_refs, store):
    blocks, rows, tokens, width = x_ref.shape
    group = rows - 2
    keys, values = [
        jnp.concatenate([ref[:, i].reshape(ref.shape[0] * tokens, width) for ref in pair_refs], axis=0)
        for i in range(2)
    ]
    lanes = FAR_BLOCKS * group * tokens
    for first in range(0, blocks, FAR_BLOCKS):
        queries = x_ref[first : first + FAR_BLOCKS, :group].reshape(lanes, width)
        place = slice(first * group * tokens, first * group * tokens + lanes)
        store(first, place, *weigh(keys, values, queries, None, [ref[:, place] for ref in state_refs]))


def last_kernel(half, me_ref, x_ref, mine_ref, neighbours_ref, *refs):
    state, out_ref = refs[:3], refs[3]
    blocks, group, tokens, width = out_ref.shape

    def store(first, place, highest, total, weighted):
        result = jnp.transpose(weighted * (1.0 / total)).astype(jnp.bfloat16)
        out_ref[first : first + FAR_BLOCKS] = result.reshape(FAR_BLOCKS, group, tokens, width)

    @pl.when(me_ref[0] >= half)
    def _():
        add_far(x_ref, [mine_ref, neighbours_ref], state, store)

    @pl.when(me_ref[0] < half)
    def _():
        lanes = FAR_BLOCKS * group * tokens
        for first in range(0, blocks, FAR_BLOCKS):
            place = slice(first * group * tokens, first * group * tokens + lanes)
            store(first, place, None, state[1][:, place], state[2][:, place])


def halves_plan(length, devices, query_states, key_states, value_states, query_gain, key_gain):
    tokens, heads, width = query_states.shape
    kv_heads = key_states.shape[1]
    group = heads // kv_heads
    half = devices // 2
    steps = half // 2
    bf16, f32 = jnp.bfloat16, jnp.float32
    me = lax.axis_index("seq")[None]

    def call(kernel, name, outs, *operands, scratch=(), specs=None, limit=VMEM_LIMIT):
        return pl.pallas_call(
            kernel,
            out_shape=outs,
            in_specs=specs or [SMEM] + [VMEM] * len(operands),
            out_specs=jax.tree.map(lambda _: VMEM, outs),
            scratch_shapes=scratch,
            compiler_params=pltpu.CompilerParams(vmem_limit_bytes=limit),
            name=name,
        )(*([me] if specs is None or SMEM in specs else []), *operands)

    def to_upper(step, array):
        links = [(device, half + ((device // 2) ^ step) * 2 + device % 2) for device in range(half)]
        return lax.ppermute(array, "seq", links)

    def to_core(array, lowest):
        return lax.ppermute(array, "seq", [(device, device ^ 1) for device in range(lowest, devices)])

    shape = jax.ShapeDtypeStruct
    *pairs, near = call(
        send_kernel,
        "send",
        [shape((2, 2, tokens, width), bf16)] * steps + [shape((half, group + 2, tokens, width), bf16)],
        query_states,
        key_states,
        value_states,
        jnp.asarray(rope_table(length, width)),
        query_gain[None],
        key_gain[None],
        specs=[SMEM, HBM, HBM, HBM, HBM, VMEM, VMEM],
        scratch=[
            pltpu.VMEM((tokens, heads, width), bf16),
            pltpu.VMEM((tokens, kv_heads, width), bf16),
            pltpu.VMEM((tokens, kv_heads, width), bf16),
            pltpu.VMEM((tokens, width), f32),
            pltpu.VMEM((tokens * heads, width), f32),
            pltpu.VMEM((tokens * kv_heads, width), f32),
            pltpu.VMEM((tokens * kv_heads, width), f32),
            pltpu.SemaphoreType.DMA((4,)),
        ],
        limit=PACK_VMEM,
    )
    groups = [list(range(half)), list(range(half, devices))]

    def inside(array):
        return lax.all_to_all(array, "seq", split_axis=0, concat_axis=0, axis_index_groups=groups, tiled=True)

    far = [to_upper(step, pair) for step, pair in enumerate(pairs)]
    arrived = lax.cond(me[0] >= 0, inside, jnp.zeros_like, near)
    arrived, far = lax.optimization_barrier((arrived, far))
    mine, others = call(
        split_kernel, "split", [shape((steps, 2, tokens, width), bf16)] * 2, *far, specs=[VMEM] * steps
    )
    neighbours = to_core(others, half)
    lanes = half * group * tokens
    state = [shape((1, lanes), f32), shape((1, lanes), f32), shape((width, lanes), f32)]
    positions = np.broadcast_to(np.arange(half * tokens, dtype=np.int32).reshape(half, 1, tokens), (half, group, tokens))
    carried = call(near_kernel, "near", state, jnp.asarray(positions.reshape(1, lanes)), arrived, specs=[VMEM] * 2)

    attended = call(
        functools.partial(last_kernel, half),
        "last",
        shape((half, group, tokens, width), bf16),
        arrived,
        mine,
        neighbours,
        *carried,
    )
    return jnp.transpose(inside(attended).reshape(heads, tokens, width), (1, 0, 2))


def solution(mesh):
    devices = mesh.shape["seq"]
    groups = mesh.shape["groups"]
    placed = P(("groups", "seq"), None, None)

    def run(query_states, key_states, value_states, query_gain, key_gain):
        length = query_states.shape[0] // groups
        plan = halves_plan if devices == 2 * key_states.shape[1] else general_plan
        return jax.shard_map(
            functools.partial(plan, length, devices),
            mesh=mesh,
            in_specs=(placed, placed, placed, P(), P()),
            out_specs=placed,
            check_vma=False,
        )(query_states, key_states, value_states, query_gain, key_gain)

    return run
```

```python
import functools
import math

import jax
import jax.numpy as jnp
import numpy as np
from jax import lax
from jax.experimental import pallas as pl
from jax.experimental.pallas import tpu as pltpu
from jax.sharding import PartitionSpec as P

ROPE_BASE = 1000000.0
EPSILON = 1e-06
MASKED = -1e30
VMEM_LIMIT = 24 * 1024 * 1024
PACK_VMEM = 56 * 1024 * 1024
VMEM = pl.BlockSpec(memory_space=pltpu.VMEM)
SMEM = pl.BlockSpec(memory_space=pltpu.SMEM)
HBM = pl.BlockSpec(memory_space=pltpu.HBM)
TILE_BLOCKS = 2
CONTRACT = (((1,), (1,)), ((), ()))


def rope_table(length, width):
    half = width // 2
    frequency = np.float64(ROPE_BASE) ** (-(np.arange(half, dtype=np.float64) * 2.0 / width))
    angles = np.arange(length, dtype=np.float32)[:, None] * frequency.astype(np.float32)[None, :]
    wide = angles.astype(np.float64)
    return np.concatenate([np.cos(wide), np.sin(wide)], axis=-1).astype(np.float32)


def pack_kernel(rep, q_ref, k_ref, v_ref, table_ref, qg_ref, kg_ref, out_ref, qf_ref, kf_ref, vf_ref):
    tokens, heads, width = q_ref.shape
    kv_heads = k_ref.shape[1]
    chips, rows = out_ref.shape[:2]
    per_chip = rows - 2
    qf_ref[...] = q_ref[...].astype(jnp.float32).reshape(tokens * heads, width)
    kf_ref[...] = k_ref[...].astype(jnp.float32).reshape(tokens * kv_heads, width)
    vf_ref[...] = v_ref[...].astype(jnp.float32).reshape(tokens * kv_heads, width)
    table = table_ref[...]
    swapped = pltpu.roll(table, width // 2, 1)
    first = lax.broadcasted_iota(jnp.int32, table.shape, 1) < width // 2
    cosine = jnp.where(first, table, swapped)
    sine = jnp.where(first, -swapped, table)

    def rotate(floats, gain):
        mean_square = jnp.mean(floats * floats, axis=-1, keepdims=True)
        normed = floats * lax.rsqrt(mean_square + EPSILON) * gain
        turned = pltpu.roll(normed, width // 2, 1)
        return (normed * cosine + turned * sine).astype(jnp.bfloat16)

    query_gain, key_gain = qg_ref[...], kg_ref[...]
    for head in range(heads):
        floats = qf_ref[pl.ds(head, tokens, stride=heads), :]
        out_ref[head // per_chip, head % per_chip] = rotate(floats, query_gain)
    for head in range(kv_heads):
        floats = kf_ref[pl.ds(head, tokens, stride=kv_heads), :]
        rotated = rotate(floats, key_gain)
        values = vf_ref[pl.ds(head, tokens, stride=kv_heads), :].astype(jnp.bfloat16)
        for copy in range(rep):
            out_ref[head * rep + copy, per_chip] = rotated
            out_ref[head * rep + copy, per_chip + 1] = values


def looped_kernel(core_ref, x_ref, other_ref, out_ref):
    _, rows, tokens, width = x_ref.shape
    per_chip = rows - 2
    core = core_ref[0]
    block = pl.program_id(0)
    scale = math.log2(math.e) / math.sqrt(width)
    queries = x_ref[block, :per_chip].reshape(per_chip * tokens, width)
    row = lax.broadcasted_iota(jnp.int32, (per_chip, tokens, tokens), 1).reshape(per_chip * tokens, tokens)
    column = lax.broadcasted_iota(jnp.int32, (per_chip * tokens, tokens), 1)

    def merge(carried, keys, values, allowed):
        highest, total, weighted = carried
        scores = lax.dot_general(queries, keys, CONTRACT, preferred_element_type=jnp.float32)
        scores = jnp.where(allowed, scores, MASKED)
        new = jnp.maximum(highest, jnp.max(scores, axis=-1, keepdims=True))
        probs = jnp.exp2((scores - new) * scale)
        factor = jnp.exp2((highest - new) * scale)
        total = total * factor + jnp.sum(probs, axis=-1, keepdims=True)
        summed = jnp.dot(probs.astype(jnp.bfloat16), values, preferred_element_type=jnp.float32)
        return new, total, weighted * factor + summed

    def advance(index, carried):
        behind = (block - index) * tokens
        carried = merge(carried, x_ref[index, per_chip], x_ref[index, per_chip + 1], column <= row + behind)
        return merge(carried, other_ref[index, 0], other_ref[index, 1], column < behind + core * tokens)

    initial = (
        jnp.full((per_chip * tokens, 1), MASKED, jnp.float32),
        jnp.zeros((per_chip * tokens, 1), jnp.float32),
        jnp.zeros((per_chip * tokens, width), jnp.float32),
    )
    _, total, weighted = lax.fori_loop(0, block + 1, advance, initial)
    out_ref[block] = (weighted / total).astype(jnp.bfloat16).reshape(per_chip, tokens, width)


def general_plan(length, devices, query_states, key_states, value_states, query_gain, key_gain):
    tokens, heads, width = query_states.shape
    kv_heads = key_states.shape[1]
    chips = devices // 2
    per_chip = heads // chips
    rep = (heads // kv_heads) // per_chip
    me = lax.axis_index("seq")
    core = lax.rem(me, 2)
    same_core = [list(range(start, devices, 2)) for start in range(2)]
    swap = [(device, device ^ 1) for device in range(devices)]
    table = lax.dynamic_slice_in_dim(jnp.asarray(rope_table(length, width)), me * tokens, tokens, 0)
    packed = pl.pallas_call(
        functools.partial(pack_kernel, rep),
        out_shape=jax.ShapeDtypeStruct((chips, per_chip + 2, tokens, width), jnp.bfloat16),
        in_specs=[VMEM] * 6,
        out_specs=VMEM,
        scratch_shapes=[
            pltpu.VMEM((tokens * heads, width), jnp.float32),
            pltpu.VMEM((tokens * kv_heads, width), jnp.float32),
            pltpu.VMEM((tokens * kv_heads, width), jnp.float32),
        ],
        compiler_params=pltpu.CompilerParams(vmem_limit_bytes=48 * 1024 * 1024),
        name="pack",
    )(query_states, key_states, value_states, table, query_gain[None], key_gain[None])
    arrived = lax.all_to_all(
        packed, "seq", split_axis=0, concat_axis=0, axis_index_groups=same_core, tiled=True
    )
    other = lax.ppermute(arrived[:, per_chip:], "seq", swap)
    attended = pl.pallas_call(
        looped_kernel,
        grid=(chips,),
        out_shape=jax.ShapeDtypeStruct((chips, per_chip, tokens, width), jnp.bfloat16),
        in_specs=[SMEM, VMEM, VMEM],
        out_specs=VMEM,
        compiler_params=pltpu.CompilerParams(vmem_limit_bytes=48 * 1024 * 1024),
        name="attention",
    )(core[None], arrived, other)
    returned = lax.all_to_all(
        attended, "seq", split_axis=0, concat_axis=0, axis_index_groups=same_core, tiled=True
    )
    return jnp.transpose(returned.reshape(heads, tokens, width), (1, 0, 2))


def rope_factors(table):
    half = table.shape[1] // 2
    swapped = pltpu.roll(table, half, 1)
    first = lax.broadcasted_iota(jnp.int32, table.shape, 1) < half
    return jnp.where(first, table, swapped), jnp.where(first, -swapped, table)


def normalize(rows):
    floats = rows.astype(jnp.float32)
    squares = floats * floats
    large = squares.astype(jnp.bfloat16)
    small = (squares - large.astype(jnp.float32)).astype(jnp.bfloat16)
    width = rows.shape[1]
    ones = jnp.ones((2 * width, width), jnp.bfloat16)
    added = jnp.dot(jnp.concatenate([large, small], axis=1), ones, preferred_element_type=jnp.float32)
    return floats * lax.rsqrt(added * (1.0 / width) + EPSILON)


def turn(normed, gain, cosine, sine):
    scaled = normed * gain
    return (scaled * cosine + pltpu.roll(scaled, scaled.shape[1] // 2, 1) * sine).astype(jnp.bfloat16)


def send_kernel(me_ref, q_hbm, k_hbm, v_hbm, table_hbm, query_gain_ref, key_gain_ref, *refs):
    (keep_ref, give_ref), fulls = refs[:2], refs[2:-8]
    q_ref, k_ref, v_ref, table_ref, qf_ref, kf_ref, vf_ref, sems = refs[-8:]
    steps, slots = len(fulls), keep_ref.shape[0]
    tokens, heads, width = q_ref.shape
    kv_heads, per_chip = k_ref.shape[1], keep_ref.shape[1]
    first, per_full = 2 * per_chip, heads // steps
    me = me_ref[0]
    chip, core = lax.rem(me // 2, steps), lax.rem(me, 2)
    start = pl.multiple_of(me * tokens, 8)
    copies = [
        pltpu.make_async_copy(k_hbm, k_ref, sems.at[0]),
        pltpu.make_async_copy(table_hbm.at[pl.ds(start, tokens)], table_ref, sems.at[1]),
        pltpu.make_async_copy(v_hbm, v_ref, sems.at[2]),
        pltpu.make_async_copy(q_hbm, q_ref, sems.at[3]),
    ]
    for copy in copies:
        copy.start()
    copies[0].wait()
    kf_ref[...] = normalize(k_ref[...].reshape(tokens * kv_heads, width))
    copies[1].wait()
    cosine, sine = rope_factors(table_ref[...])
    copies[2].wait()
    vf_ref[...] = v_ref[...].astype(jnp.float32).reshape(tokens * kv_heads, width)
    for slot in range(steps):
        step = lax.rem(core * slots + slot, steps)
        ref = keep_ref if slot < slots else give_ref
        for row in range(per_chip):
            head = (chip ^ step) * per_chip + row
            ref[slot % slots, row, 0] = turn(
                kf_ref[pl.ds(head, tokens, stride=kv_heads), :], key_gain_ref[...], cosine, sine
            )
            ref[slot % slots, row, 1] = vf_ref[pl.ds(head, tokens, stride=kv_heads), :].astype(jnp.bfloat16)
    for slot in range(slots):
        for row in range(first):
            part = (slot, row // 2, row % 2)

            @pl.when(core == 0)
            def _():
                fulls[slot][row], fulls[slots + slot][row] = keep_ref[part], give_ref[part]

            @pl.when(core == 1)
            def _():
                fulls[slot][row], fulls[slots + slot][row] = give_ref[part], keep_ref[part]

    copies[3].wait()
    qf_ref[...] = normalize(q_ref[...].reshape(tokens * heads, width))
    for step in range(steps):
        for row in range(per_full):
            normed = qf_ref[pl.ds((chip ^ step) * per_full + row, tokens, stride=heads), :]
            fulls[step][first + row] = turn(normed, query_gain_ref[...], cosine, sine)


def weigh(keys, values, queries, allowed, state):
    scale = math.log2(math.e) / math.sqrt(keys.shape[1])
    scores = lax.dot_general(keys, queries, CONTRACT, preferred_element_type=jnp.float32)
    if allowed is not None:
        scores = jnp.where(allowed, scores, MASKED)
    highest = jnp.max(scores, axis=0, keepdims=True)
    if state is not None:
        highest = jnp.maximum(state[0], highest)
    probs = jnp.exp2((scores - highest) * scale)
    total = jnp.sum(probs, axis=0, keepdims=True)
    weighted = lax.dot_general(
        values, probs.astype(jnp.bfloat16), (((0,), (0,)), ((), ())), preferred_element_type=jnp.float32
    )
    if state is not None:
        factor = jnp.exp2((state[0] - highest) * scale)
        total, weighted = state[1] * factor + total, state[2] * factor + weighted
    return highest, total, weighted


def join_kernel(keep_ref, got_ref, *outs):
    for slot, ref in enumerate(outs):
        ref[0], ref[1] = keep_ref[slot], got_ref[slot]


def gather_kernel(me_ref, *refs):
    pair_ref, query_ref = refs[-2:]
    steps, per_chip = query_ref.shape[:2]
    near, far = refs[:steps], refs[steps:-2]
    chip = lax.rem(me_ref[0] // 2, steps)
    for step in range(steps):
        pair_ref[chip ^ step] = near[step][: 2 * per_chip].reshape(pair_ref.shape[1:])
        query_ref[chip ^ step] = near[step][2 * per_chip :].reshape(query_ref.shape[1:])
    for slot, ref in enumerate(far):
        pair_ref[steps + 2 * slot : steps + 2 * slot + 2] = ref[...]


def add_core(upper, bound, query_ref, pair_ref, state_refs, store):
    steps, kv_heads, group, tokens, width = query_ref.shape
    lanes = TILE_BLOCKS * group * tokens

    def tiles(with_far):
        for head in range(kv_heads):
            for first in range(0, steps, TILE_BLOCKS):
                count = first + TILE_BLOCKS
                place = slice(first * group * tokens, first * group * tokens + lanes)
                keys, values = [
                    jnp.concatenate(
                        [pair_ref[:count, head, i].reshape(count * tokens, width)]
                        + ([pair_ref[steps:, head, i].reshape(steps * tokens, width)] if with_far else []),
                        axis=0,
                    )
                    for i in range(2)
                ]
                queries = query_ref[first:count, head].reshape(lanes, width)
                index = lax.broadcasted_iota(jnp.int32, (keys.shape[0], lanes), 0)
                allowed = index < bound[:, place]
                if with_far:
                    allowed = jnp.logical_or(allowed, index >= count * tokens)
                state = [ref[head, :, place] for ref in state_refs] if state_refs else None
                store(head, first, place, *weigh(keys, values, queries, allowed, state))

    pl.when(upper)(functools.partial(tiles, True))
    pl.when(jnp.logical_not(upper))(functools.partial(tiles, False))


def first_kernel(half, me_ref, bounds_ref, query_ref, pair_ref, *outs):
    def store(head, first, place, *values):
        for ref, value in zip(outs, values):
            ref[head, :, place] = value

    add_core(me_ref[0] >= half, bounds_ref[0:1], query_ref, pair_ref, None, store)


def second_kernel(half, me_ref, bounds_ref, query_ref, pair_ref, *refs):
    steps, kv_heads, group, tokens, width = query_ref.shape
    state, outs, out_ref = refs[:3], refs[3:-1], refs[-1]
    me = me_ref[0]

    def store(head, first, place, highest, total, weighted):
        result = jnp.transpose(weighted * (1.0 / total)).astype(jnp.bfloat16)
        rows = slice(head * group, (head + 1) * group)
        out_ref[first : first + TILE_BLOCKS, rows] = result.reshape(TILE_BLOCKS, group, tokens, width)

    bound = bounds_ref[1:2] + lax.rem(me, 2) * tokens
    add_core(me >= half, bound, query_ref, pair_ref, state, store)
    chip = lax.rem(me // 2, steps)
    for step in range(steps):
        outs[step][...] = out_ref[chip ^ step]


def unpack_kernel(me_ref, *refs):
    parts, (out_ref, floats_ref) = refs[:-2], refs[-2:]
    tokens, heads, width = out_ref.shape
    steps = len(parts)
    per_chip = heads // steps
    chip = lax.rem(me_ref[0] // 2, steps)
    for step in range(steps):
        for row in range(per_chip):
            head = (chip ^ step) * per_chip + row
            floats_ref[pl.ds(head, tokens, stride=heads), :] = parts[step][row].astype(jnp.float32)
    out_ref[...] = floats_ref[...].reshape(tokens, heads, width).astype(jnp.bfloat16)


def halves_plan(length, devices, query_states, key_states, value_states, query_gain, key_gain):
    tokens, heads, width = query_states.shape
    kv_heads = key_states.shape[1]
    group = heads // kv_heads
    half = devices // 2
    steps = half // 2
    per_chip = kv_heads // steps
    bf16, f32 = jnp.bfloat16, jnp.float32
    me = lax.axis_index("seq")[None]

    def call(kernel, name, outs, *operands, scratch=(), specs=None, limit=VMEM_LIMIT):
        return pl.pallas_call(
            kernel,
            out_shape=outs,
            in_specs=specs or [SMEM] + [VMEM] * len(operands),
            out_specs=jax.tree.map(lambda _: VMEM, outs),
            scratch_shapes=scratch,
            compiler_params=pltpu.CompilerParams(vmem_limit_bytes=limit),
            name=name,
        )(me, *operands)

    def to_upper(slot, array):
        links = []
        for device in range(half):
            chip, core = device // 2, device % 2
            links.append((device, half + (chip ^ (core * (steps // 2) + slot)) * 2 + core))
        return lax.ppermute(array, "seq", links)

    def to_chip(step, array):
        links = [(device, ((device // 2) ^ step) * 2 + device % 2) for device in range(devices)]
        return lax.ppermute(array, "seq", links)

    def to_core(array, count):
        return lax.ppermute(array, "seq", [(device, device ^ 1) for device in range(count)])

    shape = jax.ShapeDtypeStruct
    keep, give, *near = call(
        send_kernel,
        "send",
        [shape((steps // 2, per_chip, 2, tokens, width), bf16)] * 2
        + [shape((per_chip * (2 + group), tokens, width), bf16)] * steps,
        query_states,
        key_states,
        value_states,
        jnp.asarray(rope_table(length, width)),
        query_gain[None],
        key_gain[None],
        specs=[SMEM, HBM, HBM, HBM, HBM, VMEM, VMEM],
        scratch=[
            pltpu.VMEM((tokens, heads, width), bf16),
            pltpu.VMEM((tokens, kv_heads, width), bf16),
            pltpu.VMEM((tokens, kv_heads, width), bf16),
            pltpu.VMEM((tokens, width), f32),
            pltpu.VMEM((tokens * heads, width), f32),
            pltpu.VMEM((tokens * kv_heads, width), f32),
            pltpu.VMEM((tokens * kv_heads, width), f32),
            pltpu.SemaphoreType.DMA((4,)),
        ],
        limit=PACK_VMEM,
    )
    got = to_core(give, half)
    joined = pl.pallas_call(
        join_kernel,
        out_shape=[shape((2, per_chip, 2, tokens, width), bf16)] * (steps // 2),
        in_specs=[VMEM] * 2,
        out_specs=[VMEM] * (steps // 2),
        name="join",
    )(keep, got)
    far = [to_upper(slot, array) for slot, array in enumerate(joined)]
    near = [near[0]] + [to_chip(step, near[step]) for step in range(1, steps)]
    pairs, queries = call(
        gather_kernel,
        "gather",
        [shape((2 * steps, per_chip, 2, tokens, width), bf16), shape((steps, per_chip, group, tokens, width), bf16)],
        *near,
        *far,
    )
    others = to_core(pairs, devices)
    lanes = steps * group * tokens
    state = [shape((per_chip, 1, lanes), f32), shape((per_chip, 1, lanes), f32), shape((per_chip, width, lanes), f32)]
    block, _, token = np.indices((steps, group, tokens), dtype=np.int32)
    bounds = np.stack([block * tokens + token + 1, block * tokens]).reshape(2, lanes)
    carried = call(functools.partial(first_kernel, half), "first", state, jnp.asarray(bounds), queries, pairs)
    returned = call(
        functools.partial(second_kernel, half),
        "second",
        [shape((per_chip * group, tokens, width), bf16)] * steps,
        jnp.asarray(bounds),
        queries,
        others,
        *carried,
        scratch=[pltpu.VMEM((steps, per_chip * group, tokens, width), bf16)],
    )
    returned = [returned[0]] + [to_chip(step, returned[step]) for step in range(1, steps)]
    return call(
        unpack_kernel,
        "unpack",
        shape((tokens, heads, width), bf16),
        *returned,
        scratch=[pltpu.VMEM((tokens * heads, width), f32)],
    )


def solution(mesh):
    devices = mesh.shape["seq"]
    groups = mesh.shape["groups"]
    placed = P(("groups", "seq"), None, None)

    def run(query_states, key_states, value_states, query_gain, key_gain):
        length = query_states.shape[0] // groups
        plan = halves_plan if devices == 2 * key_states.shape[1] else general_plan
        return jax.shard_map(
            functools.partial(plan, length, devices),
            mesh=mesh,
            in_specs=(placed, placed, placed, P(), P()),
            out_specs=placed,
            check_vma=False,
        )(query_states, key_states, value_states, query_gain, key_gain)

    return run
```

```python
import functools
import math

import jax
import jax.numpy as jnp
import numpy as np
from jax import lax
from jax.experimental import pallas as pl
from jax.experimental.pallas import tpu as pltpu
from jax.sharding import PartitionSpec as P

ROPE_BASE = 1000000.0
EPSILON = 1e-06
MASKED = -1e30
VMEM_LIMIT = 24 * 1024 * 1024
PACK_VMEM = 56 * 1024 * 1024
VMEM = pl.BlockSpec(memory_space=pltpu.VMEM)
SMEM = pl.BlockSpec(memory_space=pltpu.SMEM)
HBM = pl.BlockSpec(memory_space=pltpu.HBM)
TILE_BLOCKS = 2
CONTRACT = (((1,), (1,)), ((), ()))


def rope_table(length, width):
    half = width // 2
    frequency = np.float64(ROPE_BASE) ** (-(np.arange(half, dtype=np.float64) * 2.0 / width))
    angles = np.arange(length, dtype=np.float32)[:, None] * frequency.astype(np.float32)[None, :]
    wide = angles.astype(np.float64)
    return np.concatenate([np.cos(wide), np.sin(wide)], axis=-1).astype(np.float32)


def pack_kernel(rep, q_ref, k_ref, v_ref, table_ref, qg_ref, kg_ref, out_ref, qf_ref, kf_ref, vf_ref):
    tokens, heads, width = q_ref.shape
    kv_heads = k_ref.shape[1]
    chips, rows = out_ref.shape[:2]
    per_chip = rows - 2
    qf_ref[...] = q_ref[...].astype(jnp.float32).reshape(tokens * heads, width)
    kf_ref[...] = k_ref[...].astype(jnp.float32).reshape(tokens * kv_heads, width)
    vf_ref[...] = v_ref[...].astype(jnp.float32).reshape(tokens * kv_heads, width)
    table = table_ref[...]
    swapped = pltpu.roll(table, width // 2, 1)
    first = lax.broadcasted_iota(jnp.int32, table.shape, 1) < width // 2
    cosine = jnp.where(first, table, swapped)
    sine = jnp.where(first, -swapped, table)

    def rotate(floats, gain):
        mean_square = jnp.mean(floats * floats, axis=-1, keepdims=True)
        normed = floats * lax.rsqrt(mean_square + EPSILON) * gain
        turned = pltpu.roll(normed, width // 2, 1)
        return (normed * cosine + turned * sine).astype(jnp.bfloat16)

    query_gain, key_gain = qg_ref[...], kg_ref[...]
    for head in range(heads):
        floats = qf_ref[pl.ds(head, tokens, stride=heads), :]
        out_ref[head // per_chip, head % per_chip] = rotate(floats, query_gain)
    for head in range(kv_heads):
        floats = kf_ref[pl.ds(head, tokens, stride=kv_heads), :]
        rotated = rotate(floats, key_gain)
        values = vf_ref[pl.ds(head, tokens, stride=kv_heads), :].astype(jnp.bfloat16)
        for copy in range(rep):
            out_ref[head * rep + copy, per_chip] = rotated
            out_ref[head * rep + copy, per_chip + 1] = values


def looped_kernel(core_ref, x_ref, other_ref, out_ref):
    _, rows, tokens, width = x_ref.shape
    per_chip = rows - 2
    core = core_ref[0]
    block = pl.program_id(0)
    scale = math.log2(math.e) / math.sqrt(width)
    queries = x_ref[block, :per_chip].reshape(per_chip * tokens, width)
    row = lax.broadcasted_iota(jnp.int32, (per_chip, tokens, tokens), 1).reshape(per_chip * tokens, tokens)
    column = lax.broadcasted_iota(jnp.int32, (per_chip * tokens, tokens), 1)

    def merge(carried, keys, values, allowed):
        highest, total, weighted = carried
        scores = lax.dot_general(queries, keys, CONTRACT, preferred_element_type=jnp.float32)
        scores = jnp.where(allowed, scores, MASKED)
        new = jnp.maximum(highest, jnp.max(scores, axis=-1, keepdims=True))
        probs = jnp.exp2((scores - new) * scale)
        factor = jnp.exp2((highest - new) * scale)
        total = total * factor + jnp.sum(probs, axis=-1, keepdims=True)
        summed = jnp.dot(probs.astype(jnp.bfloat16), values, preferred_element_type=jnp.float32)
        return new, total, weighted * factor + summed

    def advance(index, carried):
        behind = (block - index) * tokens
        carried = merge(carried, x_ref[index, per_chip], x_ref[index, per_chip + 1], column <= row + behind)
        return merge(carried, other_ref[index, 0], other_ref[index, 1], column < behind + core * tokens)

    initial = (
        jnp.full((per_chip * tokens, 1), MASKED, jnp.float32),
        jnp.zeros((per_chip * tokens, 1), jnp.float32),
        jnp.zeros((per_chip * tokens, width), jnp.float32),
    )
    _, total, weighted = lax.fori_loop(0, block + 1, advance, initial)
    out_ref[block] = (weighted / total).astype(jnp.bfloat16).reshape(per_chip, tokens, width)


def general_plan(length, devices, query_states, key_states, value_states, query_gain, key_gain):
    tokens, heads, width = query_states.shape
    kv_heads = key_states.shape[1]
    chips = devices // 2
    per_chip = heads // chips
    rep = (heads // kv_heads) // per_chip
    me = lax.axis_index("seq")
    core = lax.rem(me, 2)
    same_core = [list(range(start, devices, 2)) for start in range(2)]
    swap = [(device, device ^ 1) for device in range(devices)]
    table = lax.dynamic_slice_in_dim(jnp.asarray(rope_table(length, width)), me * tokens, tokens, 0)
    packed = pl.pallas_call(
        functools.partial(pack_kernel, rep),
        out_shape=jax.ShapeDtypeStruct((chips, per_chip + 2, tokens, width), jnp.bfloat16),
        in_specs=[VMEM] * 6,
        out_specs=VMEM,
        scratch_shapes=[
            pltpu.VMEM((tokens * heads, width), jnp.float32),
            pltpu.VMEM((tokens * kv_heads, width), jnp.float32),
            pltpu.VMEM((tokens * kv_heads, width), jnp.float32),
        ],
        compiler_params=pltpu.CompilerParams(vmem_limit_bytes=48 * 1024 * 1024),
        name="pack",
    )(query_states, key_states, value_states, table, query_gain[None], key_gain[None])
    arrived = lax.all_to_all(
        packed, "seq", split_axis=0, concat_axis=0, axis_index_groups=same_core, tiled=True
    )
    other = lax.ppermute(arrived[:, per_chip:], "seq", swap)
    attended = pl.pallas_call(
        looped_kernel,
        grid=(chips,),
        out_shape=jax.ShapeDtypeStruct((chips, per_chip, tokens, width), jnp.bfloat16),
        in_specs=[SMEM, VMEM, VMEM],
        out_specs=VMEM,
        compiler_params=pltpu.CompilerParams(vmem_limit_bytes=48 * 1024 * 1024),
        name="attention",
    )(core[None], arrived, other)
    returned = lax.all_to_all(
        attended, "seq", split_axis=0, concat_axis=0, axis_index_groups=same_core, tiled=True
    )
    return jnp.transpose(returned.reshape(heads, tokens, width), (1, 0, 2))


def rope_factors(table):
    half = table.shape[1] // 2
    swapped = pltpu.roll(table, half, 1)
    first = lax.broadcasted_iota(jnp.int32, table.shape, 1) < half
    return jnp.where(first, table, swapped), jnp.where(first, -swapped, table)


def normalize(rows):
    floats = rows.astype(jnp.float32)
    squares = floats * floats
    large = squares.astype(jnp.bfloat16)
    small = (squares - large.astype(jnp.float32)).astype(jnp.bfloat16)
    width = rows.shape[1]
    ones = jnp.ones((2 * width, width), jnp.bfloat16)
    added = jnp.dot(jnp.concatenate([large, small], axis=1), ones, preferred_element_type=jnp.float32)
    return floats * lax.rsqrt(added * (1.0 / width) + EPSILON)


def turn(normed, gain, cosine, sine):
    scaled = normed * gain
    return (scaled * cosine + pltpu.roll(scaled, scaled.shape[1] // 2, 1) * sine).astype(jnp.bfloat16)


def send_kernel(me_ref, q_hbm, k_hbm, v_hbm, other_k_hbm, other_v_hbm, table_hbm, query_gain_ref, key_gain_ref, *refs):
    outs, (q_ref, k_ref, v_ref, table_ref, qf_ref, kf_ref, vf_ref, sems) = refs[:-8], refs[-8:]
    tokens, heads, width = q_ref.shape
    slots, per_chip = (len(outs) // 3), outs[0].shape[1]
    far, fulls = outs[:slots], outs[slots:]
    steps, kv_heads = len(fulls), k_ref.shape[2]
    first, per_full = 2 * per_chip, heads // steps
    me = me_ref[0]
    chip, core = lax.rem(me // 2, steps), lax.rem(me, 2)
    copies = []
    for side, (k, v, device) in enumerate(((k_hbm, v_hbm, me), (other_k_hbm, other_v_hbm, me + 1 - 2 * core))):
        rows = pl.ds(pl.multiple_of(device * tokens, 8), tokens)
        for kind, (source, target) in enumerate(((k, k_ref), (table_hbm.at[rows], table_ref), (v, v_ref))):
            copies.append(pltpu.make_async_copy(source, target.at[side], sems.at[3 * side + kind]))
    copies.insert(3, pltpu.make_async_copy(q_hbm, q_ref, sems.at[6]))
    for copy in copies:
        copy.start()
    key_gain = key_gain_ref[...]

    def keys_of(head, factors):
        return turn(kf_ref[pl.ds(head, tokens, stride=kv_heads), :], key_gain, *factors)

    def values_of(head):
        return vf_ref[pl.ds(head, tokens, stride=kv_heads), :].astype(jnp.bfloat16)

    def load(side, waits):
        for copy in waits:
            copy.wait()
        kf_ref[...] = normalize(k_ref[side].reshape(tokens * kv_heads, width))
        vf_ref[...] = v_ref[side].astype(jnp.float32).reshape(tokens * kv_heads, width)
        return rope_factors(table_ref[side])

    factors = load(0, copies[:3])
    for step in range(steps):
        for row in range(per_chip):
            head = (chip ^ step) * per_chip + row
            fulls[step][2 * row], fulls[step][2 * row + 1] = keys_of(head, factors), values_of(head)
    copies[3].wait()
    qf_ref[...] = normalize(q_ref[...].reshape(tokens * heads, width))
    for step in range(steps):
        for row in range(per_full):
            normed = qf_ref[pl.ds((chip ^ step) * per_full + row, tokens, stride=heads), :]
            fulls[step][first + row] = turn(normed, query_gain_ref[...], *factors)
    for which in range(2):

        @pl.when(core == which)
        def _():
            for slot in range(slots):
                for row in range(first):
                    far[slot][0, row // 2, row % 2] = fulls[which * slots + slot][row]

    factors = load(1, copies[4:])
    for slot in range(slots):
        for row in range(per_chip):
            head = (chip ^ (core * slots + slot)) * per_chip + row
            far[slot][1, row, 0], far[slot][1, row, 1] = keys_of(head, factors), values_of(head)


def weigh(segments, queries, state):
    scale = math.log2(math.e) / math.sqrt(queries.shape[1])
    scores = []
    for keys, _, allowed in segments:
        part = lax.dot_general(keys, queries, CONTRACT, preferred_element_type=jnp.float32)
        scores.append(part if allowed is None else jnp.where(allowed, part, MASKED))
    tops = [jnp.max(part, axis=0, keepdims=True) for part in scores] + ([] if state is None else [state[0]])
    highest = functools.reduce(jnp.maximum, tops)
    total = weighted = None
    if state is not None:
        factor = jnp.exp2((state[0] - highest) * scale)
        total, weighted = state[1] * factor, state[2] * factor
    for part, (_, values, _) in zip(scores, segments):
        probs = jnp.exp2((part - highest) * scale)
        added = jnp.sum(probs, axis=0, keepdims=True)
        summed = lax.dot_general(
            values, probs.astype(jnp.bfloat16), (((0,), (0,)), ((), ())), preferred_element_type=jnp.float32
        )
        total = added if total is None else total + added
        weighted = summed if weighted is None else weighted + summed
    return highest, total, weighted


def gather_kernel(me_ref, *refs):
    pair_ref, query_ref = refs[-2:]
    steps, per_chip = query_ref.shape[:2]
    near, far = refs[:steps], refs[steps:-2]
    chip = lax.rem(me_ref[0] // 2, steps)
    for step in range(steps):
        pair_ref[chip ^ step] = near[step][: 2 * per_chip].reshape(pair_ref.shape[1:])
        query_ref[chip ^ step] = near[step][2 * per_chip :].reshape(query_ref.shape[1:])
    for slot, ref in enumerate(far):
        pair_ref[steps + 2 * slot : steps + 2 * slot + 2] = ref[...]


def add_core(upper, bound, query_ref, pair_ref, state_refs, store):
    steps, kv_heads, group, tokens, width = query_ref.shape
    lanes = TILE_BLOCKS * group * tokens

    def tiles(with_far):
        for head in range(kv_heads):

            def segment(start, stop, allowed):
                rows = (stop - start) * tokens
                return [pair_ref[start:stop, head, i].reshape(rows, width) for i in range(2)] + [allowed]

            for first in range(0, steps, TILE_BLOCKS):
                count = first + TILE_BLOCKS
                place = slice(first * group * tokens, first * group * tokens + lanes)
                queries = query_ref[first:count, head].reshape(lanes, width)
                index = first * tokens + lax.broadcasted_iota(jnp.int32, (TILE_BLOCKS * tokens, lanes), 0)
                segments = [segment(first, count, index < bound[:, place])]
                if first > 0:
                    segments.append(segment(0, first, None))
                if with_far:
                    segments.append(segment(steps, 2 * steps, None))
                state = [ref[head, :, place] for ref in state_refs] if state_refs else None
                store(head, first, place, *weigh(segments, queries, state))

    pl.when(upper)(functools.partial(tiles, True))
    pl.when(jnp.logical_not(upper))(functools.partial(tiles, False))


def first_kernel(half, me_ref, bounds_ref, query_ref, pair_ref, *outs):
    def store(head, first, place, *values):
        for ref, value in zip(outs, values):
            ref[head, :, place] = value

    add_core(me_ref[0] >= half, bounds_ref[0:1], query_ref, pair_ref, None, store)


def second_kernel(half, me_ref, bounds_ref, query_ref, pair_ref, *refs):
    steps, kv_heads, group, tokens, width = query_ref.shape
    state, outs, out_ref = refs[:3], refs[3:-1], refs[-1]
    me = me_ref[0]

    def store(head, first, place, highest, total, weighted):
        result = jnp.transpose(weighted * (1.0 / total)).astype(jnp.bfloat16)
        rows = slice(head * group, (head + 1) * group)
        out_ref[first : first + TILE_BLOCKS, rows] = result.reshape(TILE_BLOCKS, group, tokens, width)

    bound = bounds_ref[1:2] + lax.rem(me, 2) * tokens
    add_core(me >= half, bound, query_ref, pair_ref, state, store)
    chip = lax.rem(me // 2, steps)
    for step in range(steps):
        outs[step][...] = out_ref[chip ^ step]


def unpack_kernel(me_ref, *refs):
    parts, (out_ref, floats_ref) = refs[:-2], refs[-2:]
    tokens, heads, width = out_ref.shape
    steps = len(parts)
    per_chip = heads // steps
    chip = lax.rem(me_ref[0] // 2, steps)
    for step in range(steps):
        for row in range(per_chip):
            head = (chip ^ step) * per_chip + row
            floats_ref[pl.ds(head, tokens, stride=heads), :] = parts[step][row].astype(jnp.float32)
    out_ref[...] = floats_ref[...].reshape(tokens, heads, width).astype(jnp.bfloat16)


def halves_plan(length, devices, query_states, key_states, value_states, query_gain, key_gain):
    tokens, heads, width = query_states.shape
    kv_heads = key_states.shape[1]
    group = heads // kv_heads
    half = devices // 2
    steps = half // 2
    per_chip = kv_heads // steps
    bf16, f32 = jnp.bfloat16, jnp.float32
    me = lax.axis_index("seq")[None]

    def call(kernel, name, outs, *operands, scratch=(), specs=None, limit=VMEM_LIMIT):
        return pl.pallas_call(
            kernel,
            out_shape=outs,
            in_specs=specs or [SMEM] + [VMEM] * len(operands),
            out_specs=jax.tree.map(lambda _: VMEM, outs),
            scratch_shapes=scratch,
            compiler_params=pltpu.CompilerParams(vmem_limit_bytes=limit),
            name=name,
        )(me, *operands)

    def to_upper(slot, array):
        links = []
        for device in range(half):
            chip, core = device // 2, device % 2
            links.append((device, half + (chip ^ (core * (steps // 2) + slot)) * 2 + core))
        return lax.ppermute(array, "seq", links)

    def to_chip(step, array):
        links = [(device, ((device // 2) ^ step) * 2 + device % 2) for device in range(devices)]
        return lax.ppermute(array, "seq", links)

    def to_core(array, count):
        return lax.ppermute(array, "seq", [(device, device ^ 1) for device in range(count)])

    shape = jax.ShapeDtypeStruct
    slots = steps // 2
    others = [to_core(array, half) for array in (key_states, value_states)]
    packed = call(
        send_kernel,
        "send",
        [shape((2, per_chip, 2, tokens, width), bf16)] * slots
        + [shape((per_chip * (2 + group), tokens, width), bf16)] * steps,
        query_states,
        key_states,
        value_states,
        *others,
        jnp.asarray(rope_table(length, width)),
        query_gain[None],
        key_gain[None],
        specs=[SMEM] + [HBM] * 3 + [pl.BlockSpec(memory_space=pl.ANY)] * 2 + [HBM] + [VMEM] * 2,
        scratch=[
            pltpu.VMEM((tokens, heads, width), bf16),
            pltpu.VMEM((2, tokens, kv_heads, width), bf16),
            pltpu.VMEM((2, tokens, kv_heads, width), bf16),
            pltpu.VMEM((2, tokens, width), f32),
            pltpu.VMEM((tokens * heads, width), f32),
            pltpu.VMEM((tokens * kv_heads, width), f32),
            pltpu.VMEM((tokens * kv_heads, width), f32),
            pltpu.SemaphoreType.DMA((7,)),
        ],
        limit=PACK_VMEM,
    )
    joined, near = packed[:slots], packed[slots:]
    far = [to_upper(slot, array) for slot, array in enumerate(joined)]
    near = [near[0]] + [to_chip(step, near[step]) for step in range(1, steps)]
    pairs, queries = call(
        gather_kernel,
        "gather",
        [shape((2 * steps, per_chip, 2, tokens, width), bf16), shape((steps, per_chip, group, tokens, width), bf16)],
        *near,
        *far,
    )
    others = to_core(pairs, devices)
    lanes = steps * group * tokens
    state = [shape((per_chip, 1, lanes), f32), shape((per_chip, 1, lanes), f32), shape((per_chip, width, lanes), f32)]
    block, _, token = np.indices((steps, group, tokens), dtype=np.int32)
    bounds = np.stack([block * tokens + token + 1, block * tokens]).reshape(2, lanes)
    carried = call(functools.partial(first_kernel, half), "first", state, jnp.asarray(bounds), queries, pairs)
    returned = call(
        functools.partial(second_kernel, half),
        "second",
        [shape((per_chip * group, tokens, width), bf16)] * steps,
        jnp.asarray(bounds),
        queries,
        others,
        *carried,
        scratch=[pltpu.VMEM((steps, per_chip * group, tokens, width), bf16)],
    )
    returned = [returned[0]] + [to_chip(step, returned[step]) for step in range(1, steps)]
    return call(
        unpack_kernel,
        "unpack",
        shape((tokens, heads, width), bf16),
        *returned,
        scratch=[pltpu.VMEM((tokens * heads, width), f32)],
    )


def solution(mesh):
    devices = mesh.shape["seq"]
    groups = mesh.shape["groups"]
    placed = P(("groups", "seq"), None, None)

    def run(query_states, key_states, value_states, query_gain, key_gain):
        length = query_states.shape[0] // groups
        plan = halves_plan if devices == 2 * key_states.shape[1] else general_plan
        return jax.shard_map(
            functools.partial(plan, length, devices),
            mesh=mesh,
            in_specs=(placed, placed, placed, P(), P()),
            out_specs=placed,
            check_vma=False,
        )(query_states, key_states, value_states, query_gain, key_gain)

    return run
```

```python
import functools
import math

import jax
import jax.numpy as jnp
import numpy as np
from jax import lax
from jax.experimental import pallas as pl
from jax.experimental.pallas import tpu as pltpu
from jax.sharding import PartitionSpec as P

ROPE_BASE = 1000000.0
EPSILON = 1e-06
MASKED = -1e30
VMEM_LIMIT = 24 * 1024 * 1024
PACK_VMEM = 56 * 1024 * 1024
VMEM = pl.BlockSpec(memory_space=pltpu.VMEM)
SMEM = pl.BlockSpec(memory_space=pltpu.SMEM)
HBM = pl.BlockSpec(memory_space=pltpu.HBM)
TILE_BLOCKS = 2
CONTRACT = (((1,), (1,)), ((), ()))


def rope_table(length, width):
    half = width // 2
    frequency = np.float64(ROPE_BASE) ** (-(np.arange(half, dtype=np.float64) * 2.0 / width))
    angles = np.arange(length, dtype=np.float32)[:, None] * frequency.astype(np.float32)[None, :]
    wide = angles.astype(np.float64)
    return np.concatenate([np.cos(wide), np.sin(wide)], axis=-1).astype(np.float32)


def pack_kernel(rep, q_ref, k_ref, v_ref, table_ref, qg_ref, kg_ref, out_ref, qf_ref, kf_ref, vf_ref):
    tokens, heads, width = q_ref.shape
    kv_heads = k_ref.shape[1]
    chips, rows = out_ref.shape[:2]
    per_chip = rows - 2
    qf_ref[...] = q_ref[...].astype(jnp.float32).reshape(tokens * heads, width)
    kf_ref[...] = k_ref[...].astype(jnp.float32).reshape(tokens * kv_heads, width)
    vf_ref[...] = v_ref[...].astype(jnp.float32).reshape(tokens * kv_heads, width)
    table = table_ref[...]
    swapped = pltpu.roll(table, width // 2, 1)
    first = lax.broadcasted_iota(jnp.int32, table.shape, 1) < width // 2
    cosine = jnp.where(first, table, swapped)
    sine = jnp.where(first, -swapped, table)

    def rotate(floats, gain):
        mean_square = jnp.mean(floats * floats, axis=-1, keepdims=True)
        normed = floats * lax.rsqrt(mean_square + EPSILON) * gain
        turned = pltpu.roll(normed, width // 2, 1)
        return (normed * cosine + turned * sine).astype(jnp.bfloat16)

    query_gain, key_gain = qg_ref[...], kg_ref[...]
    for head in range(heads):
        floats = qf_ref[pl.ds(head, tokens, stride=heads), :]
        out_ref[head // per_chip, head % per_chip] = rotate(floats, query_gain)
    for head in range(kv_heads):
        floats = kf_ref[pl.ds(head, tokens, stride=kv_heads), :]
        rotated = rotate(floats, key_gain)
        values = vf_ref[pl.ds(head, tokens, stride=kv_heads), :].astype(jnp.bfloat16)
        for copy in range(rep):
            out_ref[head * rep + copy, per_chip] = rotated
            out_ref[head * rep + copy, per_chip + 1] = values


def looped_kernel(core_ref, x_ref, other_ref, out_ref):
    _, rows, tokens, width = x_ref.shape
    per_chip = rows - 2
    core = core_ref[0]
    block = pl.program_id(0)
    scale = math.log2(math.e) / math.sqrt(width)
    queries = x_ref[block, :per_chip].reshape(per_chip * tokens, width)
    row = lax.broadcasted_iota(jnp.int32, (per_chip, tokens, tokens), 1).reshape(per_chip * tokens, tokens)
    column = lax.broadcasted_iota(jnp.int32, (per_chip * tokens, tokens), 1)

    def merge(carried, keys, values, allowed):
        highest, total, weighted = carried
        scores = lax.dot_general(queries, keys, CONTRACT, preferred_element_type=jnp.float32)
        scores = jnp.where(allowed, scores, MASKED)
        new = jnp.maximum(highest, jnp.max(scores, axis=-1, keepdims=True))
        probs = jnp.exp2((scores - new) * scale)
        factor = jnp.exp2((highest - new) * scale)
        total = total * factor + jnp.sum(probs, axis=-1, keepdims=True)
        summed = jnp.dot(probs.astype(jnp.bfloat16), values, preferred_element_type=jnp.float32)
        return new, total, weighted * factor + summed

    def advance(index, carried):
        behind = (block - index) * tokens
        carried = merge(carried, x_ref[index, per_chip], x_ref[index, per_chip + 1], column <= row + behind)
        return merge(carried, other_ref[index, 0], other_ref[index, 1], column < behind + core * tokens)

    initial = (
        jnp.full((per_chip * tokens, 1), MASKED, jnp.float32),
        jnp.zeros((per_chip * tokens, 1), jnp.float32),
        jnp.zeros((per_chip * tokens, width), jnp.float32),
    )
    _, total, weighted = lax.fori_loop(0, block + 1, advance, initial)
    out_ref[block] = (weighted / total).astype(jnp.bfloat16).reshape(per_chip, tokens, width)


def general_plan(length, devices, query_states, key_states, value_states, query_gain, key_gain):
    tokens, heads, width = query_states.shape
    kv_heads = key_states.shape[1]
    chips = devices // 2
    per_chip = heads // chips
    rep = (heads // kv_heads) // per_chip
    me = lax.axis_index("seq")
    core = lax.rem(me, 2)
    same_core = [list(range(start, devices, 2)) for start in range(2)]
    swap = [(device, device ^ 1) for device in range(devices)]
    table = lax.dynamic_slice_in_dim(jnp.asarray(rope_table(length, width)), me * tokens, tokens, 0)
    packed = pl.pallas_call(
        functools.partial(pack_kernel, rep),
        out_shape=jax.ShapeDtypeStruct((chips, per_chip + 2, tokens, width), jnp.bfloat16),
        in_specs=[VMEM] * 6,
        out_specs=VMEM,
        scratch_shapes=[
            pltpu.VMEM((tokens * heads, width), jnp.float32),
            pltpu.VMEM((tokens * kv_heads, width), jnp.float32),
            pltpu.VMEM((tokens * kv_heads, width), jnp.float32),
        ],
        compiler_params=pltpu.CompilerParams(vmem_limit_bytes=48 * 1024 * 1024),
        name="pack",
    )(query_states, key_states, value_states, table, query_gain[None], key_gain[None])
    arrived = lax.all_to_all(
        packed, "seq", split_axis=0, concat_axis=0, axis_index_groups=same_core, tiled=True
    )
    other = lax.ppermute(arrived[:, per_chip:], "seq", swap)
    attended = pl.pallas_call(
        looped_kernel,
        grid=(chips,),
        out_shape=jax.ShapeDtypeStruct((chips, per_chip, tokens, width), jnp.bfloat16),
        in_specs=[SMEM, VMEM, VMEM],
        out_specs=VMEM,
        compiler_params=pltpu.CompilerParams(vmem_limit_bytes=48 * 1024 * 1024),
        name="attention",
    )(core[None], arrived, other)
    returned = lax.all_to_all(
        attended, "seq", split_axis=0, concat_axis=0, axis_index_groups=same_core, tiled=True
    )
    return jnp.transpose(returned.reshape(heads, tokens, width), (1, 0, 2))


def rope_factors(table):
    half = table.shape[1] // 2
    swapped = pltpu.roll(table, half, 1)
    first = lax.broadcasted_iota(jnp.int32, table.shape, 1) < half
    return jnp.where(first, table, swapped), jnp.where(first, -swapped, table)


def normalize(rows):
    floats = rows.astype(jnp.float32)
    squares = floats * floats
    large = squares.astype(jnp.bfloat16)
    small = (squares - large.astype(jnp.float32)).astype(jnp.bfloat16)
    width = rows.shape[1]
    ones = jnp.ones((2 * width, width), jnp.bfloat16)
    added = jnp.dot(jnp.concatenate([large, small], axis=1), ones, preferred_element_type=jnp.float32)
    return floats * lax.rsqrt(added * (1.0 / width) + EPSILON)


def turn(normed, gain, cosine, sine):
    scaled = normed * gain
    return (scaled * cosine + pltpu.roll(scaled, scaled.shape[1] // 2, 1) * sine).astype(jnp.bfloat16)


def send_kernel(me_ref, q_hbm, k_hbm, v_hbm, table_hbm, query_gain_ref, key_gain_ref, *refs):
    outs, (q_ref, k_ref, v_ref, table_ref, qf_ref, kf_ref, vf_ref, sems) = refs[:-8], refs[-8:]
    steps = len(outs) // 2
    pairs, fulls = outs[:steps], outs[steps:]
    tokens, heads, width = q_ref.shape
    kv_heads, per_chip = k_ref.shape[1], pairs[0].shape[0]
    first, per_full = 2 * per_chip, heads // steps
    me = me_ref[0]
    chip = lax.rem(me // 2, steps)
    start = pl.multiple_of(me * tokens, 8)
    copies = [
        pltpu.make_async_copy(k_hbm, k_ref, sems.at[0]),
        pltpu.make_async_copy(table_hbm.at[pl.ds(start, tokens)], table_ref, sems.at[1]),
        pltpu.make_async_copy(v_hbm, v_ref, sems.at[2]),
        pltpu.make_async_copy(q_hbm, q_ref, sems.at[3]),
    ]
    for copy in copies:
        copy.start()
    copies[0].wait()
    kf_ref[...] = normalize(k_ref[...].reshape(tokens * kv_heads, width))
    copies[1].wait()
    cosine, sine = rope_factors(table_ref[...])
    copies[2].wait()
    vf_ref[...] = v_ref[...].astype(jnp.float32).reshape(tokens * kv_heads, width)
    for step in range(steps):
        for row in range(per_chip):
            head = (chip ^ step) * per_chip + row
            keys = turn(kf_ref[pl.ds(head, tokens, stride=kv_heads), :], key_gain_ref[...], cosine, sine)
            values = vf_ref[pl.ds(head, tokens, stride=kv_heads), :].astype(jnp.bfloat16)
            pairs[step][row, 0] = keys
            fulls[step][2 * row] = keys
            pairs[step][row, 1] = values
            fulls[step][2 * row + 1] = values
    copies[3].wait()
    qf_ref[...] = normalize(q_ref[...].reshape(tokens * heads, width))
    for step in range(steps):
        for row in range(per_full):
            normed = qf_ref[pl.ds((chip ^ step) * per_full + row, tokens, stride=heads), :]
            fulls[step][first + row] = turn(normed, query_gain_ref[...], cosine, sine)


def weigh(segments, queries, state):
    scale = math.log2(math.e) / math.sqrt(queries.shape[1])
    scores = []
    for keys, _, allowed in segments:
        part = lax.dot_general(keys, queries, CONTRACT, preferred_element_type=jnp.float32)
        scores.append(part if allowed is None else jnp.where(allowed, part, MASKED))
    tops = [jnp.max(part, axis=0, keepdims=True) for part in scores] + ([] if state is None else [state[0]])
    highest = functools.reduce(jnp.maximum, tops)
    total = weighted = None
    if state is not None:
        factor = jnp.exp2((state[0] - highest) * scale)
        total, weighted = state[1] * factor, state[2] * factor
    for part, (_, values, _) in zip(scores, segments):
        probs = jnp.exp2((part - highest) * scale)
        added = jnp.sum(probs, axis=0, keepdims=True)
        summed = lax.dot_general(
            values, probs.astype(jnp.bfloat16), (((0,), (0,)), ((), ())), preferred_element_type=jnp.float32
        )
        total = added if total is None else total + added
        weighted = summed if weighted is None else weighted + summed
    return highest, total, weighted


def gather_kernel(me_ref, *refs):
    pair_ref, query_ref = refs[-2:]
    steps, per_chip = query_ref.shape[:2]
    near, far = refs[:steps], refs[steps : 2 * steps]
    chip = lax.rem(me_ref[0] // 2, steps)
    for step in range(steps):
        pair_ref[chip ^ step] = near[step][: 2 * per_chip].reshape(pair_ref.shape[1:])
        query_ref[chip ^ step] = near[step][2 * per_chip :].reshape(query_ref.shape[1:])
        pair_ref[steps + step] = far[step][...]


def add_core(upper, bound, query_ref, pair_ref, state_refs, store):
    steps, kv_heads, group, tokens, width = query_ref.shape
    lanes = TILE_BLOCKS * group * tokens

    def tiles(with_far):
        for head in range(kv_heads):

            def segment(start, stop, allowed):
                rows = (stop - start) * tokens
                return [pair_ref[start:stop, head, i].reshape(rows, width) for i in range(2)] + [allowed]

            for first in range(0, steps, TILE_BLOCKS):
                count = first + TILE_BLOCKS
                place = slice(first * group * tokens, first * group * tokens + lanes)
                queries = query_ref[first:count, head].reshape(lanes, width)
                index = first * tokens + lax.broadcasted_iota(jnp.int32, (TILE_BLOCKS * tokens, lanes), 0)
                segments = [segment(first, count, index < bound[:, place])]
                if first > 0:
                    segments.append(segment(0, first, None))
                if with_far:
                    segments.append(segment(steps, 2 * steps, None))
                state = [ref[head, :, place] for ref in state_refs] if state_refs else None
                store(head, first, place, *weigh(segments, queries, state))

    pl.when(upper)(functools.partial(tiles, True))
    pl.when(jnp.logical_not(upper))(functools.partial(tiles, False))


def first_kernel(half, me_ref, bounds_ref, query_ref, pair_ref, *outs):
    def store(head, first, place, *values):
        for ref, value in zip(outs, values):
            ref[head, :, place] = value

    add_core(me_ref[0] >= half, bounds_ref[0:1], query_ref, pair_ref, None, store)


def second_kernel(half, me_ref, bounds_ref, query_ref, pair_ref, *refs):
    steps, kv_heads, group, tokens, width = query_ref.shape
    state, outs, out_ref = refs[:3], refs[3:-1], refs[-1]
    me = me_ref[0]

    def store(head, first, place, highest, total, weighted):
        result = jnp.transpose(weighted * (1.0 / total)).astype(jnp.bfloat16)
        rows = slice(head * group, (head + 1) * group)
        out_ref[first : first + TILE_BLOCKS, rows] = result.reshape(TILE_BLOCKS, group, tokens, width)

    bound = bounds_ref[1:2] + lax.rem(me, 2) * tokens
    add_core(me >= half, bound, query_ref, pair_ref, state, store)
    chip = lax.rem(me // 2, steps)
    for step in range(steps):
        outs[step][...] = out_ref[chip ^ step]


def unpack_kernel(me_ref, *refs):
    parts, (out_ref, floats_ref) = refs[:-2], refs[-2:]
    tokens, heads, width = out_ref.shape
    steps = len(parts)
    per_chip = heads // steps
    chip = lax.rem(me_ref[0] // 2, steps)
    for step in range(steps):
        for row in range(per_chip):
            head = (chip ^ step) * per_chip + row
            floats_ref[pl.ds(head, tokens, stride=heads), :] = parts[step][row].astype(jnp.float32)
    out_ref[...] = floats_ref[...].reshape(tokens, heads, width).astype(jnp.bfloat16)


def halves_plan(length, devices, query_states, key_states, value_states, query_gain, key_gain):
    tokens, heads, width = query_states.shape
    kv_heads = key_states.shape[1]
    group = heads // kv_heads
    half = devices // 2
    steps = half // 2
    per_chip = kv_heads // steps
    bf16, f32 = jnp.bfloat16, jnp.float32
    me = lax.axis_index("seq")[None]

    def call(kernel, name, outs, *operands, scratch=(), specs=None, limit=VMEM_LIMIT):
        return pl.pallas_call(
            kernel,
            out_shape=outs,
            in_specs=specs or [SMEM] + [VMEM] * len(operands),
            out_specs=jax.tree.map(lambda _: VMEM, outs),
            scratch_shapes=scratch,
            compiler_params=pltpu.CompilerParams(vmem_limit_bytes=limit),
            name=name,
        )(me, *operands)

    def to_upper(step, array):
        links = [(device, half + ((device // 2) ^ step) * 2 + device % 2) for device in range(half)]
        return lax.ppermute(array, "seq", links)

    def to_chip(step, array):
        links = [(device, ((device // 2) ^ step) * 2 + device % 2) for device in range(devices)]
        return lax.ppermute(array, "seq", links)

    def to_core(array):
        return lax.ppermute(array, "seq", [(device, device ^ 1) for device in range(devices)])

    shape = jax.ShapeDtypeStruct
    packed = call(
        send_kernel,
        "send",
        [shape((per_chip, 2, tokens, width), bf16)] * steps
        + [shape((per_chip * (2 + group), tokens, width), bf16)] * steps,
        query_states,
        key_states,
        value_states,
        jnp.asarray(rope_table(length, width)),
        query_gain[None],
        key_gain[None],
        specs=[SMEM, HBM, HBM, HBM, HBM, VMEM, VMEM],
        scratch=[
            pltpu.VMEM((tokens, heads, width), bf16),
            pltpu.VMEM((tokens, kv_heads, width), bf16),
            pltpu.VMEM((tokens, kv_heads, width), bf16),
            pltpu.VMEM((tokens, width), f32),
            pltpu.VMEM((tokens * heads, width), f32),
            pltpu.VMEM((tokens * kv_heads, width), f32),
            pltpu.VMEM((tokens * kv_heads, width), f32),
            pltpu.SemaphoreType.DMA((4,)),
        ],
        limit=PACK_VMEM,
    )
    pairs, near = packed[:steps], packed[steps:]
    far = [to_upper(step, pair) for step, pair in enumerate(pairs)]
    near = [near[0]] + [
        lax.cond(me[0] >= 0, functools.partial(to_chip, step), jnp.zeros_like, near[step]) for step in range(1, steps)
    ]
    near, far = lax.optimization_barrier((near, far))
    pairs, queries = call(
        gather_kernel,
        "gather",
        [shape((2 * steps, per_chip, 2, tokens, width), bf16), shape((steps, per_chip, group, tokens, width), bf16)],
        *near,
        *far,
    )
    others = to_core(pairs)
    lanes = steps * group * tokens
    state = [shape((per_chip, 1, lanes), f32), shape((per_chip, 1, lanes), f32), shape((per_chip, width, lanes), f32)]
    block, _, token = np.indices((steps, group, tokens), dtype=np.int32)
    bounds = np.stack([block * tokens + token + 1, block * tokens]).reshape(2, lanes)
    carried = call(functools.partial(first_kernel, half), "first", state, jnp.asarray(bounds), queries, pairs)
    returned = call(
        functools.partial(second_kernel, half),
        "second",
        [shape((per_chip * group, tokens, width), bf16)] * steps,
        jnp.asarray(bounds),
        queries,
        others,
        *carried,
        scratch=[pltpu.VMEM((steps, per_chip * group, tokens, width), bf16)],
    )
    returned = [returned[0]] + [to_chip(step, returned[step]) for step in range(1, steps)]
    return call(
        unpack_kernel,
        "unpack",
        shape((tokens, heads, width), bf16),
        *returned,
        scratch=[pltpu.VMEM((tokens * heads, width), f32)],
    )


def solution(mesh):
    devices = mesh.shape["seq"]
    groups = mesh.shape["groups"]
    placed = P(("groups", "seq"), None, None)

    def run(query_states, key_states, value_states, query_gain, key_gain):
        length = query_states.shape[0] // groups
        plan = halves_plan if devices == 2 * key_states.shape[1] else general_plan
        return jax.shard_map(
            functools.partial(plan, length, devices),
            mesh=mesh,
            in_specs=(placed, placed, placed, P(), P()),
            out_specs=placed,
            check_vma=False,
        )(query_states, key_states, value_states, query_gain, key_gain)

    return run
```

```python
import functools
import math

import jax
import jax.numpy as jnp
import numpy as np
from jax import lax
from jax.experimental import pallas as pl
from jax.experimental.pallas import tpu as pltpu
from jax.sharding import PartitionSpec as P

ROPE_BASE = 1000000.0
EPSILON = 1e-06
MASKED = -1e30
VMEM_LIMIT = 24 * 1024 * 1024
PACK_VMEM = 56 * 1024 * 1024
VMEM = pl.BlockSpec(memory_space=pltpu.VMEM)
SMEM = pl.BlockSpec(memory_space=pltpu.SMEM)
HBM = pl.BlockSpec(memory_space=pltpu.HBM)
NEAR_BLOCKS = 2
FAR_BLOCKS = 2
CONTRACT = (((1,), (1,)), ((), ()))


def rope_table(length, width):
    half = width // 2
    frequency = np.float64(ROPE_BASE) ** (-(np.arange(half, dtype=np.float64) * 2.0 / width))
    angles = np.arange(length, dtype=np.float32)[:, None] * frequency.astype(np.float32)[None, :]
    wide = angles.astype(np.float64)
    return np.concatenate([np.cos(wide), np.sin(wide)], axis=-1).astype(np.float32)


def pack_kernel(rep, q_ref, k_ref, v_ref, table_ref, qg_ref, kg_ref, out_ref, qf_ref, kf_ref, vf_ref):
    tokens, heads, width = q_ref.shape
    kv_heads = k_ref.shape[1]
    chips, rows = out_ref.shape[:2]
    per_chip = rows - 2
    qf_ref[...] = q_ref[...].astype(jnp.float32).reshape(tokens * heads, width)
    kf_ref[...] = k_ref[...].astype(jnp.float32).reshape(tokens * kv_heads, width)
    vf_ref[...] = v_ref[...].astype(jnp.float32).reshape(tokens * kv_heads, width)
    table = table_ref[...]
    swapped = pltpu.roll(table, width // 2, 1)
    first = lax.broadcasted_iota(jnp.int32, table.shape, 1) < width // 2
    cosine = jnp.where(first, table, swapped)
    sine = jnp.where(first, -swapped, table)

    def rotate(floats, gain):
        mean_square = jnp.mean(floats * floats, axis=-1, keepdims=True)
        normed = floats * lax.rsqrt(mean_square + EPSILON) * gain
        turned = pltpu.roll(normed, width // 2, 1)
        return (normed * cosine + turned * sine).astype(jnp.bfloat16)

    query_gain, key_gain = qg_ref[...], kg_ref[...]
    for head in range(heads):
        floats = qf_ref[pl.ds(head, tokens, stride=heads), :]
        out_ref[head // per_chip, head % per_chip] = rotate(floats, query_gain)
    for head in range(kv_heads):
        floats = kf_ref[pl.ds(head, tokens, stride=kv_heads), :]
        rotated = rotate(floats, key_gain)
        values = vf_ref[pl.ds(head, tokens, stride=kv_heads), :].astype(jnp.bfloat16)
        for copy in range(rep):
            out_ref[head * rep + copy, per_chip] = rotated
            out_ref[head * rep + copy, per_chip + 1] = values


def looped_kernel(core_ref, x_ref, other_ref, out_ref):
    _, rows, tokens, width = x_ref.shape
    per_chip = rows - 2
    core = core_ref[0]
    block = pl.program_id(0)
    scale = math.log2(math.e) / math.sqrt(width)
    queries = x_ref[block, :per_chip].reshape(per_chip * tokens, width)
    row = lax.broadcasted_iota(jnp.int32, (per_chip, tokens, tokens), 1).reshape(per_chip * tokens, tokens)
    column = lax.broadcasted_iota(jnp.int32, (per_chip * tokens, tokens), 1)

    def merge(carried, keys, values, allowed):
        highest, total, weighted = carried
        scores = lax.dot_general(queries, keys, CONTRACT, preferred_element_type=jnp.float32)
        scores = jnp.where(allowed, scores, MASKED)
        new = jnp.maximum(highest, jnp.max(scores, axis=-1, keepdims=True))
        probs = jnp.exp2((scores - new) * scale)
        factor = jnp.exp2((highest - new) * scale)
        total = total * factor + jnp.sum(probs, axis=-1, keepdims=True)
        summed = jnp.dot(probs.astype(jnp.bfloat16), values, preferred_element_type=jnp.float32)
        return new, total, weighted * factor + summed

    def advance(index, carried):
        behind = (block - index) * tokens
        carried = merge(carried, x_ref[index, per_chip], x_ref[index, per_chip + 1], column <= row + behind)
        return merge(carried, other_ref[index, 0], other_ref[index, 1], column < behind + core * tokens)

    initial = (
        jnp.full((per_chip * tokens, 1), MASKED, jnp.float32),
        jnp.zeros((per_chip * tokens, 1), jnp.float32),
        jnp.zeros((per_chip * tokens, width), jnp.float32),
    )
    _, total, weighted = lax.fori_loop(0, block + 1, advance, initial)
    out_ref[block] = (weighted / total).astype(jnp.bfloat16).reshape(per_chip, tokens, width)


def general_plan(length, devices, query_states, key_states, value_states, query_gain, key_gain):
    tokens, heads, width = query_states.shape
    kv_heads = key_states.shape[1]
    chips = devices // 2
    per_chip = heads // chips
    rep = (heads // kv_heads) // per_chip
    me = lax.axis_index("seq")
    core = lax.rem(me, 2)
    same_core = [list(range(start, devices, 2)) for start in range(2)]
    swap = [(device, device ^ 1) for device in range(devices)]
    table = lax.dynamic_slice_in_dim(jnp.asarray(rope_table(length, width)), me * tokens, tokens, 0)
    packed = pl.pallas_call(
        functools.partial(pack_kernel, rep),
        out_shape=jax.ShapeDtypeStruct((chips, per_chip + 2, tokens, width), jnp.bfloat16),
        in_specs=[VMEM] * 6,
        out_specs=VMEM,
        scratch_shapes=[
            pltpu.VMEM((tokens * heads, width), jnp.float32),
            pltpu.VMEM((tokens * kv_heads, width), jnp.float32),
            pltpu.VMEM((tokens * kv_heads, width), jnp.float32),
        ],
        compiler_params=pltpu.CompilerParams(vmem_limit_bytes=48 * 1024 * 1024),
        name="pack",
    )(query_states, key_states, value_states, table, query_gain[None], key_gain[None])
    arrived = lax.all_to_all(
        packed, "seq", split_axis=0, concat_axis=0, axis_index_groups=same_core, tiled=True
    )
    other = lax.ppermute(arrived[:, per_chip:], "seq", swap)
    attended = pl.pallas_call(
        looped_kernel,
        grid=(chips,),
        out_shape=jax.ShapeDtypeStruct((chips, per_chip, tokens, width), jnp.bfloat16),
        in_specs=[SMEM, VMEM, VMEM],
        out_specs=VMEM,
        compiler_params=pltpu.CompilerParams(vmem_limit_bytes=48 * 1024 * 1024),
        name="attention",
    )(core[None], arrived, other)
    returned = lax.all_to_all(
        attended, "seq", split_axis=0, concat_axis=0, axis_index_groups=same_core, tiled=True
    )
    return jnp.transpose(returned.reshape(heads, tokens, width), (1, 0, 2))


def rope_factors(table):
    half = table.shape[1] // 2
    swapped = pltpu.roll(table, half, 1)
    first = lax.broadcasted_iota(jnp.int32, table.shape, 1) < half
    return jnp.where(first, table, swapped), jnp.where(first, -swapped, table)


def normalize(rows):
    floats = rows.astype(jnp.float32)
    squares = floats * floats
    large = squares.astype(jnp.bfloat16)
    small = (squares - large.astype(jnp.float32)).astype(jnp.bfloat16)
    width = rows.shape[1]
    ones = jnp.ones((2 * width, width), jnp.bfloat16)
    added = jnp.dot(jnp.concatenate([large, small], axis=1), ones, preferred_element_type=jnp.float32)
    return floats * lax.rsqrt(added * (1.0 / width) + EPSILON)


def turn(normed, gain, cosine, sine):
    scaled = normed * gain
    return (scaled * cosine + pltpu.roll(scaled, scaled.shape[1] // 2, 1) * sine).astype(jnp.bfloat16)


def send_kernel(me_ref, q_hbm, k_hbm, v_hbm, table_hbm, query_gain_ref, key_gain_ref, *refs):
    pairs, (near_ref, q_ref, k_ref, v_ref, table_ref, qf_ref, kf_ref, vf_ref, sems) = refs[:-9], refs[-9:]
    tokens, heads, width = q_ref.shape
    kv_heads = k_ref.shape[1]
    group = heads // kv_heads
    me = me_ref[0]
    chip, core = lax.rem(me // 2, len(pairs)), lax.rem(me, 2)
    start = pl.multiple_of(me * tokens, 8)
    copies = [
        pltpu.make_async_copy(k_hbm, k_ref, sems.at[0]),
        pltpu.make_async_copy(table_hbm.at[pl.ds(start, tokens)], table_ref, sems.at[1]),
        pltpu.make_async_copy(v_hbm, v_ref, sems.at[2]),
        pltpu.make_async_copy(q_hbm, q_ref, sems.at[3]),
    ]
    for copy in copies:
        copy.start()
    copies[0].wait()
    kf_ref[...] = normalize(k_ref[...].reshape(tokens * kv_heads, width))
    copies[1].wait()
    cosine, sine = rope_factors(table_ref[...])
    copies[2].wait()
    vf_ref[...] = v_ref[...].astype(jnp.float32).reshape(tokens * kv_heads, width)
    for step, pair in enumerate(pairs):
        for side in range(2):
            head = (chip ^ step) * 2 + lax.rem(core + side, 2)
            keys = turn(kf_ref[pl.ds(head, tokens, stride=kv_heads), :], key_gain_ref[...], cosine, sine)
            values = vf_ref[pl.ds(head, tokens, stride=kv_heads), :].astype(jnp.bfloat16)
            pair[side, 0] = keys
            near_ref[head, group] = keys
            pair[side, 1] = values
            near_ref[head, group + 1] = values
    copies[3].wait()
    qf_ref[...] = normalize(q_ref[...].reshape(tokens * heads, width))
    for head in range(heads):
        normed = qf_ref[pl.ds(head, tokens, stride=heads), :]
        near_ref[head // group, head % group] = turn(normed, query_gain_ref[...], cosine, sine)


def weigh(segments, queries, state):
    scale = math.log2(math.e) / math.sqrt(queries.shape[1])
    scores = []
    for keys, _, allowed in segments:
        part = lax.dot_general(keys, queries, CONTRACT, preferred_element_type=jnp.float32)
        scores.append(part if allowed is None else jnp.where(allowed, part, MASKED))
    tops = [jnp.max(part, axis=0, keepdims=True) for part in scores] + ([] if state is None else [state[0]])
    highest = functools.reduce(jnp.maximum, tops)
    total = weighted = None
    if state is not None:
        factor = jnp.exp2((state[0] - highest) * scale)
        total, weighted = state[1] * factor, state[2] * factor
    for part, (_, values, _) in zip(scores, segments):
        probs = jnp.exp2((part - highest) * scale)
        added = jnp.sum(probs, axis=0, keepdims=True)
        summed = lax.dot_general(
            values, probs.astype(jnp.bfloat16), (((0,), (0,)), ((), ())), preferred_element_type=jnp.float32
        )
        total = added if total is None else total + added
        weighted = summed if weighted is None else weighted + summed
    return highest, total, weighted


def near_kernel(position_ref, x_ref, highest_ref, total_ref, weighted_ref):
    blocks, rows, tokens, width = x_ref.shape
    group = rows - 2
    keys = x_ref[:, group].reshape(blocks * tokens, width)
    values = x_ref[:, group + 1].reshape(blocks * tokens, width)
    lanes = NEAR_BLOCKS * group * tokens
    for first in range(0, blocks, NEAR_BLOCKS):
        count = first + NEAR_BLOCKS
        queries = x_ref[first:count, :group].reshape(lanes, width)
        place = slice(first * group * tokens, first * group * tokens + lanes)
        start, stop = first * tokens, count * tokens
        index = start + lax.broadcasted_iota(jnp.int32, (stop - start, lanes), 0)
        segments = [(keys[start:stop], values[start:stop], index <= position_ref[:, place])]
        if first > 0:
            segments.append((keys[:start], values[:start], None))
        for ref, value in zip((highest_ref, total_ref, weighted_ref), weigh(segments, queries, None)):
            ref[:, place] = value


def split_kernel(*refs):
    for step, ref in enumerate(refs[:-2]):
        for side in range(2):
            refs[side - 2][step] = ref[side]


def add_far(x_ref, pair_refs, state_refs, store):
    blocks, rows, tokens, width = x_ref.shape
    group = rows - 2
    segments = [[ref[:, i].reshape(ref.shape[0] * tokens, width) for i in range(2)] + [None] for ref in pair_refs]
    lanes = FAR_BLOCKS * group * tokens
    for first in range(0, blocks, FAR_BLOCKS):
        queries = x_ref[first : first + FAR_BLOCKS, :group].reshape(lanes, width)
        place = slice(first * group * tokens, first * group * tokens + lanes)
        store(first, place, *weigh(segments, queries, [ref[:, place] for ref in state_refs]))


def last_kernel(half, me_ref, x_ref, mine_ref, neighbours_ref, *refs):
    state, out_ref = refs[:3], refs[3]
    blocks, group, tokens, width = out_ref.shape

    def store(first, place, highest, total, weighted):
        result = jnp.transpose(weighted * (1.0 / total)).astype(jnp.bfloat16)
        out_ref[first : first + FAR_BLOCKS] = result.reshape(FAR_BLOCKS, group, tokens, width)

    @pl.when(me_ref[0] >= half)
    def _():
        add_far(x_ref, [mine_ref, neighbours_ref], state, store)

    @pl.when(me_ref[0] < half)
    def _():
        lanes = FAR_BLOCKS * group * tokens
        for first in range(0, blocks, FAR_BLOCKS):
            place = slice(first * group * tokens, first * group * tokens + lanes)
            store(first, place, None, state[1][:, place], state[2][:, place])


def halves_plan(length, devices, query_states, key_states, value_states, query_gain, key_gain):
    tokens, heads, width = query_states.shape
    kv_heads = key_states.shape[1]
    group = heads // kv_heads
    half = devices // 2
    steps = half // 2
    bf16, f32 = jnp.bfloat16, jnp.float32
    me = lax.axis_index("seq")[None]

    def call(kernel, name, outs, *operands, scratch=(), specs=None, limit=VMEM_LIMIT):
        return pl.pallas_call(
            kernel,
            out_shape=outs,
            in_specs=specs or [SMEM] + [VMEM] * len(operands),
            out_specs=jax.tree.map(lambda _: VMEM, outs),
            scratch_shapes=scratch,
            compiler_params=pltpu.CompilerParams(vmem_limit_bytes=limit),
            name=name,
        )(*([me] if specs is None or SMEM in specs else []), *operands)

    def to_upper(step, array):
        links = [(device, half + ((device // 2) ^ step) * 2 + device % 2) for device in range(half)]
        return lax.ppermute(array, "seq", links)

    def to_core(array, lowest):
        return lax.ppermute(array, "seq", [(device, device ^ 1) for device in range(lowest, devices)])

    shape = jax.ShapeDtypeStruct
    *pairs, near = call(
        send_kernel,
        "send",
        [shape((2, 2, tokens, width), bf16)] * steps + [shape((half, group + 2, tokens, width), bf16)],
        query_states,
        key_states,
        value_states,
        jnp.asarray(rope_table(length, width)),
        query_gain[None],
        key_gain[None],
        specs=[SMEM, HBM, HBM, HBM, HBM, VMEM, VMEM],
        scratch=[
            pltpu.VMEM((tokens, heads, width), bf16),
            pltpu.VMEM((tokens, kv_heads, width), bf16),
            pltpu.VMEM((tokens, kv_heads, width), bf16),
            pltpu.VMEM((tokens, width), f32),
            pltpu.VMEM((tokens * heads, width), f32),
            pltpu.VMEM((tokens * kv_heads, width), f32),
            pltpu.VMEM((tokens * kv_heads, width), f32),
            pltpu.SemaphoreType.DMA((4,)),
        ],
        limit=PACK_VMEM,
    )
    groups = [list(range(half)), list(range(half, devices))]

    def inside(array):
        return lax.all_to_all(array, "seq", split_axis=0, concat_axis=0, axis_index_groups=groups, tiled=True)

    far = [to_upper(step, pair) for step, pair in enumerate(pairs)]
    arrived = inside(near)
    lanes = half * group * tokens
    state = [shape((1, lanes), f32), shape((1, lanes), f32), shape((width, lanes), f32)]
    positions = np.broadcast_to(np.arange(half * tokens, dtype=np.int32).reshape(half, 1, tokens), (half, group, tokens))
    carried = call(near_kernel, "near", state, jnp.asarray(positions.reshape(1, lanes)), arrived, specs=[VMEM] * 2)

    carried, far = lax.optimization_barrier((carried, far))
    mine, others = call(
        split_kernel, "split", [shape((steps, 2, tokens, width), bf16)] * 2, *far, specs=[VMEM] * steps
    )
    neighbours = to_core(others, half)
    attended = call(
        functools.partial(last_kernel, half),
        "last",
        shape((half, group, tokens, width), bf16),
        arrived,
        mine,
        neighbours,
        *carried,
    )
    return jnp.transpose(inside(attended).reshape(heads, tokens, width), (1, 0, 2))


def solution(mesh):
    devices = mesh.shape["seq"]
    groups = mesh.shape["groups"]
    placed = P(("groups", "seq"), None, None)

    def run(query_states, key_states, value_states, query_gain, key_gain):
        length = query_states.shape[0] // groups
        plan = halves_plan if devices == 2 * key_states.shape[1] else general_plan
        return jax.shard_map(
            functools.partial(plan, length, devices),
            mesh=mesh,
            in_specs=(placed, placed, placed, P(), P()),
            out_specs=placed,
            check_vma=False,
        )(query_states, key_states, value_states, query_gain, key_gain)

    return run
```

```python
import functools
import math

import jax
import jax.numpy as jnp
import numpy as np
from jax import lax
from jax.experimental import pallas as pl
from jax.experimental.pallas import tpu as pltpu
from jax.sharding import PartitionSpec as P

ROPE_BASE = 1000000.0
EPSILON = 1e-06
MASKED = -1e30
VMEM_LIMIT = 24 * 1024 * 1024
PACK_VMEM = 56 * 1024 * 1024
VMEM = pl.BlockSpec(memory_space=pltpu.VMEM)
SMEM = pl.BlockSpec(memory_space=pltpu.SMEM)
HBM = pl.BlockSpec(memory_space=pltpu.HBM)
NEAR_BLOCKS = 2
FAR_BLOCKS = 2
CONTRACT = (((1,), (1,)), ((), ()))


def rope_table(length, width):
    half = width // 2
    frequency = np.float64(ROPE_BASE) ** (-(np.arange(half, dtype=np.float64) * 2.0 / width))
    angles = np.arange(length, dtype=np.float32)[:, None] * frequency.astype(np.float32)[None, :]
    wide = angles.astype(np.float64)
    return np.concatenate([np.cos(wide), np.sin(wide)], axis=-1).astype(np.float32)


def pack_kernel(rep, q_ref, k_ref, v_ref, table_ref, qg_ref, kg_ref, out_ref, qf_ref, kf_ref, vf_ref):
    tokens, heads, width = q_ref.shape
    kv_heads = k_ref.shape[1]
    chips, rows = out_ref.shape[:2]
    per_chip = rows - 2
    qf_ref[...] = q_ref[...].astype(jnp.float32).reshape(tokens * heads, width)
    kf_ref[...] = k_ref[...].astype(jnp.float32).reshape(tokens * kv_heads, width)
    vf_ref[...] = v_ref[...].astype(jnp.float32).reshape(tokens * kv_heads, width)
    table = table_ref[...]
    swapped = pltpu.roll(table, width // 2, 1)
    first = lax.broadcasted_iota(jnp.int32, table.shape, 1) < width // 2
    cosine = jnp.where(first, table, swapped)
    sine = jnp.where(first, -swapped, table)

    def rotate(floats, gain):
        mean_square = jnp.mean(floats * floats, axis=-1, keepdims=True)
        normed = floats * lax.rsqrt(mean_square + EPSILON) * gain
        turned = pltpu.roll(normed, width // 2, 1)
        return (normed * cosine + turned * sine).astype(jnp.bfloat16)

    query_gain, key_gain = qg_ref[...], kg_ref[...]
    for head in range(heads):
        floats = qf_ref[pl.ds(head, tokens, stride=heads), :]
        out_ref[head // per_chip, head % per_chip] = rotate(floats, query_gain)
    for head in range(kv_heads):
        floats = kf_ref[pl.ds(head, tokens, stride=kv_heads), :]
        rotated = rotate(floats, key_gain)
        values = vf_ref[pl.ds(head, tokens, stride=kv_heads), :].astype(jnp.bfloat16)
        for copy in range(rep):
            out_ref[head * rep + copy, per_chip] = rotated
            out_ref[head * rep + copy, per_chip + 1] = values


def looped_kernel(core_ref, x_ref, other_ref, out_ref):
    _, rows, tokens, width = x_ref.shape
    per_chip = rows - 2
    core = core_ref[0]
    block = pl.program_id(0)
    scale = math.log2(math.e) / math.sqrt(width)
    queries = x_ref[block, :per_chip].reshape(per_chip * tokens, width)
    row = lax.broadcasted_iota(jnp.int32, (per_chip, tokens, tokens), 1).reshape(per_chip * tokens, tokens)
    column = lax.broadcasted_iota(jnp.int32, (per_chip * tokens, tokens), 1)

    def merge(carried, keys, values, allowed):
        highest, total, weighted = carried
        scores = lax.dot_general(queries, keys, CONTRACT, preferred_element_type=jnp.float32)
        scores = jnp.where(allowed, scores, MASKED)
        new = jnp.maximum(highest, jnp.max(scores, axis=-1, keepdims=True))
        probs = jnp.exp2((scores - new) * scale)
        factor = jnp.exp2((highest - new) * scale)
        total = total * factor + jnp.sum(probs, axis=-1, keepdims=True)
        summed = jnp.dot(probs.astype(jnp.bfloat16), values, preferred_element_type=jnp.float32)
        return new, total, weighted * factor + summed

    def advance(index, carried):
        behind = (block - index) * tokens
        carried = merge(carried, x_ref[index, per_chip], x_ref[index, per_chip + 1], column <= row + behind)
        return merge(carried, other_ref[index, 0], other_ref[index, 1], column < behind + core * tokens)

    initial = (
        jnp.full((per_chip * tokens, 1), MASKED, jnp.float32),
        jnp.zeros((per_chip * tokens, 1), jnp.float32),
        jnp.zeros((per_chip * tokens, width), jnp.float32),
    )
    _, total, weighted = lax.fori_loop(0, block + 1, advance, initial)
    out_ref[block] = (weighted / total).astype(jnp.bfloat16).reshape(per_chip, tokens, width)


def general_plan(length, devices, query_states, key_states, value_states, query_gain, key_gain):
    tokens, heads, width = query_states.shape
    kv_heads = key_states.shape[1]
    chips = devices // 2
    per_chip = heads // chips
    rep = (heads // kv_heads) // per_chip
    me = lax.axis_index("seq")
    core = lax.rem(me, 2)
    same_core = [list(range(start, devices, 2)) for start in range(2)]
    swap = [(device, device ^ 1) for device in range(devices)]
    table = lax.dynamic_slice_in_dim(jnp.asarray(rope_table(length, width)), me * tokens, tokens, 0)
    packed = pl.pallas_call(
        functools.partial(pack_kernel, rep),
        out_shape=jax.ShapeDtypeStruct((chips, per_chip + 2, tokens, width), jnp.bfloat16),
        in_specs=[VMEM] * 6,
        out_specs=VMEM,
        scratch_shapes=[
            pltpu.VMEM((tokens * heads, width), jnp.float32),
            pltpu.VMEM((tokens * kv_heads, width), jnp.float32),
            pltpu.VMEM((tokens * kv_heads, width), jnp.float32),
        ],
        compiler_params=pltpu.CompilerParams(vmem_limit_bytes=48 * 1024 * 1024),
        name="pack",
    )(query_states, key_states, value_states, table, query_gain[None], key_gain[None])
    arrived = lax.all_to_all(
        packed, "seq", split_axis=0, concat_axis=0, axis_index_groups=same_core, tiled=True
    )
    other = lax.ppermute(arrived[:, per_chip:], "seq", swap)
    attended = pl.pallas_call(
        looped_kernel,
        grid=(chips,),
        out_shape=jax.ShapeDtypeStruct((chips, per_chip, tokens, width), jnp.bfloat16),
        in_specs=[SMEM, VMEM, VMEM],
        out_specs=VMEM,
        compiler_params=pltpu.CompilerParams(vmem_limit_bytes=48 * 1024 * 1024),
        name="attention",
    )(core[None], arrived, other)
    returned = lax.all_to_all(
        attended, "seq", split_axis=0, concat_axis=0, axis_index_groups=same_core, tiled=True
    )
    return jnp.transpose(returned.reshape(heads, tokens, width), (1, 0, 2))


def rope_factors(table):
    half = table.shape[1] // 2
    swapped = pltpu.roll(table, half, 1)
    first = lax.broadcasted_iota(jnp.int32, table.shape, 1) < half
    return jnp.where(first, table, swapped), jnp.where(first, -swapped, table)


def normalize(rows):
    floats = rows.astype(jnp.float32)
    squares = floats * floats
    large = squares.astype(jnp.bfloat16)
    small = (squares - large.astype(jnp.float32)).astype(jnp.bfloat16)
    width = rows.shape[1]
    ones = jnp.ones((2 * width, width), jnp.bfloat16)
    added = jnp.dot(jnp.concatenate([large, small], axis=1), ones, preferred_element_type=jnp.float32)
    return floats * lax.rsqrt(added * (1.0 / width) + EPSILON)


def turn(normed, gain, cosine, sine):
    scaled = normed * gain
    return (scaled * cosine + pltpu.roll(scaled, scaled.shape[1] // 2, 1) * sine).astype(jnp.bfloat16)


def send_kernel(me_ref, q_hbm, k_hbm, v_hbm, table_hbm, query_gain_ref, key_gain_ref, *refs):
    pairs, (near_ref, q_ref, k_ref, v_ref, table_ref, qf_ref, kf_ref, vf_ref, sems) = refs[:-9], refs[-9:]
    tokens, heads, width = q_ref.shape
    kv_heads = k_ref.shape[1]
    group = heads // kv_heads
    me = me_ref[0]
    chip, core = lax.rem(me // 2, len(pairs)), lax.rem(me, 2)
    start = pl.multiple_of(me * tokens, 8)
    copies = [
        pltpu.make_async_copy(k_hbm, k_ref, sems.at[0]),
        pltpu.make_async_copy(table_hbm.at[pl.ds(start, tokens)], table_ref, sems.at[1]),
        pltpu.make_async_copy(v_hbm, v_ref, sems.at[2]),
        pltpu.make_async_copy(q_hbm, q_ref, sems.at[3]),
    ]
    for copy in copies:
        copy.start()
    copies[0].wait()
    kf_ref[...] = normalize(k_ref[...].reshape(tokens * kv_heads, width))
    copies[1].wait()
    cosine, sine = rope_factors(table_ref[...])
    copies[2].wait()
    vf_ref[...] = v_ref[...].astype(jnp.float32).reshape(tokens * kv_heads, width)
    for step, pair in enumerate(pairs):
        for side in range(2):
            head = (chip ^ step) * 2 + lax.rem(core + side, 2)
            keys = turn(kf_ref[pl.ds(head, tokens, stride=kv_heads), :], key_gain_ref[...], cosine, sine)
            values = vf_ref[pl.ds(head, tokens, stride=kv_heads), :].astype(jnp.bfloat16)
            pair[side, 0] = keys
            near_ref[head, group] = keys
            pair[side, 1] = values
            near_ref[head, group + 1] = values
    copies[3].wait()
    qf_ref[...] = normalize(q_ref[...].reshape(tokens * heads, width))
    for head in range(heads):
        normed = qf_ref[pl.ds(head, tokens, stride=heads), :]
        near_ref[head // group, head % group] = turn(normed, query_gain_ref[...], cosine, sine)


def weigh(segments, queries, state):
    scale = math.log2(math.e) / math.sqrt(queries.shape[1])
    scores = []
    for keys, _, allowed in segments:
        part = lax.dot_general(keys, queries, CONTRACT, preferred_element_type=jnp.float32)
        scores.append(part if allowed is None else jnp.where(allowed, part, MASKED))
    tops = [jnp.max(part, axis=0, keepdims=True) for part in scores] + ([] if state is None else [state[0]])
    highest = functools.reduce(jnp.maximum, tops)
    total = weighted = None
    if state is not None:
        factor = jnp.exp2((state[0] - highest) * scale)
        total, weighted = state[1] * factor, state[2] * factor
    for part, (_, values, _) in zip(scores, segments):
        probs = jnp.exp2((part - highest) * scale)
        added = jnp.sum(probs, axis=0, keepdims=True)
        summed = lax.dot_general(
            values, probs.astype(jnp.bfloat16), (((0,), (0,)), ((), ())), preferred_element_type=jnp.float32
        )
        total = added if total is None else total + added
        weighted = summed if weighted is None else weighted + summed
    return highest, total, weighted


def near_kernel(position_ref, x_ref, highest_ref, total_ref, weighted_ref):
    blocks, rows, tokens, width = x_ref.shape
    group = rows - 2
    keys = x_ref[:, group].reshape(blocks * tokens, width)
    values = x_ref[:, group + 1].reshape(blocks * tokens, width)
    lanes = NEAR_BLOCKS * group * tokens
    for first in range(0, blocks, NEAR_BLOCKS):
        count = first + NEAR_BLOCKS
        queries = x_ref[first:count, :group].reshape(lanes, width)
        place = slice(first * group * tokens, first * group * tokens + lanes)
        start, stop = first * tokens, count * tokens
        index = start + lax.broadcasted_iota(jnp.int32, (stop - start, lanes), 0)
        segments = [(keys[start:stop], values[start:stop], index <= position_ref[:, place])]
        if first > 0:
            segments.append((keys[:start], values[:start], None))
        for ref, value in zip((highest_ref, total_ref, weighted_ref), weigh(segments, queries, None)):
            ref[:, place] = value


def split_kernel(*refs):
    for step, ref in enumerate(refs[:-2]):
        for side in range(2):
            refs[side - 2][step] = ref[side]


def add_far(x_ref, pairs_ref, state_refs, store):
    blocks, rows, tokens, width = x_ref.shape
    group = rows - 2
    segments = [[pairs_ref[:, i].reshape(pairs_ref.shape[0] * tokens, width) for i in range(2)] + [None]]
    lanes = FAR_BLOCKS * group * tokens
    for first in range(0, blocks, FAR_BLOCKS):
        queries = x_ref[first : first + FAR_BLOCKS, :group].reshape(lanes, width)
        place = slice(first * group * tokens, first * group * tokens + lanes)
        store(first, place, *weigh(segments, queries, [ref[:, place] for ref in state_refs]))


def far_kernel(half, me_ref, x_ref, pairs_ref, *refs):
    state, outs = refs[:3], refs[3:]

    def store(first, place, *values):
        for ref, value in zip(outs, values):
            ref[:, place] = value

    @pl.when(me_ref[0] >= half)
    def _():
        add_far(x_ref, pairs_ref, state, store)

    @pl.when(me_ref[0] < half)
    def _():
        for ref, before in zip(outs, state):
            ref[...] = before[...]


def last_kernel(half, me_ref, x_ref, pairs_ref, *refs):
    state, out_ref = refs[:3], refs[3]
    blocks, group, tokens, width = out_ref.shape

    def store(first, place, highest, total, weighted):
        result = jnp.transpose(weighted * (1.0 / total)).astype(jnp.bfloat16)
        out_ref[first : first + FAR_BLOCKS] = result.reshape(FAR_BLOCKS, group, tokens, width)

    @pl.when(me_ref[0] >= half)
    def _():
        add_far(x_ref, pairs_ref, state, store)

    @pl.when(me_ref[0] < half)
    def _():
        lanes = FAR_BLOCKS * group * tokens
        for first in range(0, blocks, FAR_BLOCKS):
            place = slice(first * group * tokens, first * group * tokens + lanes)
            store(first, place, None, state[1][:, place], state[2][:, place])


def halves_plan(length, devices, query_states, key_states, value_states, query_gain, key_gain):
    tokens, heads, width = query_states.shape
    kv_heads = key_states.shape[1]
    group = heads // kv_heads
    half = devices // 2
    steps = half // 2
    bf16, f32 = jnp.bfloat16, jnp.float32
    me = lax.axis_index("seq")[None]

    def call(kernel, name, outs, *operands, scratch=(), specs=None, limit=VMEM_LIMIT):
        return pl.pallas_call(
            kernel,
            out_shape=outs,
            in_specs=specs or [SMEM] + [VMEM] * len(operands),
            out_specs=jax.tree.map(lambda _: VMEM, outs),
            scratch_shapes=scratch,
            compiler_params=pltpu.CompilerParams(vmem_limit_bytes=limit),
            name=name,
        )(*([me] if specs is None or SMEM in specs else []), *operands)

    def to_upper(step, array):
        links = [(device, half + ((device // 2) ^ step) * 2 + device % 2) for device in range(half)]
        return lax.ppermute(array, "seq", links)

    def to_core(array, lowest):
        return lax.ppermute(array, "seq", [(device, device ^ 1) for device in range(lowest, devices)])

    shape = jax.ShapeDtypeStruct
    *pairs, near = call(
        send_kernel,
        "send",
        [shape((2, 2, tokens, width), bf16)] * steps + [shape((half, group + 2, tokens, width), bf16)],
        query_states,
        key_states,
        value_states,
        jnp.asarray(rope_table(length, width)),
        query_gain[None],
        key_gain[None],
        specs=[SMEM, HBM, HBM, HBM, HBM, VMEM, VMEM],
        scratch=[
            pltpu.VMEM((tokens, heads, width), bf16),
            pltpu.VMEM((tokens, kv_heads, width), bf16),
            pltpu.VMEM((tokens, kv_heads, width), bf16),
            pltpu.VMEM((tokens, width), f32),
            pltpu.VMEM((tokens * heads, width), f32),
            pltpu.VMEM((tokens * kv_heads, width), f32),
            pltpu.VMEM((tokens * kv_heads, width), f32),
            pltpu.SemaphoreType.DMA((4,)),
        ],
        limit=PACK_VMEM,
    )
    groups = [list(range(half)), list(range(half, devices))]

    def inside(array):
        return lax.all_to_all(array, "seq", split_axis=0, concat_axis=0, axis_index_groups=groups, tiled=True)

    far = [to_upper(step, pair) for step, pair in enumerate(pairs)]
    arrived = inside(near)
    lanes = half * group * tokens
    state = [shape((1, lanes), f32), shape((1, lanes), f32), shape((width, lanes), f32)]
    positions = np.broadcast_to(np.arange(half * tokens, dtype=np.int32).reshape(half, 1, tokens), (half, group, tokens))
    carried = call(near_kernel, "near", state, jnp.asarray(positions.reshape(1, lanes)), arrived, specs=[VMEM] * 2)

    carried, far = lax.optimization_barrier((carried, far))
    mine, others = call(
        split_kernel, "split", [shape((steps, 2, tokens, width), bf16)] * 2, *far, specs=[VMEM] * steps
    )
    neighbours = to_core(others, 0)
    carried = call(functools.partial(far_kernel, half), "far", state, arrived, mine, *carried)
    attended = call(
        functools.partial(last_kernel, half),
        "last",
        shape((half, group, tokens, width), bf16),
        arrived,
        neighbours,
        *carried,
    )
    return jnp.transpose(inside(attended).reshape(heads, tokens, width), (1, 0, 2))


def solution(mesh):
    devices = mesh.shape["seq"]
    groups = mesh.shape["groups"]
    placed = P(("groups", "seq"), None, None)

    def run(query_states, key_states, value_states, query_gain, key_gain):
        length = query_states.shape[0] // groups
        plan = halves_plan if devices == 2 * key_states.shape[1] else general_plan
        return jax.shard_map(
            functools.partial(plan, length, devices),
            mesh=mesh,
            in_specs=(placed, placed, placed, P(), P()),
            out_specs=placed,
            check_vma=False,
        )(query_states, key_states, value_states, query_gain, key_gain)

    return run
```

```python
import functools
import math

import jax
import jax.numpy as jnp
import numpy as np
from jax import lax
from jax.experimental import pallas as pl
from jax.experimental.pallas import tpu as pltpu
from jax.sharding import PartitionSpec as P

ROPE_BASE = 1000000.0
EPSILON = 1e-06
MASKED = -1e30
VMEM_LIMIT = 24 * 1024 * 1024
PACK_VMEM = 56 * 1024 * 1024
VMEM = pl.BlockSpec(memory_space=pltpu.VMEM)
SMEM = pl.BlockSpec(memory_space=pltpu.SMEM)
HBM = pl.BlockSpec(memory_space=pltpu.HBM)
NEAR_BLOCKS = 2
FAR_BLOCKS = 2
CONTRACT = (((1,), (1,)), ((), ()))


def rope_table(length, width):
    half = width // 2
    frequency = np.float64(ROPE_BASE) ** (-(np.arange(half, dtype=np.float64) * 2.0 / width))
    angles = np.arange(length, dtype=np.float32)[:, None] * frequency.astype(np.float32)[None, :]
    wide = angles.astype(np.float64)
    return np.concatenate([np.cos(wide), np.sin(wide)], axis=-1).astype(np.float32)


def pack_kernel(rep, q_ref, k_ref, v_ref, table_ref, qg_ref, kg_ref, out_ref, qf_ref, kf_ref, vf_ref):
    tokens, heads, width = q_ref.shape
    kv_heads = k_ref.shape[1]
    chips, rows = out_ref.shape[:2]
    per_chip = rows - 2
    qf_ref[...] = q_ref[...].astype(jnp.float32).reshape(tokens * heads, width)
    kf_ref[...] = k_ref[...].astype(jnp.float32).reshape(tokens * kv_heads, width)
    vf_ref[...] = v_ref[...].astype(jnp.float32).reshape(tokens * kv_heads, width)
    table = table_ref[...]
    swapped = pltpu.roll(table, width // 2, 1)
    first = lax.broadcasted_iota(jnp.int32, table.shape, 1) < width // 2
    cosine = jnp.where(first, table, swapped)
    sine = jnp.where(first, -swapped, table)

    def rotate(floats, gain):
        mean_square = jnp.mean(floats * floats, axis=-1, keepdims=True)
        normed = floats * lax.rsqrt(mean_square + EPSILON) * gain
        turned = pltpu.roll(normed, width // 2, 1)
        return (normed * cosine + turned * sine).astype(jnp.bfloat16)

    query_gain, key_gain = qg_ref[...], kg_ref[...]
    for head in range(heads):
        floats = qf_ref[pl.ds(head, tokens, stride=heads), :]
        out_ref[head // per_chip, head % per_chip] = rotate(floats, query_gain)
    for head in range(kv_heads):
        floats = kf_ref[pl.ds(head, tokens, stride=kv_heads), :]
        rotated = rotate(floats, key_gain)
        values = vf_ref[pl.ds(head, tokens, stride=kv_heads), :].astype(jnp.bfloat16)
        for copy in range(rep):
            out_ref[head * rep + copy, per_chip] = rotated
            out_ref[head * rep + copy, per_chip + 1] = values


def looped_kernel(core_ref, x_ref, other_ref, out_ref):
    _, rows, tokens, width = x_ref.shape
    per_chip = rows - 2
    core = core_ref[0]
    block = pl.program_id(0)
    scale = math.log2(math.e) / math.sqrt(width)
    queries = x_ref[block, :per_chip].reshape(per_chip * tokens, width)
    row = lax.broadcasted_iota(jnp.int32, (per_chip, tokens, tokens), 1).reshape(per_chip * tokens, tokens)
    column = lax.broadcasted_iota(jnp.int32, (per_chip * tokens, tokens), 1)

    def merge(carried, keys, values, allowed):
        highest, total, weighted = carried
        scores = lax.dot_general(queries, keys, CONTRACT, preferred_element_type=jnp.float32)
        scores = jnp.where(allowed, scores, MASKED)
        new = jnp.maximum(highest, jnp.max(scores, axis=-1, keepdims=True))
        probs = jnp.exp2((scores - new) * scale)
        factor = jnp.exp2((highest - new) * scale)
        total = total * factor + jnp.sum(probs, axis=-1, keepdims=True)
        summed = jnp.dot(probs.astype(jnp.bfloat16), values, preferred_element_type=jnp.float32)
        return new, total, weighted * factor + summed

    def advance(index, carried):
        behind = (block - index) * tokens
        carried = merge(carried, x_ref[index, per_chip], x_ref[index, per_chip + 1], column <= row + behind)
        return merge(carried, other_ref[index, 0], other_ref[index, 1], column < behind + core * tokens)

    initial = (
        jnp.full((per_chip * tokens, 1), MASKED, jnp.float32),
        jnp.zeros((per_chip * tokens, 1), jnp.float32),
        jnp.zeros((per_chip * tokens, width), jnp.float32),
    )
    _, total, weighted = lax.fori_loop(0, block + 1, advance, initial)
    out_ref[block] = (weighted / total).astype(jnp.bfloat16).reshape(per_chip, tokens, width)


def general_plan(length, devices, query_states, key_states, value_states, query_gain, key_gain):
    tokens, heads, width = query_states.shape
    kv_heads = key_states.shape[1]
    chips = devices // 2
    per_chip = heads // chips
    rep = (heads // kv_heads) // per_chip
    me = lax.axis_index("seq")
    core = lax.rem(me, 2)
    same_core = [list(range(start, devices, 2)) for start in range(2)]
    swap = [(device, device ^ 1) for device in range(devices)]
    table = lax.dynamic_slice_in_dim(jnp.asarray(rope_table(length, width)), me * tokens, tokens, 0)
    packed = pl.pallas_call(
        functools.partial(pack_kernel, rep),
        out_shape=jax.ShapeDtypeStruct((chips, per_chip + 2, tokens, width), jnp.bfloat16),
        in_specs=[VMEM] * 6,
        out_specs=VMEM,
        scratch_shapes=[
            pltpu.VMEM((tokens * heads, width), jnp.float32),
            pltpu.VMEM((tokens * kv_heads, width), jnp.float32),
            pltpu.VMEM((tokens * kv_heads, width), jnp.float32),
        ],
        compiler_params=pltpu.CompilerParams(vmem_limit_bytes=48 * 1024 * 1024),
        name="pack",
    )(query_states, key_states, value_states, table, query_gain[None], key_gain[None])
    arrived = lax.all_to_all(
        packed, "seq", split_axis=0, concat_axis=0, axis_index_groups=same_core, tiled=True
    )
    other = lax.ppermute(arrived[:, per_chip:], "seq", swap)
    attended = pl.pallas_call(
        looped_kernel,
        grid=(chips,),
        out_shape=jax.ShapeDtypeStruct((chips, per_chip, tokens, width), jnp.bfloat16),
        in_specs=[SMEM, VMEM, VMEM],
        out_specs=VMEM,
        compiler_params=pltpu.CompilerParams(vmem_limit_bytes=48 * 1024 * 1024),
        name="attention",
    )(core[None], arrived, other)
    returned = lax.all_to_all(
        attended, "seq", split_axis=0, concat_axis=0, axis_index_groups=same_core, tiled=True
    )
    return jnp.transpose(returned.reshape(heads, tokens, width), (1, 0, 2))


def rope_factors(table):
    half = table.shape[1] // 2
    swapped = pltpu.roll(table, half, 1)
    first = lax.broadcasted_iota(jnp.int32, table.shape, 1) < half
    return jnp.where(first, table, swapped), jnp.where(first, -swapped, table)


def normalize(rows):
    floats = rows.astype(jnp.float32)
    squares = floats * floats
    large = squares.astype(jnp.bfloat16)
    small = (squares - large.astype(jnp.float32)).astype(jnp.bfloat16)
    width = rows.shape[1]
    ones = jnp.ones((2 * width, width), jnp.bfloat16)
    added = jnp.dot(jnp.concatenate([large, small], axis=1), ones, preferred_element_type=jnp.float32)
    return floats * lax.rsqrt(added * (1.0 / width) + EPSILON)


def turn(normed, gain, cosine, sine):
    scaled = normed * gain
    return (scaled * cosine + pltpu.roll(scaled, scaled.shape[1] // 2, 1) * sine).astype(jnp.bfloat16)


def send_kernel(me_ref, q_hbm, k_hbm, v_hbm, table_hbm, query_gain_ref, key_gain_ref, *refs):
    pairs, (near_ref, q_ref, k_ref, v_ref, table_ref, qf_ref, kf_ref, vf_ref, sems) = refs[:-9], refs[-9:]
    tokens, heads, width = q_ref.shape
    kv_heads = k_ref.shape[1]
    group = heads // kv_heads
    me = me_ref[0]
    chip, core = lax.rem(me // 2, len(pairs)), lax.rem(me, 2)
    start = pl.multiple_of(me * tokens, 8)
    copies = [
        pltpu.make_async_copy(k_hbm, k_ref, sems.at[0]),
        pltpu.make_async_copy(table_hbm.at[pl.ds(start, tokens)], table_ref, sems.at[1]),
        pltpu.make_async_copy(v_hbm, v_ref, sems.at[2]),
        pltpu.make_async_copy(q_hbm, q_ref, sems.at[3]),
    ]
    for copy in copies:
        copy.start()
    copies[0].wait()
    kf_ref[...] = normalize(k_ref[...].reshape(tokens * kv_heads, width))
    copies[1].wait()
    cosine, sine = rope_factors(table_ref[...])
    copies[2].wait()
    vf_ref[...] = v_ref[...].astype(jnp.float32).reshape(tokens * kv_heads, width)
    for step, pair in enumerate(pairs):
        for side in range(2):
            head = (chip ^ step) * 2 + lax.rem(core + side, 2)
            keys = turn(kf_ref[pl.ds(head, tokens, stride=kv_heads), :], key_gain_ref[...], cosine, sine)
            values = vf_ref[pl.ds(head, tokens, stride=kv_heads), :].astype(jnp.bfloat16)
            pair[side, 0] = keys
            near_ref[head, group] = keys
            pair[side, 1] = values
            near_ref[head, group + 1] = values
    copies[3].wait()
    qf_ref[...] = normalize(q_ref[...].reshape(tokens * heads, width))
    for head in range(heads):
        normed = qf_ref[pl.ds(head, tokens, stride=heads), :]
        near_ref[head // group, head % group] = turn(normed, query_gain_ref[...], cosine, sine)


def weigh(segments, queries, state):
    scale = math.log2(math.e) / math.sqrt(queries.shape[1])
    scores = []
    for keys, _, allowed in segments:
        part = lax.dot_general(keys, queries, CONTRACT, preferred_element_type=jnp.float32)
        scores.append(part if allowed is None else jnp.where(allowed, part, MASKED))
    tops = [jnp.max(part, axis=0, keepdims=True) for part in scores] + ([] if state is None else [state[0]])
    highest = functools.reduce(jnp.maximum, tops)
    total = weighted = None
    if state is not None:
        factor = jnp.exp2((state[0] - highest) * scale)
        total, weighted = state[1] * factor, state[2] * factor
    for part, (_, values, _) in zip(scores, segments):
        probs = jnp.exp2((part - highest) * scale)
        added = jnp.sum(probs, axis=0, keepdims=True)
        summed = lax.dot_general(
            values, probs.astype(jnp.bfloat16), (((0,), (0,)), ((), ())), preferred_element_type=jnp.float32
        )
        total = added if total is None else total + added
        weighted = summed if weighted is None else weighted + summed
    return highest, total, weighted


def near_kernel(position_ref, x_ref, highest_ref, total_ref, weighted_ref):
    blocks, rows, tokens, width = x_ref.shape
    group = rows - 2
    keys = x_ref[:, group].reshape(blocks * tokens, width)
    values = x_ref[:, group + 1].reshape(blocks * tokens, width)
    lanes = NEAR_BLOCKS * group * tokens
    for first in range(0, blocks, NEAR_BLOCKS):
        count = first + NEAR_BLOCKS
        queries = x_ref[first:count, :group].reshape(lanes, width)
        place = slice(first * group * tokens, first * group * tokens + lanes)
        start, stop = first * tokens, count * tokens
        index = start + lax.broadcasted_iota(jnp.int32, (stop - start, lanes), 0)
        segments = [(keys[start:stop], values[start:stop], index <= position_ref[:, place])]
        if first > 0:
            segments.append((keys[:start], values[:start], None))
        for ref, value in zip((highest_ref, total_ref, weighted_ref), weigh(segments, queries, None)):
            ref[:, place] = value


def split_kernel(*refs):
    for step, ref in enumerate(refs[:-2]):
        for side in range(2):
            refs[side - 2][step] = ref[side]


def add_far(x_ref, pairs_ref, state_refs, store):
    blocks, rows, tokens, width = x_ref.shape
    group = rows - 2
    segments = [[pairs_ref[:, i].reshape(pairs_ref.shape[0] * tokens, width) for i in range(2)] + [None]]
    lanes = FAR_BLOCKS * group * tokens
    for first in range(0, blocks, FAR_BLOCKS):
        queries = x_ref[first : first + FAR_BLOCKS, :group].reshape(lanes, width)
        place = slice(first * group * tokens, first * group * tokens + lanes)
        store(first, place, *weigh(segments, queries, [ref[:, place] for ref in state_refs]))


def far_kernel(half, me_ref, x_ref, pairs_ref, *refs):
    state, outs = refs[:3], refs[3:]

    def store(first, place, *values):
        for ref, value in zip(outs, values):
            ref[:, place] = value

    @pl.when(me_ref[0] >= half)
    def _():
        add_far(x_ref, pairs_ref, state, store)

    @pl.when(me_ref[0] < half)
    def _():
        for ref, before in zip(outs, state):
            ref[...] = before[...]


def last_kernel(half, me_ref, x_ref, pairs_ref, *refs):
    state, out_ref = refs[:3], refs[3]
    blocks, group, tokens, width = out_ref.shape

    def store(first, place, highest, total, weighted):
        result = jnp.transpose(weighted * (1.0 / total)).astype(jnp.bfloat16)
        out_ref[first : first + FAR_BLOCKS] = result.reshape(FAR_BLOCKS, group, tokens, width)

    @pl.when(me_ref[0] >= half)
    def _():
        add_far(x_ref, pairs_ref, state, store)

    @pl.when(me_ref[0] < half)
    def _():
        lanes = FAR_BLOCKS * group * tokens
        for first in range(0, blocks, FAR_BLOCKS):
            place = slice(first * group * tokens, first * group * tokens + lanes)
            store(first, place, None, state[1][:, place], state[2][:, place])


def halves_plan(length, devices, query_states, key_states, value_states, query_gain, key_gain):
    tokens, heads, width = query_states.shape
    kv_heads = key_states.shape[1]
    group = heads // kv_heads
    half = devices // 2
    steps = half // 2
    bf16, f32 = jnp.bfloat16, jnp.float32
    me = lax.axis_index("seq")[None]

    def call(kernel, name, outs, *operands, scratch=(), specs=None, limit=VMEM_LIMIT):
        return pl.pallas_call(
            kernel,
            out_shape=outs,
            in_specs=specs or [SMEM] + [VMEM] * len(operands),
            out_specs=jax.tree.map(lambda _: VMEM, outs),
            scratch_shapes=scratch,
            compiler_params=pltpu.CompilerParams(vmem_limit_bytes=limit),
            name=name,
        )(*([me] if specs is None or SMEM in specs else []), *operands)

    def to_upper(step, array):
        links = [(device, ((device // 2) ^ (steps + step)) * 2 + device % 2) for device in range(devices)]
        return lax.ppermute(array, "seq", links)

    def to_core(array, lowest):
        return lax.ppermute(array, "seq", [(device, device ^ 1) for device in range(lowest, devices)])

    shape = jax.ShapeDtypeStruct
    *pairs, near = call(
        send_kernel,
        "send",
        [shape((2, 2, tokens, width), bf16)] * steps + [shape((half, group + 2, tokens, width), bf16)],
        query_states,
        key_states,
        value_states,
        jnp.asarray(rope_table(length, width)),
        query_gain[None],
        key_gain[None],
        specs=[SMEM, HBM, HBM, HBM, HBM, VMEM, VMEM],
        scratch=[
            pltpu.VMEM((tokens, heads, width), bf16),
            pltpu.VMEM((tokens, kv_heads, width), bf16),
            pltpu.VMEM((tokens, kv_heads, width), bf16),
            pltpu.VMEM((tokens, width), f32),
            pltpu.VMEM((tokens * heads, width), f32),
            pltpu.VMEM((tokens * kv_heads, width), f32),
            pltpu.VMEM((tokens * kv_heads, width), f32),
            pltpu.SemaphoreType.DMA((4,)),
        ],
        limit=PACK_VMEM,
    )
    groups = [list(range(half)), list(range(half, devices))]

    def inside(array):
        return lax.all_to_all(array, "seq", split_axis=0, concat_axis=0, axis_index_groups=groups, tiled=True)

    far = [to_upper(step, pair) for step, pair in enumerate(pairs)]
    arrived = inside(near)
    lanes = half * group * tokens
    state = [shape((1, lanes), f32), shape((1, lanes), f32), shape((width, lanes), f32)]
    positions = np.broadcast_to(np.arange(half * tokens, dtype=np.int32).reshape(half, 1, tokens), (half, group, tokens))
    carried = call(near_kernel, "near", state, jnp.asarray(positions.reshape(1, lanes)), arrived, specs=[VMEM] * 2)

    carried, far = lax.optimization_barrier((carried, far))
    mine, others = call(
        split_kernel, "split", [shape((steps, 2, tokens, width), bf16)] * 2, *far, specs=[VMEM] * steps
    )
    neighbours = to_core(others, 0)
    carried = call(functools.partial(far_kernel, half), "far", state, arrived, mine, *carried)
    attended = call(
        functools.partial(last_kernel, half),
        "last",
        shape((half, group, tokens, width), bf16),
        arrived,
        neighbours,
        *carried,
    )
    return jnp.transpose(inside(attended).reshape(heads, tokens, width), (1, 0, 2))


def solution(mesh):
    devices = mesh.shape["seq"]
    groups = mesh.shape["groups"]
    placed = P(("groups", "seq"), None, None)

    def run(query_states, key_states, value_states, query_gain, key_gain):
        length = query_states.shape[0] // groups
        plan = halves_plan if devices == 2 * key_states.shape[1] else general_plan
        return jax.shard_map(
            functools.partial(plan, length, devices),
            mesh=mesh,
            in_specs=(placed, placed, placed, P(), P()),
            out_specs=placed,
            check_vma=False,
        )(query_states, key_states, value_states, query_gain, key_gain)

    return run
```

```python
import functools
import math

import jax
import jax.numpy as jnp
import numpy as np
from jax import lax
from jax.experimental import pallas as pl
from jax.experimental.pallas import tpu as pltpu
from jax.sharding import PartitionSpec as P

ROPE_BASE = 1000000.0
EPSILON = 1e-06
MASKED = -1e30
VMEM_LIMIT = 24 * 1024 * 1024
PACK_VMEM = 56 * 1024 * 1024
VMEM = pl.BlockSpec(memory_space=pltpu.VMEM)
SMEM = pl.BlockSpec(memory_space=pltpu.SMEM)
HBM = pl.BlockSpec(memory_space=pltpu.HBM)
NEAR_BLOCKS = 2
FAR_BLOCKS = 2
CONTRACT = (((1,), (1,)), ((), ()))


def rope_table(length, width):
    half = width // 2
    frequency = np.float64(ROPE_BASE) ** (-(np.arange(half, dtype=np.float64) * 2.0 / width))
    angles = np.arange(length, dtype=np.float32)[:, None] * frequency.astype(np.float32)[None, :]
    wide = angles.astype(np.float64)
    return np.concatenate([np.cos(wide), np.sin(wide)], axis=-1).astype(np.float32)


def pack_kernel(rep, q_ref, k_ref, v_ref, table_ref, qg_ref, kg_ref, out_ref, qf_ref, kf_ref, vf_ref):
    tokens, heads, width = q_ref.shape
    kv_heads = k_ref.shape[1]
    chips, rows = out_ref.shape[:2]
    per_chip = rows - 2
    qf_ref[...] = q_ref[...].astype(jnp.float32).reshape(tokens * heads, width)
    kf_ref[...] = k_ref[...].astype(jnp.float32).reshape(tokens * kv_heads, width)
    vf_ref[...] = v_ref[...].astype(jnp.float32).reshape(tokens * kv_heads, width)
    table = table_ref[...]
    swapped = pltpu.roll(table, width // 2, 1)
    first = lax.broadcasted_iota(jnp.int32, table.shape, 1) < width // 2
    cosine = jnp.where(first, table, swapped)
    sine = jnp.where(first, -swapped, table)

    def rotate(floats, gain):
        mean_square = jnp.mean(floats * floats, axis=-1, keepdims=True)
        normed = floats * lax.rsqrt(mean_square + EPSILON) * gain
        turned = pltpu.roll(normed, width // 2, 1)
        return (normed * cosine + turned * sine).astype(jnp.bfloat16)

    query_gain, key_gain = qg_ref[...], kg_ref[...]
    for head in range(heads):
        floats = qf_ref[pl.ds(head, tokens, stride=heads), :]
        out_ref[head // per_chip, head % per_chip] = rotate(floats, query_gain)
    for head in range(kv_heads):
        floats = kf_ref[pl.ds(head, tokens, stride=kv_heads), :]
        rotated = rotate(floats, key_gain)
        values = vf_ref[pl.ds(head, tokens, stride=kv_heads), :].astype(jnp.bfloat16)
        for copy in range(rep):
            out_ref[head * rep + copy, per_chip] = rotated
            out_ref[head * rep + copy, per_chip + 1] = values


def looped_kernel(core_ref, x_ref, other_ref, out_ref):
    _, rows, tokens, width = x_ref.shape
    per_chip = rows - 2
    core = core_ref[0]
    block = pl.program_id(0)
    scale = math.log2(math.e) / math.sqrt(width)
    queries = x_ref[block, :per_chip].reshape(per_chip * tokens, width)
    row = lax.broadcasted_iota(jnp.int32, (per_chip, tokens, tokens), 1).reshape(per_chip * tokens, tokens)
    column = lax.broadcasted_iota(jnp.int32, (per_chip * tokens, tokens), 1)

    def merge(carried, keys, values, allowed):
        highest, total, weighted = carried
        scores = lax.dot_general(queries, keys, CONTRACT, preferred_element_type=jnp.float32)
        scores = jnp.where(allowed, scores, MASKED)
        new = jnp.maximum(highest, jnp.max(scores, axis=-1, keepdims=True))
        probs = jnp.exp2((scores - new) * scale)
        factor = jnp.exp2((highest - new) * scale)
        total = total * factor + jnp.sum(probs, axis=-1, keepdims=True)
        summed = jnp.dot(probs.astype(jnp.bfloat16), values, preferred_element_type=jnp.float32)
        return new, total, weighted * factor + summed

    def advance(index, carried):
        behind = (block - index) * tokens
        carried = merge(carried, x_ref[index, per_chip], x_ref[index, per_chip + 1], column <= row + behind)
        return merge(carried, other_ref[index, 0], other_ref[index, 1], column < behind + core * tokens)

    initial = (
        jnp.full((per_chip * tokens, 1), MASKED, jnp.float32),
        jnp.zeros((per_chip * tokens, 1), jnp.float32),
        jnp.zeros((per_chip * tokens, width), jnp.float32),
    )
    _, total, weighted = lax.fori_loop(0, block + 1, advance, initial)
    out_ref[block] = (weighted / total).astype(jnp.bfloat16).reshape(per_chip, tokens, width)


def general_plan(length, devices, query_states, key_states, value_states, query_gain, key_gain):
    tokens, heads, width = query_states.shape
    kv_heads = key_states.shape[1]
    chips = devices // 2
    per_chip = heads // chips
    rep = (heads // kv_heads) // per_chip
    me = lax.axis_index("seq")
    core = lax.rem(me, 2)
    same_core = [list(range(start, devices, 2)) for start in range(2)]
    swap = [(device, device ^ 1) for device in range(devices)]
    table = lax.dynamic_slice_in_dim(jnp.asarray(rope_table(length, width)), me * tokens, tokens, 0)
    packed = pl.pallas_call(
        functools.partial(pack_kernel, rep),
        out_shape=jax.ShapeDtypeStruct((chips, per_chip + 2, tokens, width), jnp.bfloat16),
        in_specs=[VMEM] * 6,
        out_specs=VMEM,
        scratch_shapes=[
            pltpu.VMEM((tokens * heads, width), jnp.float32),
            pltpu.VMEM((tokens * kv_heads, width), jnp.float32),
            pltpu.VMEM((tokens * kv_heads, width), jnp.float32),
        ],
        compiler_params=pltpu.CompilerParams(vmem_limit_bytes=48 * 1024 * 1024),
        name="pack",
    )(query_states, key_states, value_states, table, query_gain[None], key_gain[None])
    arrived = lax.all_to_all(
        packed, "seq", split_axis=0, concat_axis=0, axis_index_groups=same_core, tiled=True
    )
    other = lax.ppermute(arrived[:, per_chip:], "seq", swap)
    attended = pl.pallas_call(
        looped_kernel,
        grid=(chips,),
        out_shape=jax.ShapeDtypeStruct((chips, per_chip, tokens, width), jnp.bfloat16),
        in_specs=[SMEM, VMEM, VMEM],
        out_specs=VMEM,
        compiler_params=pltpu.CompilerParams(vmem_limit_bytes=48 * 1024 * 1024),
        name="attention",
    )(core[None], arrived, other)
    returned = lax.all_to_all(
        attended, "seq", split_axis=0, concat_axis=0, axis_index_groups=same_core, tiled=True
    )
    return jnp.transpose(returned.reshape(heads, tokens, width), (1, 0, 2))


def rope_factors(table):
    half = table.shape[1] // 2
    swapped = pltpu.roll(table, half, 1)
    first = lax.broadcasted_iota(jnp.int32, table.shape, 1) < half
    return jnp.where(first, table, swapped), jnp.where(first, -swapped, table)


def normalize(rows):
    floats = rows.astype(jnp.float32)
    squares = floats * floats
    large = squares.astype(jnp.bfloat16)
    small = (squares - large.astype(jnp.float32)).astype(jnp.bfloat16)
    width = rows.shape[1]
    ones = jnp.ones((2 * width, width), jnp.bfloat16)
    added = jnp.dot(jnp.concatenate([large, small], axis=1), ones, preferred_element_type=jnp.float32)
    return floats * lax.rsqrt(added * (1.0 / width) + EPSILON)


def turn(normed, gain, cosine, sine):
    scaled = normed * gain
    return (scaled * cosine + pltpu.roll(scaled, scaled.shape[1] // 2, 1) * sine).astype(jnp.bfloat16)


def send_kernel(me_ref, q_hbm, k_hbm, v_hbm, table_hbm, query_gain_ref, key_gain_ref, *refs):
    pairs, (near_ref, q_ref, k_ref, v_ref, table_ref, qf_ref, kf_ref, vf_ref, sems) = refs[:-9], refs[-9:]
    tokens, heads, width = q_ref.shape
    kv_heads = k_ref.shape[1]
    group = heads // kv_heads
    me = me_ref[0]
    chip, core = lax.rem(me // 2, len(pairs)), lax.rem(me, 2)
    start = pl.multiple_of(me * tokens, 8)
    copies = [
        pltpu.make_async_copy(k_hbm, k_ref, sems.at[0]),
        pltpu.make_async_copy(table_hbm.at[pl.ds(start, tokens)], table_ref, sems.at[1]),
        pltpu.make_async_copy(v_hbm, v_ref, sems.at[2]),
        pltpu.make_async_copy(q_hbm, q_ref, sems.at[3]),
    ]
    for copy in copies:
        copy.start()
    copies[0].wait()
    kf_ref[...] = normalize(k_ref[...].reshape(tokens * kv_heads, width))
    copies[1].wait()
    cosine, sine = rope_factors(table_ref[...])
    copies[2].wait()
    vf_ref[...] = v_ref[...].astype(jnp.float32).reshape(tokens * kv_heads, width)
    for step, pair in enumerate(pairs):
        for side in range(2):
            head = (chip ^ step) * 2 + lax.rem(core + side, 2)
            keys = turn(kf_ref[pl.ds(head, tokens, stride=kv_heads), :], key_gain_ref[...], cosine, sine)
            values = vf_ref[pl.ds(head, tokens, stride=kv_heads), :].astype(jnp.bfloat16)
            pair[side, 0] = keys
            near_ref[head, group] = keys
            pair[side, 1] = values
            near_ref[head, group + 1] = values
    copies[3].wait()
    qf_ref[...] = normalize(q_ref[...].reshape(tokens * heads, width))
    for head in range(heads):
        normed = qf_ref[pl.ds(head, tokens, stride=heads), :]
        near_ref[head // group, head % group] = turn(normed, query_gain_ref[...], cosine, sine)


def weigh(segments, queries, state):
    scale = math.log2(math.e) / math.sqrt(queries.shape[1])
    scores = []
    for keys, _, allowed in segments:
        part = lax.dot_general(keys, queries, CONTRACT, preferred_element_type=jnp.float32)
        scores.append(part if allowed is None else jnp.where(allowed, part, MASKED))
    tops = [jnp.max(part, axis=0, keepdims=True) for part in scores] + ([] if state is None else [state[0]])
    highest = functools.reduce(jnp.maximum, tops)
    total = weighted = None
    if state is not None:
        factor = jnp.exp2((state[0] - highest) * scale)
        total, weighted = state[1] * factor, state[2] * factor
    for part, (_, values, _) in zip(scores, segments):
        probs = jnp.exp2((part - highest) * scale)
        added = jnp.sum(probs, axis=0, keepdims=True)
        summed = lax.dot_general(
            values, probs.astype(jnp.bfloat16), (((0,), (0,)), ((), ())), preferred_element_type=jnp.float32
        )
        total = added if total is None else total + added
        weighted = summed if weighted is None else weighted + summed
    return highest, total, weighted


def near_kernel(position_ref, x_ref, highest_ref, total_ref, weighted_ref):
    blocks, rows, tokens, width = x_ref.shape
    group = rows - 2
    keys = x_ref[:, group].reshape(blocks * tokens, width)
    values = x_ref[:, group + 1].reshape(blocks * tokens, width)
    lanes = NEAR_BLOCKS * group * tokens
    for first in range(0, blocks, NEAR_BLOCKS):
        count = first + NEAR_BLOCKS
        queries = x_ref[first:count, :group].reshape(lanes, width)
        place = slice(first * group * tokens, first * group * tokens + lanes)
        start, stop = first * tokens, count * tokens
        index = start + lax.broadcasted_iota(jnp.int32, (stop - start, lanes), 0)
        segments = [(keys[start:stop], values[start:stop], index <= position_ref[:, place])]
        if first > 0:
            segments.append((keys[:start], values[:start], None))
        for ref, value in zip((highest_ref, total_ref, weighted_ref), weigh(segments, queries, None)):
            ref[:, place] = value


def split_kernel(*refs):
    for step, ref in enumerate(refs[:-2]):
        for side in range(2):
            refs[side - 2][step] = ref[side]


def add_far(x_ref, pair_refs, state_refs, store):
    blocks, rows, tokens, width = x_ref.shape
    group = rows - 2
    segments = [[ref[:, i].reshape(ref.shape[0] * tokens, width) for i in range(2)] + [None] for ref in pair_refs]
    lanes = FAR_BLOCKS * group * tokens
    for first in range(0, blocks, FAR_BLOCKS):
        queries = x_ref[first : first + FAR_BLOCKS, :group].reshape(lanes, width)
        place = slice(first * group * tokens, first * group * tokens + lanes)
        store(first, place, *weigh(segments, queries, [ref[:, place] for ref in state_refs]))


def last_kernel(half, me_ref, x_ref, mine_ref, neighbours_ref, *refs):
    state, out_ref = refs[:3], refs[3]
    blocks, group, tokens, width = out_ref.shape

    def store(first, place, highest, total, weighted):
        result = jnp.transpose(weighted * (1.0 / total)).astype(jnp.bfloat16)
        out_ref[first : first + FAR_BLOCKS] = result.reshape(FAR_BLOCKS, group, tokens, width)

    @pl.when(me_ref[0] >= half)
    def _():
        add_far(x_ref, [mine_ref, neighbours_ref], state, store)

    @pl.when(me_ref[0] < half)
    def _():
        lanes = FAR_BLOCKS * group * tokens
        for first in range(0, blocks, FAR_BLOCKS):
            place = slice(first * group * tokens, first * group * tokens + lanes)
            store(first, place, None, state[1][:, place], state[2][:, place])


def halves_plan(length, devices, query_states, key_states, value_states, query_gain, key_gain):
    tokens, heads, width = query_states.shape
    kv_heads = key_states.shape[1]
    group = heads // kv_heads
    half = devices // 2
    steps = half // 2
    bf16, f32 = jnp.bfloat16, jnp.float32
    me = lax.axis_index("seq")[None]

    def call(kernel, name, outs, *operands, scratch=(), specs=None, limit=VMEM_LIMIT):
        return pl.pallas_call(
            kernel,
            out_shape=outs,
            in_specs=specs or [SMEM] + [VMEM] * len(operands),
            out_specs=jax.tree.map(lambda _: VMEM, outs),
            scratch_shapes=scratch,
            compiler_params=pltpu.CompilerParams(vmem_limit_bytes=limit),
            name=name,
        )(*([me] if specs is None or SMEM in specs else []), *operands)

    def to_upper(step, array):
        links = [(device, ((device // 2) ^ (steps + step)) * 2 + device % 2) for device in range(devices)]
        return lax.ppermute(array, "seq", links)

    def to_core(array, lowest):
        return lax.ppermute(array, "seq", [(device, device ^ 1) for device in range(lowest, devices)])

    shape = jax.ShapeDtypeStruct
    *pairs, near = call(
        send_kernel,
        "send",
        [shape((2, 2, tokens, width), bf16)] * steps + [shape((half, group + 2, tokens, width), bf16)],
        query_states,
        key_states,
        value_states,
        jnp.asarray(rope_table(length, width)),
        query_gain[None],
        key_gain[None],
        specs=[SMEM, HBM, HBM, HBM, HBM, VMEM, VMEM],
        scratch=[
            pltpu.VMEM((tokens, heads, width), bf16),
            pltpu.VMEM((tokens, kv_heads, width), bf16),
            pltpu.VMEM((tokens, kv_heads, width), bf16),
            pltpu.VMEM((tokens, width), f32),
            pltpu.VMEM((tokens * heads, width), f32),
            pltpu.VMEM((tokens * kv_heads, width), f32),
            pltpu.VMEM((tokens * kv_heads, width), f32),
            pltpu.SemaphoreType.DMA((4,)),
        ],
        limit=PACK_VMEM,
    )
    groups = [list(range(half)), list(range(half, devices))]

    def inside(array):
        return lax.all_to_all(array, "seq", split_axis=0, concat_axis=0, axis_index_groups=groups, tiled=True)

    far = [to_upper(step, pair) for step, pair in enumerate(pairs)]
    arrived = lax.cond(me[0] >= 0, inside, jnp.zeros_like, near)
    arrived, far = lax.optimization_barrier((arrived, far))
    mine, others = call(
        split_kernel, "split", [shape((steps, 2, tokens, width), bf16)] * 2, *far, specs=[VMEM] * steps
    )
    neighbours = to_core(others, 0)
    lanes = half * group * tokens
    state = [shape((1, lanes), f32), shape((1, lanes), f32), shape((width, lanes), f32)]
    positions = np.broadcast_to(np.arange(half * tokens, dtype=np.int32).reshape(half, 1, tokens), (half, group, tokens))
    carried = call(near_kernel, "near", state, jnp.asarray(positions.reshape(1, lanes)), arrived, specs=[VMEM] * 2)

    attended = call(
        functools.partial(last_kernel, half),
        "last",
        shape((half, group, tokens, width), bf16),
        arrived,
        mine,
        neighbours,
        *carried,
    )
    return jnp.transpose(inside(attended).reshape(heads, tokens, width), (1, 0, 2))


def solution(mesh):
    devices = mesh.shape["seq"]
    groups = mesh.shape["groups"]
    placed = P(("groups", "seq"), None, None)

    def run(query_states, key_states, value_states, query_gain, key_gain):
        length = query_states.shape[0] // groups
        plan = halves_plan if devices == 2 * key_states.shape[1] else general_plan
        return jax.shard_map(
            functools.partial(plan, length, devices),
            mesh=mesh,
            in_specs=(placed, placed, placed, P(), P()),
            out_specs=placed,
            check_vma=False,
        )(query_states, key_states, value_states, query_gain, key_gain)

    return run
```
